32 devices in a mesh: ctx: 8 (over z, y), fsdp: 4 (over x, core).
Axes of the slice: x: 2, y: 2, z: 4, core: 2. Of those that a mesh axis runs over, the one named last changes fastest.
Arguments:
- tokens: bfloat16 [4, 1024, 2048], P('fsdp', 'ctx'), may hold values from -6 to 6
- attn_gain: float32 [2048], replicated, may hold values from 0.1 to 1.9
- w_query: bfloat16 [2048, 2048], P('fsdp'), may hold values from -0.125 to 0.125
- w_key: bfloat16 [2048, 2048], P('fsdp'), may hold values from -0.125 to 0.125
- w_value: bfloat16 [2048, 2048], P('fsdp'), may hold values from -0.125 to 0.125
- query_gain: float32 [128], replicated, may hold values from 0.1 to 1.9
- key_gain: float32 [128], replicated, may hold values from 0.1 to 1.9
- w_out: bfloat16 [2048, 2048], P('fsdp'), may hold values from -2.53125 to 2.53125
- ffn_gain: float32 [2048], replicated, may hold values from 0.1 to 1.9
- w_router: bfloat16 [2048, 16], P('fsdp'), may hold values from -0.06591797 to 0.06591797
- w_gate: bfloat16 [2048, 16, 1024], P('fsdp', 'ctx'), may hold values from -0.125 to 0.125
- w_up: bfloat16 [2048, 16, 1024], P('fsdp', 'ctx'), may hold values from -0.125 to 0.125
- w_down: bfloat16 [2048, 16, 1024], P('fsdp', 'ctx'), may hold values from -0.75 to 0.75
- routes: int32 [4, 1024, 8], P('fsdp', 'ctx'), may hold values from 0 to 15, all different within a row; in each aligned block of 128 rows (0 to 127, 128 to 255, ..., all dimensions but the last counted through in order) at most 80 rows name the same one
- cotangent: bfloat16 [4, 1024, 2048], P('fsdp', 'ctx'), may hold values from -8 to 8
Outputs:
- out: bfloat16 [4, 1024, 2048], P('fsdp', 'ctx')
- d_tokens: float32 [4, 1024, 2048], P('fsdp', 'ctx')
- d_attn_gain: float32 [2048], replicated
- d_query: float32 [2048, 2048], P('fsdp')
- d_key: float32 [2048, 2048], P('fsdp')
- d_value: float32 [2048, 2048], P('fsdp')
- d_query_gain: float32 [128], replicated
- d_key_gain: float32 [128], replicated
- d_out_proj: float32 [2048, 2048], P('fsdp')
- d_ffn_gain: float32 [2048], replicated
- d_router: float32 [2048, 16], P('fsdp')
- d_gate: float32 [2048, 16, 1024], P('fsdp', 'ctx')
- d_up: float32 [2048, 16, 1024], P('fsdp', 'ctx')
- d_down: float32 [2048, 16, 1024], P('fsdp', 'ctx')
The draws below stay inside these ranges and needn't reach their ends.
Inputs may be any that keep to these rules, and one draw needn't show every extreme that they name: `routes`: each token names 8 different experts; in each aligned block of 128 tokens (the tokens of one device) no expert is named more than 80 times, and in some blocks one is named exactly 80 times.
All inputs are finite; a program needn't handle non-finite values.
Results may differ from the reference program's by a relative error of at most 0.025.
Values may be sent and summed in bfloat16 or wider, within the bound.
No kernel may reach another device: no remote copies, remote signals or barrier semaphores. Data moves between devices by JAX's collectives and lax.ppermute only.
A program may use at most 384 MiB of HBM per device.

```python
import functools
import math
import jax
import jax.numpy as jnp
import numpy as np
from jax import lax

D = 2048
HEADS = 16
HEAD_DIM = 128
FFE = 1024
TOP = 8
TOK_DEV = 128
EXPERTS = 16
SEQS = 4
LEN = 1024
CAP = 80
N_CTX = 8


def draw_cotangent(key, part):
    key = jax.random.fold_in(key, 11)
    first_key = jax.random.fold_in(key, 0)
    rising = 0.5 + jnp.arange(LEN, dtype=jnp.float32) / LEN
    sample = jax.random.normal(first_key, (SEQS, LEN, D), jnp.float32)
    values = jnp.clip(sample * rising[None, :, None], -8.0, 8.0)
    return values.astype(jnp.bfloat16)


def levels(rng, shape, cuts, least, high):
    gain, own = 1.0, jax.random.fold_in(rng, 6)
    for axis_at, parts in cuts:
        heights = jnp.exp(jax.random.uniform(jax.random.fold_in(own, axis_at), (parts,), jnp.float32, least / len(cuts), high / len(cuts)))
        gain = gain * jnp.repeat(heights, shape[axis_at] // parts).reshape([-1 if axis == axis_at else 1 for axis in range(len(shape))])
    return gain


def shared_out(stream_key, own, number, rows, number_of, top, reach, lean):
    sequence = jax.random.permutation(stream_key, number_of)
    crowded, common = portions_of(number_of, rows * top, reach, lean, True), portions_of(number_of, rows * top, reach, lean, False)
    places = jnp.arange(number_of)

    def named(lengths, turn):
        used = int((lengths > 0).sum())
        fixed = max(1, used // 4)
        moved = fixed + (places - fixed + turn * (used - fixed)) % max(1, number_of - fixed)
        return jnp.zeros((number_of,), jnp.int32).at[sequence[jnp.where(places < fixed, places, moved)]].set(jnp.asarray(lengths, jnp.int32))

    lengths = jnp.where(number % 4 == 0, named(crowded, number // 4), named(common, number - number // 4 - 1))
    mixed = jax.random.permutation(jax.random.fold_in(own, 3), number_of)
    donor, receiver = mixed[0:number_of // 2 * 2:2], mixed[1:number_of // 2 * 2:2]
    slack = jnp.minimum(lengths[donor] - 1, reach - lengths[receiver]) // 2
    slack = jnp.where((donor == sequence[0]) | (receiver == sequence[0]) | (lengths[receiver] == 0), 0, jnp.maximum(slack, 0))
    moved = jax.random.randint(jax.random.fold_in(own, 4), (number_of // 2,), 0, 1 << 20) % (slack + 1)
    lengths = lengths.at[donor].add(-moved).at[receiver].add(moved)
    labels = jnp.searchsorted(jnp.cumsum(lengths), jnp.arange(rows * top), side="right").astype(jnp.int32)
    table = labels.reshape(top, rows).T
    table = table[jax.random.permutation(jax.random.fold_in(own, 1), rows)]
    turn = jax.random.randint(jax.random.fold_in(own, 2), (rows, 1), 0, top)
    return jnp.take_along_axis(table, (jnp.arange(top)[None, :] + turn) % top, axis=1)


def portions_of(count, total, most, lean, full):
    loads = [(1 << 20) // math.isqrt(grade ** lean) + 1 for grade in range(1, count + 1)]
    largest = most if full else min(most, max(-(-total // count), total * loads[0] // sum(loads)))
    least = 1 if total - largest >= count - 1 else 0
    counts, rest = [largest] + [least] * (count - 1), total - largest - least * (count - 1)
    while rest > 0:
        movable = [i for i in range(1, count) if counts[i] < largest] or [i for i in range(1, count) if counts[i] < most]
        whole, budget = sum([loads[i] for i in movable]), rest
        for i in movable:
            more = min(most - counts[i], max(1, budget * loads[i] // whole), rest)
            counts[i] = counts[i] + more
            rest = rest - more
    return np.array(counts)


def scatter_about(own_key, dims, scale, bound, cuts=(), kind=jnp.bfloat16):
    entries = scale * jax.random.normal(own_key, dims, jnp.float32)
    if cuts:
        entries = entries * levels(own_key, dims, cuts, -0.22, 0.18)
    return jnp.clip(entries, -bound, bound).astype(kind)


def setup_inputs(seed: int = 0) -> dict:
    splits = jax.random.split(jax.random.key(seed), 16)
    tokens = scatter_about(splits[0], (SEQS, LEN, D), 1.0, 6.0, ((0, 4), (1, 8)))
    attn_gain = jnp.clip(1.0 + 0.18 * jax.random.normal(splits[1], (D,), jnp.float32), 0.1, 1.9)
    w_query = scatter_about(splits[2], (D, D), D ** -0.5, 0.125, ((0, 4),))
    w_key = scatter_about(splits[3], (D, D), D ** -0.5, 0.125, ((0, 4),))
    w_value = scatter_about(splits[4], (D, D), D ** -0.5, 0.125, ((0, 4),))
    query_gain = jnp.clip(1.0 + 0.18 * jax.random.normal(splits[5], (HEAD_DIM,), jnp.float32), 0.1, 1.9)
    key_gain = jnp.clip(1.0 + 0.18 * jax.random.normal(splits[6], (HEAD_DIM,), jnp.float32), 0.1, 1.9)
    w_out = scatter_about(splits[7], (D, D), (0.6 * LEN ** 0.5 * D ** (0 - 0.5)), 2.53125, ((0, 4),))
    ffn_gain = jnp.clip(1.0 + 0.18 * jax.random.normal(splits[8], (D,), jnp.float32), 0.1, 1.9)
    w_router = scatter_about(splits[9], (D, EXPERTS), (0.5 * D ** (0 - 0.5)), 0.06591797, ((0, 4),))
    w_gate = scatter_about(splits[10], (D, EXPERTS, FFE), D ** -0.5, 0.125, ((0, 4), (1, 8)))
    w_up = scatter_about(splits[11], (D, EXPERTS, FFE), D ** -0.5, 0.125, ((0, 4), (1, 8)))
    w_down = scatter_about(splits[12], (D, EXPERTS, FFE), (4 * FFE ** (0 - 0.5)), 0.75, ((0, 4), (1, 8)))
    routes_keys = jax.random.split(jax.random.fold_in(splits[13], 1), SEQS * LEN // TOK_DEV)
    routes_turns = jax.random.permutation(jax.random.fold_in(splits[13], 3), SEQS * LEN // TOK_DEV)
    routes = jax.vmap(lambda own, number: shared_out(jax.random.fold_in(splits[13], 2), own, number, TOK_DEV, EXPERTS, TOP, CAP, 0))(routes_keys, routes_turns).reshape((SEQS, LEN, TOP))
    cotangent = draw_cotangent(jax.random.fold_in(splits[15], 71), 0)
    return dict(tokens=tokens, attn_gain=attn_gain, w_query=w_query, w_key=w_key, w_value=w_value, query_gain=query_gain, key_gain=key_gain, w_out=w_out, ffn_gain=ffn_gain, w_router=w_router, w_gate=w_gate, w_up=w_up, w_down=w_down, routes=routes, cotangent=cotangent)


EPSILON = 1e-06
ROPE_BASE = 10000.0
PRECISE = lax.Precision.HIGHEST

@jax.custom_vjp
def low(v):
    return lax.optimization_barrier(v.astype(jnp.bfloat16)).astype(jnp.float32)

@jax.custom_vjp
def low_back(v):
    return v

def low_keep(v):
    return (low(v), None)

def low_pass(kept, grad):
    return (grad,)

def back_keep(v):
    return (v, None)

def back_low(kept, grad):
    return (low(grad),)
low.defvjp(low_keep, low_pass)
low_back.defvjp(back_keep, back_low)

def rms_norm(values, gain_vec):
    factor = lax.rsqrt(lax.optimization_barrier(jnp.mean(values * values, axis=-1, keepdims=True)) + EPSILON)
    return values * factor * gain_vec

def rope_turn(values, places):
    half_dim = values.shape[-1] // 2
    frequency = ROPE_BASE ** (-jnp.arange(half_dim, dtype=jnp.float32) * 2.0 / values.shape[-1])
    angles = places.astype(jnp.float32)[:, None, None] * frequency[None, None, :]
    cosine = jnp.cos(angles)
    sine_part = jnp.sin(angles)
    first_half = values[..., :half_dim]
    second_half = values[..., half_dim:]
    return jnp.concatenate([first_half * cosine - second_half * sine_part, second_half * cosine + first_half * sine_part], axis=-1)

def attend_sequence(queries, keys, values):
    length = queries.shape[0]
    block_rows = min(512, length)
    scale = queries.shape[-1] ** (-0.5)

    def one_block(query_block):
        scores = low_back(scale * jnp.einsum('qhd,khd->hqk', query_block, keys, precision=PRECISE))
        probs = jax.nn.softmax(scores, axis=-1)
        return jnp.einsum('hqk,khd->qhd', low(probs), values, precision=PRECISE)
    blocks = queries.reshape(length // block_rows, block_rows, queries.shape[1], queries.shape[2])
    outputs = lax.map(jax.checkpoint(one_block), blocks)
    return outputs.reshape(queries.shape)

def expert_apply(operands):
    rows_in, gate_w, up_w, down_w = operands
    gate_pre = low_back(jnp.dot(rows_in, gate_w, precision=PRECISE))
    up_pre = low_back(jnp.dot(rows_in, up_w, precision=PRECISE))
    act = low(jax.nn.silu(gate_pre) * up_pre)
    return low_back(low(jnp.dot(act, down_w.T, precision=PRECISE)))

def layer_forward(routes, tokens, attn_gain, w_query, w_key, w_value, query_gain, key_gain, w_out, ffn_gain, w_router, w_gate, w_up, w_down):
    total = SEQS * LEN
    flat = tokens.reshape(total, D)
    normed = low(rms_norm(flat, attn_gain))
    query_pre = low_back(jnp.dot(normed, w_query, precision=PRECISE))
    key_pre = low_back(jnp.dot(normed, w_key, precision=PRECISE))
    value_all = low_back(low(jnp.dot(normed, w_value, precision=PRECISE)))
    places = jnp.tile(jnp.arange(LEN, dtype=jnp.int32), SEQS)
    queries = low(rope_turn(rms_norm(query_pre.reshape(total, HEADS, HEAD_DIM), query_gain), places))
    keys = low(rope_turn(rms_norm(key_pre.reshape(total, HEADS, HEAD_DIM), key_gain), places))

    def per_sequence(operands):
        return attend_sequence(operands[0], operands[1], operands[2])
    attended = lax.map(jax.checkpoint(per_sequence), (queries.reshape(SEQS, LEN, HEADS, HEAD_DIM), keys.reshape(SEQS, LEN, HEADS, HEAD_DIM), value_all.reshape(SEQS, LEN, HEADS, HEAD_DIM)))
    mixed = low_back(low(attended.reshape(total, D)))
    projected = low_back(jnp.dot(mixed, w_out, precision=PRECISE))
    hidden = flat + projected
    ffn_in = low(rms_norm(hidden, ffn_gain))
    logits = jnp.dot(ffn_in, w_router, precision=PRECISE)
    route_table = routes.reshape(total, TOP)
    chosen = jnp.take_along_axis(logits, route_table, axis=1)
    gates = jax.nn.softmax(chosen, axis=-1)
    route_rows = route_table.reshape(-1)
    member = (route_rows[:, None] == jnp.arange(EXPERTS, dtype=jnp.int32)[None, :]).astype(jnp.int32)
    ranking = jnp.cumsum(member, axis=0) - 1
    depth = CAP * SEQS * N_CTX
    target = (route_rows * depth + lax.optimization_barrier(jnp.sum(ranking * member, axis=1))).astype(jnp.int32)
    owner = (jnp.arange(total * TOP, dtype=jnp.int32) // TOP).astype(jnp.int32)
    buffer = low_back(jnp.zeros((EXPERTS * depth, D), jnp.float32).at[target].set(ffn_in[owner]))
    expert_rows = lax.map(jax.checkpoint(expert_apply), (buffer.reshape(EXPERTS, depth, D), jnp.transpose(w_gate, (1, 0, 2)), jnp.transpose(w_up, (1, 0, 2)), jnp.transpose(w_down, (1, 0, 2))))
    picked = expert_rows.reshape(EXPERTS * depth, D)[target].reshape(total, TOP, D)
    result = hidden + lax.optimization_barrier(jnp.sum(gates[..., None] * picked, axis=1))
    return result.reshape(SEQS, LEN, D)

def reference(tokens, attn_gain, w_query, w_key, w_value, query_gain, key_gain, w_out, ffn_gain, w_router, w_gate, w_up, w_down, routes, cotangent):
    floats = [array.astype(jnp.float32) for array in (tokens, attn_gain, w_query, w_key, w_value, query_gain, key_gain, w_out, ffn_gain, w_router, w_gate, w_up, w_down)]
    output, pullback = jax.vjp(functools.partial(layer_forward, routes), *floats)
    gradients = pullback(cotangent.astype(jnp.float32))
    return (output.astype(jnp.bfloat16), gradients[0], gradients[1], gradients[2], gradients[3], gradients[4], gradients[5], gradients[6], gradients[7], gradients[8], gradients[9], gradients[10], gradients[11], gradients[12])
```

```python
import functools

import jax
import jax.numpy as jnp
import numpy as np
from jax import lax
from jax.experimental import pallas as pl
from jax.experimental.pallas import tpu as pltpu
from jax.sharding import PartitionSpec as P

EPSILON = 1e-06
ROPE_BASE = 10000.0
BF = jnp.bfloat16
F32 = jnp.float32


def dot(a, b, contract=((1,), (0,)), precision=None):
    return lax.dot_general(a, b, (contract, ((), ())), precision=precision, preferred_element_type=F32)


def dot_nt(a, b):
    return dot(a, b, ((1,), (1,)))


def dot_tn(a, b):
    return dot(a, b, ((0,), (0,)))


def head_norm(v, gain):
    factor = lax.rsqrt(jnp.mean(v * v, axis=-1, keepdims=True) + EPSILON)
    return v * factor * gain, factor


def turn(v, cosine, sine):
    return v * cosine + pltpu.roll(v, v.shape[-1] // 2, 1) * sine


def head_back(grad, v, gain, cosine, sine):
    grad = turn(grad, cosine, -sine)
    factor = lax.rsqrt(jnp.mean(v * v, axis=-1, keepdims=True) + EPSILON)
    gain_grad = jnp.sum(grad * v * factor, axis=0, keepdims=True)
    inner = grad * gain
    return factor * inner - v * (factor * factor * factor) * jnp.mean(inner * v, axis=-1, keepdims=True), gain_grad


def rows_of(ref):
    block = ref[...]
    return block.reshape(-1, block.shape[-1])


def attend_kernel(q_ref, k_ref, v_ref, qg_ref, kg_ref, cos_ref, sin_ref, o_ref, keys, values_t):
    step = pl.program_id(1)

    @pl.when(step == 0)
    def _():
        normed, _unused = head_norm(rows_of(k_ref).astype(F32), kg_ref[...])
        keys[...] = turn(normed, cos_ref[...], sin_ref[...]).astype(BF)
        values_t[...] = rows_of(v_ref).astype(F32).T.astype(BF)

    queries = rows_of(q_ref).astype(F32)
    number, head_dim = queries.shape
    here = pl.ds(pl.multiple_of(step * number, number), number)
    normed, _unused = head_norm(queries, qg_ref[...])
    queries = turn(normed, cos_ref[here, :], sin_ref[here, :]).astype(BF)
    weights = jnp.exp(dot_nt(keys[...], queries) * (head_dim**-0.5))
    total = jnp.sum(weights, axis=0, keepdims=True)
    mixed = dot(values_t[...], weights.astype(BF)) / total
    o_ref[...] = mixed.T.astype(BF).reshape(o_ref.shape)


def attend_back_kernel(
    q_ref, k_ref, v_ref, m_ref, qg_ref, kg_ref, cos_ref, sin_ref,
    g_ref, gain_ref, keys, keys_t, key_acc, value_acc,
):
    pair = pl.program_id(0)
    step = pl.program_id(1)
    last = pl.num_programs(1) - 1

    @pl.when((pair == 0) & (step == 0))
    def _():
        gain_ref[...] = jnp.zeros_like(gain_ref)

    @pl.when(step == 0)
    def _():
        normed, _unused = head_norm(rows_of(k_ref).astype(F32), kg_ref[...])
        turned = turn(normed, cos_ref[...], sin_ref[...])
        keys[...] = turned.astype(BF)
        keys_t[...] = turned.T.astype(BF)
        key_acc[...] = jnp.zeros_like(key_acc)
        value_acc[...] = jnp.zeros_like(value_acc)

    query_pre = rows_of(q_ref).astype(F32)
    grad_mixed = rows_of(m_ref)
    number, head_dim = query_pre.shape
    scale = head_dim**-0.5
    here = pl.ds(pl.multiple_of(step * number, number), number)
    cosine, sine = cos_ref[here, :], sin_ref[here, :]
    normed, _unused = head_norm(query_pre, qg_ref[...])
    queries = turn(normed, cosine, sine).astype(BF)
    weights = jnp.exp(dot_nt(keys[...], queries) * scale)
    probs = weights * (1.0 / jnp.sum(weights, axis=0, keepdims=True))
    value_acc[...] += dot(probs.astype(BF), grad_mixed)
    weighted = probs * dot_nt(rows_of(v_ref), grad_mixed)
    delta = jnp.sum(weighted, axis=0, keepdims=True)
    grad_scores = (weighted - probs * delta).astype(BF)
    key_acc[...] += dot(grad_scores, queries)
    grad_query = dot(keys_t[...], grad_scores).T * scale
    grad_query, gain_grad = head_back(grad_query, query_pre, qg_ref[...], cosine, sine)
    rows = g_ref.shape[2]
    blocks = number // rows
    g_ref[pl.ds(step * blocks, blocks), 0] = grad_query.astype(BF).reshape(blocks, rows, head_dim)
    gain_ref[0:1, :] += gain_grad

    @pl.when(step == last)
    def _():
        grad_key, gain_grad = head_back(
            key_acc[...] * scale, rows_of(k_ref).astype(F32), kg_ref[...], cos_ref[...], sin_ref[...]
        )
        g_ref[:, 1] = grad_key.astype(BF).reshape(-1, rows, head_dim)
        g_ref[:, 2] = value_acc[...].astype(BF).reshape(-1, rows, head_dim)
        gain_ref[1:2, :] += gain_grad


def attention_specs(shape):
    blocks, pairs, rows, head_dim = shape
    at_once = max(1, 256 // rows)
    while blocks % at_once:
        at_once -= 1
    pairs //= 3
    part = pl.BlockSpec((at_once, 1, rows, head_dim), lambda p, i: (i, p, 0, 0))
    three = [
        pl.BlockSpec((at_once, 1, rows, head_dim), lambda p, i: (i, 3 * p, 0, 0)),
        pl.BlockSpec((blocks, 1, rows, head_dim), lambda p, i: (0, 3 * p + 1, 0, 0)),
        pl.BlockSpec((blocks, 1, rows, head_dim), lambda p, i: (0, 3 * p + 2, 0, 0)),
    ]
    gain = pl.BlockSpec((1, head_dim), lambda p, i: (0, 0))
    table = pl.BlockSpec((blocks * rows, head_dim), lambda p, i: (0, 0))
    params = pltpu.CompilerParams(
        dimension_semantics=("arbitrary", "arbitrary"),
        vmem_limit_bytes=(24 if blocks * rows <= 1024 else 56) * 2**20,
    )
    return part, three, gain, table, (pairs, blocks // at_once), params


def attend(qkv, query_gain, key_gain, cosine, sine):
    part, three, gain, table, grid, params = attention_specs(qkv.shape)
    blocks, _unused, rows, head_dim = qkv.shape
    length = blocks * rows
    work = grid[0] * length * length
    return pl.pallas_call(
        attend_kernel,
        grid=grid,
        in_specs=[*three, gain, gain, table, table],
        out_specs=part,
        out_shape=jax.ShapeDtypeStruct((blocks, grid[0], rows, head_dim), BF),
        scratch_shapes=[pltpu.VMEM((length, head_dim), BF), pltpu.VMEM((head_dim, length), BF)],
        compiler_params=params,
        cost_estimate=pl.CostEstimate(flops=4 * work * head_dim, bytes_accessed=3 * qkv.size, transcendentals=work),
        name="attend",
    )(qkv, qkv, qkv, query_gain, key_gain, cosine, sine)


def attend_back(qkv, grad_mixed, query_gain, key_gain, cosine, sine):
    part, three, gain, table, grid, params = attention_specs(qkv.shape)
    blocks, _unused, rows, head_dim = qkv.shape
    length = blocks * rows
    work = grid[0] * length * length
    return pl.pallas_call(
        attend_back_kernel,
        grid=grid,
        in_specs=[*three, part, gain, gain, table, table],
        out_specs=[
            pl.BlockSpec((blocks, 3, rows, head_dim), lambda p, i: (0, p, 0, 0)),
            pl.BlockSpec((8, head_dim), lambda p, i: (0, 0)),
        ],
        out_shape=[jax.ShapeDtypeStruct(qkv.shape, BF), jax.ShapeDtypeStruct((8, head_dim), F32)],
        scratch_shapes=[
            pltpu.VMEM((length, head_dim), BF),
            pltpu.VMEM((head_dim, length), BF),
            pltpu.VMEM((length, head_dim), F32),
            pltpu.VMEM((length, head_dim), F32),
        ],
        compiler_params=params,
        cost_estimate=pl.CostEstimate(flops=10 * work * head_dim, bytes_accessed=5 * qkv.size, transcendentals=work),
        name="attend_back",
    )(qkv, qkv, qkv, grad_mixed, query_gain, key_gain, cosine, sine)


def swap(v, mask):
    size = lax.axis_size("fsdp")
    return lax.ppermute(v, "fsdp", [(i, i ^ mask) for i in range(size)])


def ring_order(size):
    if size == 8:
        return [0, 2, 4, 6, 7, 5, 3, 1]
    return list(range(size))


def ring_send(v, direction):
    order = ring_order(lax.axis_size("ctx"))
    size = len(order)
    return lax.ppermute(v, "ctx", [(order[i], order[(i + direction) % size]) for i in range(size)])


def ring_gather(v):
    size = lax.axis_size("ctx")
    far, half = size // 2, v.shape[0] // 2
    found = {0: v}
    right, left = v, v
    for step in range(1, far):
        right, left = ring_send(right, 1), ring_send(left, -1)
        found[size - step], found[step] = right, left
    found[far] = jnp.concatenate([ring_send(right[:half], 1), ring_send(left[half:], -1)])
    return found


def ring_scatter(term, watch=None):
    size = lax.axis_size("ctx")
    far = size // 2
    first = term(far)
    half = first.shape[0] // 2
    right, left = ring_send(first[:half].astype(BF), 1), ring_send(first[half:].astype(BF), -1)
    if watch is not None:
        watch += [right, left]
    for offset in range(far - 1, 0, -1):
        ahead, behind = term(offset), term(size - offset)
        if offset == far - 1:
            ahead = jnp.concatenate([ahead[:half] + right.astype(F32), ahead[half:]])
            behind = jnp.concatenate([behind[:half], behind[half:] + left.astype(F32)])
        else:
            ahead, behind = ahead + right.astype(F32), behind + left.astype(F32)
        right, left = ring_send(ahead.astype(BF), 1), ring_send(behind.astype(BF), -1)
    return term(0) + right.astype(F32) + left.astype(F32)


def after(v, *others):
    return lax.optimization_barrier((v, *others))[0]


class Order:
    def __init__(self, first):
        self.last = first

    def __call__(self, *values):
        self.last, *values = lax.optimization_barrier((self.last, *values))
        return values[0] if len(values) == 1 else values


def sum_all(v):
    for axis in ("fsdp", "ctx"):
        size = lax.axis_size(axis)
        mask = 1
        while mask < size:
            v = v + lax.ppermute(v, axis, [(i, i ^ mask) for i in range(size)])
            mask *= 2
    return v


def body(
    tokens, attn_gain, w_query, w_key, w_value, query_gain, key_gain, w_out,
    ffn_gain, w_router, w_gate, w_up, w_down, routes, cotangent,
):
    ctx_size = lax.axis_size("ctx")
    parts = lax.axis_size("fsdp")
    mine = lax.axis_index("fsdp")
    place = lax.axis_index("ctx")
    rows = tokens.shape[1]
    width = tokens.shape[2]
    slab = w_query.shape[0]
    head_dim = query_gain.shape[0]
    own_heads = width // head_dim // parts
    own_experts = w_gate.shape[1]
    hidden_units = w_gate.shape[2]
    experts = own_experts * ctx_size
    seq_length = rows * ctx_size
    order = ring_order(ctx_size)
    ring_place = jnp.asarray(np.argsort(np.array(order)), jnp.int32)[place]
    ring_table = jnp.asarray(order, jnp.int32)

    pairs = own_heads * parts
    per = max(1, pairs // ctx_size)
    repeats = max(1, ctx_size // pairs)

    def to_pairs(v, kinds):
        v = v.reshape(parts, rows, kinds, own_heads, head_dim).transpose(3, 0, 2, 1, 4)
        v = v.reshape(pairs // per, per * kinds, rows, head_dim)
        if repeats > 1:
            v = jnp.repeat(v, repeats, axis=0)
        return lax.all_to_all(v, "ctx", split_axis=0, concat_axis=0, tiled=True)

    def from_pairs(v):
        v = lax.all_to_all(v, "ctx", split_axis=0, concat_axis=0, tiled=True)
        if repeats > 1:
            v = v[::repeats]
        kinds = v.shape[1] // per
        v = v.reshape(own_heads, -1, per, kinds, rows, head_dim).transpose(1, 2, 4, 3, 0, 5)
        return v.reshape(parts * rows, kinds * own_heads * head_dim)

    def block(v, index, size, axis):
        return lax.dynamic_slice_in_dim(v, index * size, size, axis)

    def assemble(pieces, axis):
        size = pieces[0].shape[axis]
        shape = list(pieces[0].shape)
        shape[axis] = size * parts
        whole = jnp.zeros(shape, pieces[0].dtype)
        for mask, piece in enumerate(pieces):
            whole = lax.dynamic_update_slice_in_dim(whole, piece, (mine ^ mask) * size, axis)
        return whole

    def fsdp_gather(v, axis):
        across = swap(v, 2)
        return assemble([v, swap(v, 1), across, swap(across, 1)], axis)

    def fsdp_scatter(term):
        near = swap(term(mine ^ 1).astype(BF), 1)
        far = swap(term(mine ^ 3).astype(BF), 1)
        far = (term(mine ^ 2) + far.astype(F32)).astype(BF)
        return term(mine) + near.astype(F32) + swap(far, 2).astype(F32)

    half = head_dim // 2
    frequency = ROPE_BASE ** (-jnp.arange(half, dtype=F32) * 2.0 / head_dim)
    angles = jnp.arange(seq_length, dtype=jnp.int32).astype(F32)[:, None] * frequency[None, :]
    cosine, sine = jnp.cos(angles), jnp.sin(angles)
    cosine = jnp.concatenate([cosine, cosine], axis=1)
    sine = jnp.concatenate([-sine, sine], axis=1)
    q_gain, k_gain = query_gain[None, :], key_gain[None, :]

    source = tokens[0].astype(F32)
    factor_one = lax.rsqrt(jnp.mean(source * source, axis=-1, keepdims=True) + EPSILON)
    normed = (source * factor_one * attn_gain).astype(BF)
    in_order = Order(jnp.zeros((), F32))
    normed = in_order(normed)
    w_query, w_key, w_value, w_router, w_gate, w_up, w_down, routes = after(
        (w_query, w_key, w_value, w_router, w_gate, w_up, w_down, routes), normed
    )
    normed_all = fsdp_gather(normed, 0)
    normed_slab = block(normed_all, mine, slab, 1)
    own_width = own_heads * head_dim
    projections = [
        jnp.concatenate([block(w, mine ^ mask, own_width, 1) for w in (w_query, w_key, w_value)], axis=1)
        for mask in range(parts)
    ]
    near, far = [swap(dot(normed_slab, projections[mask]).astype(BF), 1) for mask in (1, 3)]
    far = in_order((dot(normed_slab, projections[2]) + far.astype(F32)).astype(BF))
    cot_low = after(cotangent[0], far)
    own = dot(normed_slab, projections[0]) + near.astype(F32)
    qkv = in_order(to_pairs((own + swap(far, 2).astype(F32)).astype(BF), 3))

    gate_w = lax.all_gather(w_gate.reshape(slab, -1), "fsdp", axis=0, tiled=True)
    up_w = lax.all_gather(w_up.reshape(slab, -1), "fsdp", axis=0, tiled=True)
    down_w = lax.all_gather(w_down.reshape(slab, -1), "fsdp", axis=0, tiled=True)
    router_w = fsdp_gather(w_router, 0)
    routes_all = lax.all_to_all(
        jnp.broadcast_to(routes, (ctx_size, *routes.shape[1:])), "ctx", split_axis=0, concat_axis=0, tiled=True
    )
    cot_blocks = ring_gather(cot_low)

    mixed_low = attend(qkv, q_gain, k_gain, cosine, sine)
    mixed = in_order(from_pairs(mixed_low))
    hidden = source + fsdp_scatter(lambda index: dot(block(mixed, index, rows, 0), w_out))
    factor_two = lax.rsqrt(jnp.mean(hidden * hidden, axis=-1, keepdims=True) + EPSILON)
    ffn_in = in_order((hidden * factor_two * ffn_gain).astype(BF))

    expert_ids = jnp.arange(experts, dtype=jnp.int32)

    def gates_of(rows_in, named):
        logits = dot(rows_in, router_w)
        chosen = jnp.any(named[:, :, None] == expert_ids[None, None, :], axis=1)
        high = jnp.max(jnp.where(chosen, logits, -1e30), axis=-1, keepdims=True)
        weights = jnp.where(chosen, jnp.exp(jnp.where(chosen, logits - high, 0.0)), 0.0)
        return weights / jnp.sum(weights, axis=-1, keepdims=True)

    def at_offset(offset):
        return ring_table[(ring_place + offset) % ctx_size]

    columns = lax.broadcasted_iota(jnp.int32, (1, own_experts * hidden_units), 1) // hidden_units

    def spread(per_expert):
        out = per_expert[:, 0:1]
        for index in range(1, own_experts):
            out = jnp.where(columns == index, per_expert[:, index : index + 1], out)
        return out

    def per_expert_sum(v):
        return jnp.stack(
            [jnp.sum(v[:, i * hidden_units : (i + 1) * hidden_units], axis=1) for i in range(own_experts)]
        )

    ffn_blocks = ring_gather(ffn_in)
    offsets = [0] + [o for step in range(1, ctx_size // 2) for o in (step, ctx_size - step)] + [ctx_size // 2]
    cots = jnp.concatenate([cot_blocks[o] for o in offsets])
    cots, down_w = after((cots, down_w), ffn_in)
    grad_act = in_order(dot(cots, down_w))
    inputs = in_order(jnp.concatenate([ffn_blocks[o] for o in offsets]))
    named = jnp.concatenate([routes_all[at_offset(o)] for o in offsets])
    gates = lax.dynamic_slice_in_dim(gates_of(inputs, named), place * own_experts, own_experts, 1)
    wide_gates = spread(gates)
    gate_pre = dot(inputs, gate_w)
    up_pre = dot(inputs, up_w)
    sigmoid = jax.nn.sigmoid(gate_pre)
    silu = gate_pre * sigmoid
    acts = (silu * up_pre).astype(BF).astype(F32)
    d_gates = per_expert_sum(acts * grad_act).reshape(own_experts, ctx_size, rows)
    grad_act = wide_gates * grad_act
    up_grads = (grad_act * silu).astype(BF)
    gate_grads = (grad_act * up_pre * (sigmoid * (1.0 + gate_pre * (1.0 - sigmoid)))).astype(BF)
    acts = (wide_gates * acts).astype(BF)
    grad_rows = dot_nt(gate_grads, gate_w) + dot_nt(up_grads, up_w)
    grad_rows = in_order(grad_rows)

    def term_of(terms):
        return lambda offset: terms[offsets.index(offset) * rows :][:rows]

    watch = []
    grad_ffn_in = ring_scatter(term_of(grad_rows), watch)
    acts = after(acts, *watch)
    weighted = dot_nt(acts, down_w)
    back_index = jnp.asarray(np.argsort(np.array(offsets)), jnp.int32)
    by_place = jnp.asarray(np.argsort(np.array(order)), jnp.int32)
    d_gates = d_gates[:, back_index[(by_place - ring_place) % ctx_size], :].transpose(1, 0, 2)
    d_gates = lax.all_to_all(d_gates, "ctx", split_axis=0, concat_axis=0, tiled=True)
    d_gates = d_gates.reshape(experts, rows).T

    def weight_grad(left, right):
        grad = dot_tn(left, after(right, *watch)).astype(BF)
        return lax.psum_scatter(grad, "fsdp", scatter_dimension=0, tiled=True)

    expert_grads = [weight_grad(cots, acts), weight_grad(inputs, gate_grads), weight_grad(inputs, up_grads)]

    gates = gates_of(ffn_in, routes[0])
    grad_logits = gates * (d_gates - jnp.sum(gates * d_gates, axis=-1, keepdims=True))
    grad_ffn_in = grad_ffn_in + dot(
        grad_logits, router_w.astype(F32), ((1,), (1,)), precision=lax.Precision.HIGHEST
    )
    d_router = dot(grad_logits, ffn_in.astype(F32), ((0,), (0,)), precision=lax.Precision.HIGHEST)
    d_router = block(sum_all(d_router), mine, slab, 1).T
    d_ffn_gain = jnp.sum(grad_ffn_in * hidden * factor_two, axis=0)
    inner = grad_ffn_in * ffn_gain
    grad_hidden = (
        cot_low.astype(F32)
        + factor_two * inner
        - hidden * (factor_two * factor_two * factor_two) * jnp.mean(inner * hidden, axis=-1, keepdims=True)
    )

    output = hidden + ring_scatter(term_of(after(weighted, grad_ffn_in)))
    grad_hidden = in_order(grad_hidden)

    grad_proj = fsdp_gather(grad_hidden.astype(BF), 0)
    grad_mixed = in_order(to_pairs(dot_nt(grad_proj, w_out).astype(BF), 1))
    grads, head_gains = attend_back(qkv, grad_mixed, q_gain, k_gain, cosine, sine)
    if repeats > 1:
        head_gains = jnp.where(place % repeats == 0, head_gains, 0.0)
    grads = in_order(from_pairs(grads))
    across = swap(grads, 2)
    grad_normed = sum(
        dot_nt(piece, projections[mask])
        for mask, piece in enumerate([grads, swap(grads, 1), across, swap(across, 1)])
    ).astype(BF)
    grad_normed = assemble(
        [block(grad_normed, mine, rows, 0)]
        + [swap(block(grad_normed, mine ^ mask, rows, 0), mask) for mask in range(1, parts)],
        1,
    ).astype(F32)
    d_attn_gain = jnp.sum(grad_normed * source * factor_one, axis=0)
    inner = grad_normed * attn_gain
    d_tokens = (
        grad_hidden
        + factor_one * inner
        - source * (factor_one * factor_one * factor_one) * jnp.mean(inner * source, axis=-1, keepdims=True)
    )

    own_rows = slab // ctx_size

    def gather_rows(pieces, count):
        pieces = ring_gather(pieces)
        wholes = [jnp.zeros((slab, width), F32) for _ in range(count)]
        for offset, piece in pieces.items():
            at = ((ring_place + offset) % ctx_size) * own_rows
            for index in range(count):
                part = piece[index * own_rows : (index + 1) * own_rows].astype(F32)
                wholes[index] = lax.dynamic_update_slice_in_dim(wholes[index], part, at, 0)
        return wholes

    grad = dot_tn(mixed, grad_proj)
    d_out = ring_scatter(lambda offset: block(grad, (ring_place + offset) % ctx_size, own_rows, 0))
    (d_out,) = gather_rows(d_out.astype(BF), 1)

    all_grads = dot_tn(normed_all, grads).reshape(parts, ctx_size, own_rows, -1)
    total = ring_scatter(
        lambda offset: block(all_grads, (ring_place + offset) % ctx_size, 1, 1).reshape(parts * own_rows, -1)
    )
    total = total.astype(BF).reshape(parts, own_rows, -1)
    pieces = [block(total, mine ^ mask, 1, 0)[0] for mask in range(parts)]
    pieces = [piece if mask == 0 else swap(piece, mask) for mask, piece in enumerate(pieces)]
    pieces = [
        jnp.concatenate([piece[:, kind * own_width : (kind + 1) * own_width] for kind in range(3)]) for piece in pieces
    ]
    pieces = assemble(pieces, 1)
    d_down, d_gate, d_up = [
        grad.astype(F32).reshape(slab, own_experts, hidden_units) for grad in after(expert_grads, pieces)
    ]
    d_query, d_key, d_value = gather_rows(pieces, 3)
    gains = jnp.concatenate([d_attn_gain, head_gains[0], head_gains[1], d_ffn_gain])
    gains = sum_all(gains.reshape(-1, 128)).reshape(-1)
    return (
        output[None].astype(BF),
        d_tokens[None],
        gains[:width],
        d_query,
        d_key,
        d_value,
        gains[width : width + head_dim],
        gains[width + head_dim : width + 2 * head_dim],
        d_out,
        gains[width + 2 * head_dim :],
        d_router,
        d_gate,
        d_up,
        d_down,
    )


def solution(mesh):
    token_split = P("fsdp", "ctx", None)
    row_split = P("fsdp", None)
    return jax.shard_map(
        body,
        mesh=mesh,
        in_specs=(
            token_split, P(), row_split, row_split, row_split, P(), P(), row_split,
            P(), row_split, token_split, token_split, token_split, token_split, token_split,
        ),
        out_specs=(
            token_split, token_split, P(), row_split, row_split, row_split, P(), P(),
            row_split, P(), row_split, token_split, token_split, token_split,
        ),
        check_vma=False,
    )
```

```python
import functools

import jax
import jax.numpy as jnp
import numpy as np
from jax import lax
from jax.experimental import pallas as pl
from jax.experimental.pallas import tpu as pltpu
from jax.sharding import PartitionSpec as P

EPSILON = 1e-06
ROPE_BASE = 10000.0
BF = jnp.bfloat16
F32 = jnp.float32
LONG = pl.CostEstimate(flops=10**12, bytes_accessed=10**9, transcendentals=0)
MEDIUM = pl.CostEstimate(flops=2 * 10**10, bytes_accessed=5 * 10**7, transcendentals=0)
SMALL = pl.CostEstimate(flops=1, bytes_accessed=1, transcendentals=0)


def dot(a, b, contract=((1,), (0,)), precision=None):
    return lax.dot_general(a, b, (contract, ((), ())), precision=precision, preferred_element_type=F32)


def dot_nt(a, b):
    return dot(a, b, ((1,), (1,)))


def dot_tn(a, b):
    return dot(a, b, ((0,), (0,)))


def head_norm(v, gain):
    factor = lax.rsqrt(jnp.mean(v * v, axis=-1, keepdims=True) + EPSILON)
    return v * factor * gain, factor


def turn(v, cosine, sine):
    return v * cosine + pltpu.roll(v, v.shape[-1] // 2, 1) * sine


def head_back(grad, v, gain, cosine, sine):
    grad = turn(grad, cosine, -sine)
    factor = lax.rsqrt(jnp.mean(v * v, axis=-1, keepdims=True) + EPSILON)
    gain_grad = jnp.sum(grad * v * factor, axis=0, keepdims=True)
    inner = grad * gain
    return factor * inner - v * (factor * factor * factor) * jnp.mean(inner * v, axis=-1, keepdims=True), gain_grad


def rows_of(ref):
    block = ref[...]
    return block.reshape(-1, block.shape[-1])


def attend_kernel(q_ref, k_ref, v_ref, qg_ref, kg_ref, cos_ref, sin_ref, o_ref, keys, values_t):
    step = pl.program_id(1)

    @pl.when(step == 0)
    def _():
        normed, _unused = head_norm(rows_of(k_ref).astype(F32), kg_ref[...])
        keys[...] = turn(normed, cos_ref[...], sin_ref[...]).astype(BF)
        values_t[...] = rows_of(v_ref).astype(F32).T.astype(BF)

    queries = rows_of(q_ref).astype(F32)
    number, head_dim = queries.shape
    here = pl.ds(pl.multiple_of(step * number, number), number)
    normed, _unused = head_norm(queries, qg_ref[...])
    queries = turn(normed, cos_ref[here, :], sin_ref[here, :]).astype(BF)
    weights = jnp.exp(dot_nt(keys[...], queries) * (head_dim**-0.5))
    total = jnp.sum(weights, axis=0, keepdims=True)
    mixed = dot(values_t[...], weights.astype(BF)) / total
    o_ref[...] = mixed.T.astype(BF).reshape(o_ref.shape)


def attend_back_kernel(
    q_ref, k_ref, v_ref, m_ref, qg_ref, kg_ref, cos_ref, sin_ref,
    g_ref, gain_ref, keys, keys_t, key_acc, value_acc,
):
    pair = pl.program_id(0)
    step = pl.program_id(1)
    last = pl.num_programs(1) - 1

    @pl.when((pair == 0) & (step == 0))
    def _():
        gain_ref[...] = jnp.zeros_like(gain_ref)

    @pl.when(step == 0)
    def _():
        normed, _unused = head_norm(rows_of(k_ref).astype(F32), kg_ref[...])
        turned = turn(normed, cos_ref[...], sin_ref[...])
        keys[...] = turned.astype(BF)
        keys_t[...] = turned.T.astype(BF)
        key_acc[...] = jnp.zeros_like(key_acc)
        value_acc[...] = jnp.zeros_like(value_acc)

    query_pre = rows_of(q_ref).astype(F32)
    grad_mixed = rows_of(m_ref)
    number, head_dim = query_pre.shape
    scale = head_dim**-0.5
    here = pl.ds(pl.multiple_of(step * number, number), number)
    cosine, sine = cos_ref[here, :], sin_ref[here, :]
    normed, _unused = head_norm(query_pre, qg_ref[...])
    queries = turn(normed, cosine, sine).astype(BF)
    weights = jnp.exp(dot_nt(keys[...], queries) * scale)
    probs = weights * (1.0 / jnp.sum(weights, axis=0, keepdims=True))
    value_acc[...] += dot(probs.astype(BF), grad_mixed)
    weighted = probs * dot_nt(rows_of(v_ref), grad_mixed)
    delta = jnp.sum(weighted, axis=0, keepdims=True)
    grad_scores = (weighted - probs * delta).astype(BF)
    key_acc[...] += dot(grad_scores, queries)
    grad_query = dot(keys_t[...], grad_scores).T * scale
    grad_query, gain_grad = head_back(grad_query, query_pre, qg_ref[...], cosine, sine)
    rows = g_ref.shape[2]
    blocks = number // rows
    g_ref[pl.ds(step * blocks, blocks), 0] = grad_query.astype(BF).reshape(blocks, rows, head_dim)
    gain_ref[0:1, :] += gain_grad

    @pl.when(step == last)
    def _():
        grad_key, gain_grad = head_back(
            key_acc[...] * scale, rows_of(k_ref).astype(F32), kg_ref[...], cos_ref[...], sin_ref[...]
        )
        g_ref[:, 1] = grad_key.astype(BF).reshape(-1, rows, head_dim)
        g_ref[:, 2] = value_acc[...].astype(BF).reshape(-1, rows, head_dim)
        gain_ref[1:2, :] += gain_grad


def attention_specs(shape):
    blocks, pairs, rows, head_dim = shape
    at_once = max(1, 256 // rows)
    while blocks % at_once:
        at_once -= 1
    pairs //= 3
    part = pl.BlockSpec((at_once, 1, rows, head_dim), lambda p, i: (i, p, 0, 0))
    three = [
        pl.BlockSpec((at_once, 1, rows, head_dim), lambda p, i: (i, 3 * p, 0, 0)),
        pl.BlockSpec((blocks, 1, rows, head_dim), lambda p, i: (0, 3 * p + 1, 0, 0)),
        pl.BlockSpec((blocks, 1, rows, head_dim), lambda p, i: (0, 3 * p + 2, 0, 0)),
    ]
    gain = pl.BlockSpec((1, head_dim), lambda p, i: (0, 0))
    table = pl.BlockSpec((blocks * rows, head_dim), lambda p, i: (0, 0))
    params = pltpu.CompilerParams(
        dimension_semantics=("arbitrary", "arbitrary"),
        vmem_limit_bytes=(24 if blocks * rows <= 1024 else 56) * 2**20,
    )
    return part, three, gain, table, (pairs, blocks // at_once), params


def attend(qkv, query_gain, key_gain, cosine, sine):
    part, three, gain, table, grid, params = attention_specs(qkv.shape)
    blocks, _unused, rows, head_dim = qkv.shape
    length = blocks * rows
    return pl.pallas_call(
        attend_kernel,
        grid=grid,
        in_specs=[*three, gain, gain, table, table],
        out_specs=part,
        out_shape=jax.ShapeDtypeStruct((blocks, grid[0], rows, head_dim), BF),
        scratch_shapes=[pltpu.VMEM((length, head_dim), BF), pltpu.VMEM((head_dim, length), BF)],
        compiler_params=params,
        cost_estimate=MEDIUM,
        name="attend",
    )(qkv, qkv, qkv, query_gain, key_gain, cosine, sine)


def attend_back(qkv, grad_mixed, query_gain, key_gain, cosine, sine):
    part, three, gain, table, grid, params = attention_specs(qkv.shape)
    blocks, _unused, rows, head_dim = qkv.shape
    length = blocks * rows
    return pl.pallas_call(
        attend_back_kernel,
        grid=grid,
        in_specs=[*three, part, gain, gain, table, table],
        out_specs=[
            pl.BlockSpec((blocks, 3, rows, head_dim), lambda p, i: (0, p, 0, 0)),
            pl.BlockSpec((8, head_dim), lambda p, i: (0, 0)),
        ],
        out_shape=[jax.ShapeDtypeStruct(qkv.shape, BF), jax.ShapeDtypeStruct((8, head_dim), F32)],
        scratch_shapes=[
            pltpu.VMEM((length, head_dim), BF),
            pltpu.VMEM((head_dim, length), BF),
            pltpu.VMEM((length, head_dim), F32),
            pltpu.VMEM((length, head_dim), F32),
        ],
        compiler_params=params,
        cost_estimate=LONG,
        name="attend_back",
    )(qkv, qkv, qkv, grad_mixed, query_gain, key_gain, cosine, sine)


def stack_blocks(block_refs, out_ref):
    rows = block_refs[0].shape[0]
    for index, block_ref in enumerate(block_refs):
        out_ref[index * rows : (index + 1) * rows, :] = block_ref[...]


def stacked_kernel(w_ref, *refs):
    *block_refs, o_ref, rows_ref = refs

    @pl.when(pl.program_id(0) == 0)
    def _():
        stack_blocks(block_refs, rows_ref)

    o_ref[...] = dot(rows_ref[...], w_ref[...])


def stacked_matmul(blocks, weight):
    rows, depth = len(blocks) * blocks[0].shape[0], weight.shape[0]
    wide = min(512, weight.shape[1])
    return pl.pallas_call(
        stacked_kernel,
        grid=(weight.shape[1] // wide,),
        in_specs=[pl.BlockSpec((depth, wide), lambda n: (0, n))]
        + [pl.BlockSpec(block.shape, lambda n: (0, 0)) for block in blocks],
        out_specs=[pl.BlockSpec((rows, wide), lambda n: (0, n)), pl.BlockSpec((rows, depth), lambda n: (0, 0))],
        out_shape=[jax.ShapeDtypeStruct((rows, weight.shape[1]), F32), jax.ShapeDtypeStruct((rows, depth), BF)],
        compiler_params=pltpu.CompilerParams(dimension_semantics=("arbitrary",), vmem_limit_bytes=56 * 2**20),
        cost_estimate=LONG,
        name="stacked_matmul",
    )(weight, *blocks)


def routed_gates(logits, routes):
    columns = lax.broadcasted_iota(jnp.int32, logits.shape, 1)
    chosen = columns == routes[:, 0:1]
    for index in range(1, routes.shape[1]):
        chosen = chosen | (columns == routes[:, index : index + 1])
    high = jnp.max(jnp.where(chosen, logits, -1e30), axis=-1, keepdims=True)
    weights = jnp.where(chosen, jnp.exp(jnp.where(chosen, logits - high, 0.0)), 0.0)
    return weights / jnp.sum(weights, axis=-1, keepdims=True)


def expert_kernel(table_ref, router_ref, routes_ref, gate_w_ref, up_w_ref, grad_ref, *refs, per, place, at):
    *block_refs, act_ref, gate_ref, up_ref, d_gates_ref, x_ref, gates_ref = refs
    step = pl.program_id(0)

    @pl.when(step == 0)
    def _():
        stack_blocks(block_refs, x_ref)
        routes = jnp.concatenate([routes_ref[table_ref[at + index]] for index in range(len(block_refs))], axis=0)
        gates = routed_gates(dot(x_ref[...], router_ref[...]), routes)
        columns = lax.broadcasted_iota(jnp.int32, gates.shape, 1)
        count = gates_ref.shape[0]
        for index in range(count):
            here = columns == table_ref[place] * count + index
            gates_ref[index] = jnp.sum(jnp.where(here, gates, 0.0), axis=1, keepdims=True)

    @pl.when(step % per == 0)
    def _():
        d_gates_ref[...] = jnp.zeros_like(d_gates_ref)

    gate_pre = dot(x_ref[...], gate_w_ref[...])
    up_pre = dot(x_ref[...], up_w_ref[...])
    grad_act = grad_ref[...]
    gates = gates_ref[step // per]
    sigmoid = 1.0 / (1.0 + jnp.exp(-gate_pre))
    silu = gate_pre * sigmoid
    act = (silu * up_pre).astype(BF).astype(F32)
    d_gates_ref[0] += jnp.sum(act * grad_act, axis=1, keepdims=True)
    grad_act = grad_act * gates
    act_ref[...] = (act * gates).astype(BF)
    up_ref[...] = (grad_act * silu).astype(BF)
    gate_ref[...] = (grad_act * up_pre * (sigmoid * (1.0 + gate_pre * (1.0 - sigmoid)))).astype(BF)


def expert_units(table, place, at, group, blocks, routes, router_w, gate_w, up_w, grad_act, count):
    rows, width = len(blocks) * blocks[0].shape[0], blocks[0].shape[1]
    units = gate_w.shape[1]
    wide = min(512, units // count)
    per = units // wide // count
    weight = pl.BlockSpec((width, wide), lambda n: (0, n))
    tile = pl.BlockSpec((rows, wide), lambda n: (0, n))
    out = jax.ShapeDtypeStruct((rows, units), BF)
    return pl.pallas_call(
        functools.partial(expert_kernel, per=per, place=place, at=at),
        grid=(units // wide,),
        in_specs=[
            pl.BlockSpec(memory_space=pltpu.SMEM),
            pl.BlockSpec(router_w.shape, lambda n: (0, 0)),
            pl.BlockSpec(routes.shape, lambda n: (0, 0, 0)),
            weight,
            weight,
            pl.BlockSpec((rows, wide), lambda n: (group, n)),
        ]
        + [pl.BlockSpec(block.shape, lambda n: (0, 0)) for block in blocks],
        out_specs=[
            tile,
            tile,
            tile,
            pl.BlockSpec((1, rows, 1), lambda n: (n // per, 0, 0)),
            pl.BlockSpec((rows, width), lambda n: (0, 0)),
        ],
        out_shape=[
            out, out, out, jax.ShapeDtypeStruct((count, rows, 1), F32), jax.ShapeDtypeStruct((rows, width), BF),
        ],
        scratch_shapes=[pltpu.VMEM((count, rows, 1), F32)],
        compiler_params=pltpu.CompilerParams(dimension_semantics=("arbitrary",), vmem_limit_bytes=58 * 2**20),
        cost_estimate=LONG,
        name="expert_units",
    )(table, router_w, routes, gate_w, up_w, grad_act, *blocks)


def grouped(call, blocks, *arrays):
    size, rows = 8, blocks[0].shape[0]
    results = []
    for first in range(0, len(blocks), size):
        some = blocks[first : first + size]
        results.append(call(first, some, *[v[first * rows : (first + len(some)) * rows] for v in arrays]))
    if len(results) == 1:
        return results[0]
    return [jnp.concatenate(parts, axis=1 if parts[0].ndim == 3 else 0) for parts in zip(*results)]


def expert_rows_kernel(gate_ref, up_ref, gate_w_ref, up_w_ref, o_ref):
    o_ref[...] = (dot_nt(gate_ref[...], gate_w_ref[...]) + dot_nt(up_ref[...], up_w_ref[...])).astype(BF)


def expert_rows(gate_grads, up_grads, gate_w, up_w):
    rows, units = gate_grads.shape
    width = gate_w.shape[0]
    wide = min(512, width)
    whole = pl.BlockSpec((rows, units), lambda n: (0, 0))
    weight = pl.BlockSpec((wide, units), lambda n: (n, 0))
    return pl.pallas_call(
        expert_rows_kernel,
        grid=(width // wide,),
        in_specs=[whole, whole, weight, weight],
        out_specs=pl.BlockSpec((rows, wide), lambda n: (0, n)),
        out_shape=jax.ShapeDtypeStruct((rows, width), BF),
        compiler_params=pltpu.CompilerParams(dimension_semantics=("arbitrary",), vmem_limit_bytes=56 * 2**20),
        cost_estimate=LONG,
        name="expert_rows",
    )(gate_grads, up_grads, gate_w, up_w)


def times_kernel(a_ref, b_ref, o_ref):
    o_ref[...] = dot_nt(a_ref[...], b_ref[...]).astype(o_ref.dtype)


def times_transpose(a, b):
    (rows, depth), columns = a.shape, b.shape[0]
    wide = min(512, columns)
    return pl.pallas_call(
        times_kernel,
        grid=(columns // wide,),
        in_specs=[pl.BlockSpec((rows, depth), lambda n: (0, 0)), pl.BlockSpec((wide, depth), lambda n: (n, 0))],
        out_specs=pl.BlockSpec((rows, wide), lambda n: (0, n)),
        out_shape=jax.ShapeDtypeStruct((rows, columns), BF),
        compiler_params=pltpu.CompilerParams(dimension_semantics=("arbitrary",), vmem_limit_bytes=56 * 2**20),
        cost_estimate=LONG,
        name="times_transpose",
    )(a, b)


def sum_kernel(*refs):
    *pair_refs, o_ref = refs
    count = len(pair_refs) // 2
    total = dot_tn(pair_refs[0][...], pair_refs[count][...])
    for index in range(1, count):
        total = total + dot_tn(pair_refs[index][...], pair_refs[count + index][...])
    o_ref[...] = total.astype(o_ref.dtype)


def sum_of_outer(lefts, rights):
    rows, columns = lefts[0].shape[1], rights[0].shape[1]
    tall, wide = min(512, rows), columns if len(lefts) <= 2 else min(1024, columns)
    return pl.pallas_call(
        sum_kernel,
        grid=(columns // wide, rows // tall),
        in_specs=[pl.BlockSpec((left.shape[0], tall), lambda n, m: (0, m)) for left in lefts]
        + [pl.BlockSpec((right.shape[0], wide), lambda n, m: (0, n)) for right in rights],
        out_specs=pl.BlockSpec((tall, wide), lambda n, m: (m, n)),
        out_shape=jax.ShapeDtypeStruct((rows, columns), BF),
        compiler_params=pltpu.CompilerParams(
            dimension_semantics=("arbitrary", "arbitrary"), vmem_limit_bytes=56 * 2**20
        ),
        cost_estimate=LONG,
        name="sum_of_outer",
    )(*lefts, *rights)


NN, NT = ((1,), (0,)), ((1,), (1,))


def pairs_kernel(b_ref, *refs, contract, kinds, parts):
    *block_refs, o_ref, rows_ref = refs
    kind = pl.program_id(1)

    @pl.when((pl.program_id(0) == 0) & (kind == 0))
    def _():
        stack_blocks(block_refs, rows_ref)

    product = dot(rows_ref[...], b_ref[...], contract).astype(BF)
    rows, head_dim = o_ref.shape[2:]
    per = o_ref.shape[1] // kinds
    for pair in range(2 * parts):
        head, part = divmod(pair, parts)
        piece = product[part * rows : (part + 1) * rows, head * head_dim : (head + 1) * head_dim]
        o_ref[pair // per, pair % per * kinds + kind] = piece


def matmul_to_pairs(blocks, b, contract, kinds, per, head_dim, cost):
    parts, (rows, depth) = len(blocks), blocks[0].shape
    heads = b.shape[1 - contract[1][0]] // head_dim // kinds
    if contract[1][0] == 0:
        right = pl.BlockSpec((depth, 2 * head_dim), lambda h, k: (0, k * (heads // 2) + h))
    else:
        right = pl.BlockSpec((2 * head_dim, depth), lambda h, k: (k * (heads // 2) + h, 0))
    return pl.pallas_call(
        functools.partial(pairs_kernel, contract=contract, kinds=kinds, parts=parts),
        grid=(heads // 2, kinds),
        in_specs=[right] + [pl.BlockSpec((rows, depth), lambda h, k: (0, 0))] * parts,
        out_specs=pl.BlockSpec((2 * parts // per, per * kinds, rows, head_dim), lambda h, k: (h, 0, 0, 0)),
        out_shape=jax.ShapeDtypeStruct((heads * parts // per, per * kinds, rows, head_dim), BF),
        scratch_shapes=[pltpu.VMEM((parts * rows, depth), BF)],
        compiler_params=pltpu.CompilerParams(
            dimension_semantics=("arbitrary", "arbitrary"), vmem_limit_bytes=32 * 2**20
        ),
        cost_estimate=cost,
        name="matmul_to_pairs",
    )(b, *blocks)


def own_pairs_kernel(table_ref, *refs, parts, kinds, places):
    *piece_refs, o_ref, columns_ref, rows_ref = refs
    block_refs, piece_refs = piece_refs[:parts], piece_refs[parts:]
    head_step, kind = pl.program_id(0), pl.program_id(1)

    @pl.when((head_step == 0) & (kind == 0))
    def _():
        stack_blocks(block_refs, rows_ref)
        place_kernel(table_ref, *piece_refs, columns_ref, slabs=parts, places=places)

    rows, head_dim = o_ref.shape[2:]
    per = o_ref.shape[1] // kinds
    wide = 2 * head_dim
    at = (kind * pl.num_programs(0) + head_step) * wide
    product = dot(rows_ref[...], columns_ref[:, pl.ds(pl.multiple_of(at, wide), wide)]).astype(BF)
    for pair in range(2 * parts):
        head, part = divmod(pair, parts)
        piece = product[part * rows : (part + 1) * rows, head * head_dim : (head + 1) * head_dim]
        o_ref[pair // per, pair % per * kinds + kind] = piece


def own_pairs(table, blocks, pieces, places, kinds, per, head_dim):
    parts, (rows, depth) = len(blocks), blocks[0].shape
    columns = pieces[0].shape[1]
    heads = columns // head_dim // kinds
    whole = [pl.BlockSpec(v.shape, lambda h, k: (0, 0)) for v in (*blocks, *pieces)]
    return pl.pallas_call(
        functools.partial(own_pairs_kernel, parts=parts, kinds=kinds, places=places),
        grid=(heads // 2, kinds),
        in_specs=[pl.BlockSpec(memory_space=pltpu.SMEM)] + whole,
        out_specs=[
            pl.BlockSpec((2 * parts // per, per * kinds, rows, head_dim), lambda h, k: (h, 0, 0, 0)),
            pl.BlockSpec((depth, columns), lambda h, k: (0, 0)),
        ],
        out_shape=[
            jax.ShapeDtypeStruct((heads * parts // per, per * kinds, rows, head_dim), BF),
            jax.ShapeDtypeStruct((depth, columns), BF),
        ],
        scratch_shapes=[pltpu.VMEM((parts * rows, depth), BF)],
        compiler_params=pltpu.CompilerParams(
            dimension_semantics=("arbitrary", "arbitrary"), vmem_limit_bytes=48 * 2**20
        ),
        cost_estimate=SMALL,
        name="own_pairs",
    )(table, *blocks, *pieces)


def small_call(kernel, name, out_shape, *operands, cost=SMALL, scratch=(), **kwargs):
    vmem = pl.BlockSpec(memory_space=pltpu.VMEM)
    return pl.pallas_call(
        functools.partial(kernel, **kwargs),
        in_specs=[pl.BlockSpec(memory_space=pltpu.SMEM)] + [vmem] * (len(operands) - 1),
        out_specs=jax.tree.map(lambda _unused: vmem, out_shape),
        out_shape=out_shape,
        scratch_shapes=list(scratch),
        compiler_params=pltpu.CompilerParams(vmem_limit_bytes=40 * 2**20),
        cost_estimate=cost,
        name=name,
    )(*operands)


def pair_rows(ref, head, parts):
    per = ref.shape[1]
    return [ref[(head * parts + part) // per, (head * parts + part) % per] for part in range(parts)]


def mixed_out_kernel(_unused, m_ref, w_ref, *refs, parts):
    heads = m_ref.shape[0] * m_ref.shape[1] // parts
    pieces = [pair_rows(m_ref, head, parts) for head in range(heads)]
    for part, ref in enumerate(refs):
        ref[...] = dot(jnp.concatenate([p[part] for p in pieces], axis=1), w_ref[...]).astype(ref.dtype)


def mixed_out(table, mixed, w_out, parts):
    shape = (mixed.shape[2], w_out.shape[1])
    out = [jax.ShapeDtypeStruct(shape, kind) for kind in (F32, BF, F32, BF)]
    return small_call(mixed_out_kernel, "mixed_out", out, table, mixed, w_out, cost=MEDIUM, parts=parts)


def out_grads_kernel(table_ref, m_ref, *refs, parts, turn, own_rows):
    *block_refs, o_ref, mixed_ref, turned_ref, grads_ref = refs
    head_dim = m_ref.shape[3]
    for head in range(m_ref.shape[0] * m_ref.shape[1] // parts):
        rows = jnp.concatenate(pair_rows(m_ref, head, parts), axis=0)
        mixed_ref[head * head_dim : (head + 1) * head_dim, :] = rows.astype(F32).T.astype(BF)
    for index in range(mixed_ref.shape[0] // own_rows):
        at = pl.multiple_of(table_ref[turn + index] * own_rows, own_rows)
        turned_ref[index * own_rows : (index + 1) * own_rows, :] = mixed_ref[pl.ds(at, own_rows), :]
    stack_blocks(block_refs, grads_ref)
    o_ref[...] = dot(turned_ref[...], grads_ref[...])


def out_grads(table, mixed, blocks, turn, own_rows):
    parts, (rows, width) = len(blocks), blocks[0].shape
    features = mixed.shape[0] * mixed.shape[1] // parts * mixed.shape[3]
    side = pltpu.VMEM((features, parts * rows), BF)
    out = jax.ShapeDtypeStruct((features, width), F32)
    scratch = [side, side, pltpu.VMEM((parts * rows, width), BF)]
    return small_call(
        out_grads_kernel, "out_grads", out, table, mixed, *blocks, scratch=scratch, parts=parts, turn=turn,
        own_rows=own_rows,
    )


def turned_kernel(table_ref, *refs, turn, own_rows, parts, order):
    *block_refs, o_ref, rows_ref = refs
    rows, width = block_refs[0].shape
    slab = width // parts
    for index, block_ref in enumerate(block_refs):
        rows_ref[:, index * rows : (index + 1) * rows] = block_ref[...].astype(F32).T.astype(BF)
    for index in range(width // own_rows):
        step, first = divmod(index, parts)
        at = first * slab + table_ref[turn + order[step]] * own_rows
        o_ref[index * own_rows : (index + 1) * own_rows, :] = rows_ref[pl.ds(pl.multiple_of(at, own_rows), own_rows), :]


def turned_transpose(table, blocks, turn, own_rows, order):
    parts, (rows, width) = len(blocks), blocks[0].shape
    out = jax.ShapeDtypeStruct((width, parts * rows), BF)
    scratch = [pltpu.VMEM((width, parts * rows), BF)]
    return small_call(
        turned_kernel, "turned_transpose", out, table, *blocks, scratch=scratch, turn=turn, own_rows=own_rows,
        parts=parts, order=order,
    )


def pair_tile(g_ref, kind, kinds, parts):
    per = g_ref.shape[1] // kinds
    heads = []
    for head in range(2):
        pieces = [g_ref[pair // per, pair % per * kinds + kind] for pair in range(head * parts, (head + 1) * parts)]
        heads.append(jnp.concatenate(pieces, axis=0))
    return jnp.concatenate(heads, axis=1)


def pair_weights_kernel(g_ref, n_ref, dw_ref, *, kinds, parts):
    dw_ref[...] = dot(n_ref[...], pair_tile(g_ref, pl.program_id(1), kinds, parts)).astype(BF)


def pair_rows_kernel(g_ref, w_ref, *refs, kinds, parts):
    *out_refs, dn_ref = refs
    kind = pl.program_id(1)

    @pl.when((pl.program_id(0) == 0) & (kind == 0))
    def _():
        dn_ref[...] = jnp.zeros_like(dn_ref)

    dn_ref[...] += dot_nt(pair_tile(g_ref, kind, kinds, parts), w_ref[...])

    @pl.when((pl.program_id(0) == pl.num_programs(0) - 1) & (kind == kinds - 1))
    def _():
        for part, out_ref in enumerate(out_refs):
            rows = out_ref.shape[0]
            out_ref[...] = dn_ref[part * rows : (part + 1) * rows, :].astype(out_ref.dtype)


def pair_specs(grads, kinds, parts):
    places, slots, rows, head_dim = grads.shape
    heads = places * slots // kinds // parts
    per = slots // kinds
    block = pl.BlockSpec((2 * parts // per, slots, rows, head_dim), lambda h, k: (h, 0, 0, 0))
    params = pltpu.CompilerParams(dimension_semantics=("arbitrary", "arbitrary"), vmem_limit_bytes=48 * 2**20)
    return block, heads, 2 * head_dim, params


def pair_weights(grads, normed_t, kinds, parts, half):
    width, total = normed_t.shape
    block, heads, wide, params = pair_specs(grads, kinds, parts)
    return pl.pallas_call(
        functools.partial(pair_weights_kernel, kinds=kinds, parts=parts),
        grid=(heads // 2, kinds),
        in_specs=[block, pl.BlockSpec((width // 2, total), lambda h, k: (half, 0))],
        out_specs=pl.BlockSpec((width // 2, wide), lambda h, k: (0, k * (heads // 2) + h)),
        out_shape=jax.ShapeDtypeStruct((width // 2, kinds * heads * wide // 2), BF),
        compiler_params=params,
        cost_estimate=LONG,
        name="pair_weights",
    )(grads, normed_t)


def pair_normed(grads, columns, kinds, parts):
    rows, width = grads.shape[2], columns.shape[0]
    block, heads, wide, params = pair_specs(grads, kinds, parts)
    return pl.pallas_call(
        functools.partial(pair_rows_kernel, kinds=kinds, parts=parts),
        grid=(heads // 2, kinds),
        in_specs=[block, pl.BlockSpec((width, wide), lambda h, k: (0, k * (heads // 2) + h))],
        out_specs=[pl.BlockSpec((rows, width), lambda h, k: (0, 0))] * parts,
        out_shape=[jax.ShapeDtypeStruct((rows, width), kind) for kind in (F32, BF, F32, BF)],
        scratch_shapes=[pltpu.VMEM((parts * rows, width), F32)],
        compiler_params=params,
        cost_estimate=LONG,
        name="pair_normed",
    )(grads, columns)


def part_kernel(_unused, *refs, count):
    weights, outs = refs[:-count], refs[-count:]
    wide = weights[0].shape[1]
    per = len(weights) // count
    for index, weight in enumerate(weights):
        outs[index // per][:, index % per * wide : (index % per + 1) * wide] = weight[...]


def take_parts(table, weights, shape, places, cost):
    def spec(row, column):
        return pl.BlockSpec(shape, lambda i, t: (0 if row is None else t[row], t[column]))

    out = (shape[0], shape[1] * len(weights))
    return pl.pallas_call(
        functools.partial(part_kernel, count=len(places)),
        grid_spec=pltpu.PrefetchScalarGridSpec(
            num_scalar_prefetch=1,
            grid=(1,),
            in_specs=[spec(*where) for where in places for _unused in weights],
            out_specs=[pl.BlockSpec(out, lambda i, t: (0, 0))] * len(places),
        ),
        out_shape=[jax.ShapeDtypeStruct(out, weights[0].dtype)] * len(places),
        compiler_params=pltpu.CompilerParams(vmem_limit_bytes=32 * 2**20),
        cost_estimate=cost,
        name="take_parts",
    )(table, *[w for _unused in places for w in weights])


def stack_kernel(_unused, *refs):
    stack_blocks(refs[:-1], refs[-1])


def stack_rows(table, *pieces):
    rows = sum(piece.shape[0] for piece in pieces)
    out = jax.ShapeDtypeStruct((rows, pieces[0].shape[1]), pieces[0].dtype)
    return small_call(stack_kernel, "stack_rows", out, table, *pieces)


def place_kernel(table_ref, *refs, slabs, places):
    *pieces, out = refs
    slab = out.shape[0] // slabs
    for piece, (where, then) in zip(pieces, places):
        half = piece.shape[0] // len(where)
        for index, slot in enumerate(where):
            at = table_ref[slot] * slab
            if then is not None:
                at = at + table_ref[then] * half
            out[pl.ds(pl.multiple_of(at, half), half), :] = piece[index * half : (index + 1) * half, :]


def place_rows(table, pieces, slabs, places):
    rows = sum(piece.shape[0] for piece in pieces)
    out = jax.ShapeDtypeStruct((rows, pieces[0].shape[1]), pieces[0].dtype)
    return small_call(place_kernel, "place_rows", out, table, *pieces, slabs=slabs, places=places)


def total_kernel(table_ref, term_ref, right_ref, left_ref, *refs, slots):
    own_rows = refs[0].shape[0]
    for slot, ref in zip(slots, refs):
        slab = table_ref[slot]
        here = pl.ds(pl.multiple_of(slab * own_rows, own_rows), own_rows)
        ref[...] = (term_ref[here, :].astype(F32) + right_ref[here, :].astype(F32) + left_ref[here, :].astype(F32)).astype(BF)


def total_parts(table, term, right, left, slots):
    out = [jax.ShapeDtypeStruct((term.shape[0] // len(slots), term.shape[1]), BF)] * len(slots)
    return small_call(total_kernel, "total_parts", out, table, term, right, left, slots=slots)


def join_kernel(table_ref, below_ref, last_ref, *refs, slots, kinds):
    *pieces, out = refs
    own_rows, wide = pieces[0].shape[0], pieces[0].shape[1] // kinds
    for slot, piece in zip(slots, pieces):
        here = pl.ds(pl.multiple_of(table_ref[slot] * wide, wide), wide)
        for kind in range(kinds):
            out[kind * own_rows : (kind + 1) * own_rows, here] = piece[:, kind * wide : (kind + 1) * wide]
    out[kinds * own_rows : (kinds + 1) * own_rows, :] = below_ref[...].astype(BF)
    out[(kinds + 1) * own_rows :, :] = last_ref[...]


def join_columns(table, pieces, below, last, slots, kinds):
    rows, columns = pieces[0].shape
    height = rows * (kinds + 1) + last.shape[0]
    out = jax.ShapeDtypeStruct((height, columns // kinds * len(pieces)), pieces[0].dtype)
    return small_call(join_kernel, "join_columns", out, table, below, last, *pieces, slots=slots, kinds=kinds)


def pack_kernel(table_ref, early_ref, late_ref, o_ref, *, slot, experts):
    slab = o_ref.shape[1] // 4
    here = pl.ds(pl.multiple_of(table_ref[slot] * slab, slab), slab)
    o_ref[...] = jnp.zeros_like(o_ref)
    for index in range(experts):
        row = early_ref[index : index + 1, here].astype(BF)
        o_ref[index // 4 : index // 4 + 1, index % 4 * slab : (index % 4 + 1) * slab] = row
    o_ref[experts // 4 : experts // 4 + 1, :] = early_ref[experts : experts + 1, :].astype(BF)
    o_ref[experts // 4 + 1 : experts // 4 + 3, :] = late_ref[...].astype(BF)


def pack_gains(table, early, late, slot, experts):
    height = -(-(experts // 4 + 3) // 16) * 16
    out = jax.ShapeDtypeStruct((height, early.shape[1]), BF)
    return small_call(pack_kernel, "pack_gains", out, table, early, late, slot=slot, experts=experts)


def unpack_kernel(table_ref, *refs, back, experts):
    *pieces, router_ref, gains_ref, all_ref = refs
    height = all_ref.shape[1]
    for index, piece in enumerate(pieces):
        all_ref[index] = piece[piece.shape[0] - height :, :].astype(F32)
    total = all_ref[table_ref[back]]
    for place in range(1, len(pieces)):
        total = total + all_ref[table_ref[back + place]]
    slab = total.shape[1] // 4
    rows = [total[i // 4 : i // 4 + 1, i % 4 * slab : (i % 4 + 1) * slab] for i in range(experts)]
    router_ref[...] = jnp.concatenate(rows, axis=0).T
    gains_ref[...] = total[experts // 4 : experts // 4 + 3, :]


def unpack_gains(table, pieces, back, experts, height):
    width = pieces[0].shape[1]
    out = [jax.ShapeDtypeStruct((width // 4, experts), F32), jax.ShapeDtypeStruct((3, width), F32)]
    scratch = [pltpu.VMEM((len(pieces), height, width), F32)]
    return small_call(
        unpack_kernel, "unpack_gains", out, table, *pieces, scratch=scratch, back=back, experts=experts
    )


def spread_kernel(table_ref, *refs, slots, count, fresh):
    pieces = refs[: len(slots)]
    outs = refs[len(slots) + (0 if fresh else count) :][:count]
    wide_ref, sems = refs[-2:]
    own_rows = wide_ref.shape[1]
    copies = []
    for index, (slot, piece) in enumerate(zip(slots, pieces)):
        here = pl.ds(pl.multiple_of(table_ref[slot] * own_rows, own_rows), own_rows)
        for kind in range(count):
            at = index * count + kind
            wide_ref[at] = piece[kind * own_rows : (kind + 1) * own_rows, :].astype(F32)
            copies.append(pltpu.make_async_copy(wide_ref.at[at], outs[kind].at[here, :], sems.at[at]))
            copies[-1].start()
    for copy in copies:
        copy.wait()


def spread_rows(table, pieces, slots, shape, places, count, before):
    vmem, anywhere = pl.BlockSpec(memory_space=pltpu.VMEM), pl.BlockSpec(memory_space=pl.ANY)
    number = len(pieces) * count
    fresh = before is None
    own_rows = shape[0] // places
    return pl.pallas_call(
        functools.partial(spread_kernel, slots=slots, count=count, fresh=fresh),
        in_specs=[pl.BlockSpec(memory_space=pltpu.SMEM)] + [vmem] * len(pieces) + [anywhere] * (0 if fresh else count),
        out_specs=[anywhere] * count,
        out_shape=[jax.ShapeDtypeStruct(shape, F32)] * count,
        input_output_aliases={} if fresh else {1 + len(pieces) + kind: kind for kind in range(count)},
        scratch_shapes=[pltpu.VMEM((number, own_rows, shape[1]), F32), pltpu.SemaphoreType.DMA((number,))],
        compiler_params=pltpu.CompilerParams(vmem_limit_bytes=24 * 2**20),
        cost_estimate=SMALL,
        name="spread_rows",
    )(table, *pieces, *([] if fresh else before))


def merge_kernel(w_ref, o_ref):
    units = w_ref.shape[2]
    for index in range(w_ref.shape[1]):
        o_ref[:, index * units : (index + 1) * units] = w_ref[:, index, :]


def merge_experts(weight):
    rows, count, units = weight.shape
    at_once = 128
    return pl.pallas_call(
        merge_kernel,
        grid=(rows // at_once,),
        in_specs=[pl.BlockSpec((at_once, count, units), lambda m: (m, 0, 0))],
        out_specs=pl.BlockSpec((at_once, count * units), lambda m: (m, 0)),
        out_shape=jax.ShapeDtypeStruct((rows, count * units), weight.dtype),
        cost_estimate=MEDIUM,
        name="merge_experts",
    )(weight)


def split_kernel(w_ref, o_ref):
    units = o_ref.shape[2]
    for index in range(o_ref.shape[1]):
        o_ref[:, index, :] = w_ref[:, index * units : (index + 1) * units].astype(F32)


def split_experts(grad, count):
    rows, columns = grad.shape
    at_once = 128
    return pl.pallas_call(
        split_kernel,
        grid=(rows // at_once,),
        in_specs=[pl.BlockSpec((at_once, columns), lambda m: (m, 0))],
        out_specs=pl.BlockSpec((at_once, count, columns // count), lambda m: (m, 0, 0)),
        out_shape=jax.ShapeDtypeStruct((rows, count, columns // count), F32),
        cost_estimate=SMALL,
        name="split_experts",
    )(grad)


def swap(v, mask):
    size = lax.axis_size("fsdp")
    return lax.ppermute(v, "fsdp", [(i, i ^ mask) for i in range(size)])


def ring_order(size):
    if size == 8:
        return [0, 2, 4, 6, 7, 5, 3, 1]
    return list(range(size))


def ring_send(v, direction):
    order = ring_order(lax.axis_size("ctx"))
    size = len(order)
    return lax.ppermute(v, "ctx", [(order[i], order[(i + direction) % size]) for i in range(size)])


class Ring:
    def __init__(self, steps):
        self.steps = steps
        self.value = None
        self.flying = False
        self.advance()

    def advance(self):
        try:
            next(self.steps)
            self.flying = not self.flying
        except StopIteration as end:
            self.value = end.value

    def land(self):
        if self.value is None and self.flying:
            self.advance()

    def step(self):
        self.land()
        if self.value is None:
            self.advance()

    def finish(self):
        while self.value is None:
            self.step()
        return self.value


def ring_gather(v, in_order, found):
    size = lax.axis_size("ctx")
    far, half = size // 2, v.shape[0] // 2
    found[0] = v
    right, left = v, v
    for step in range(1, far):
        right, left = ring_send(right, 1), ring_send(left, -1)
        yield
        right, left = in_order(right, left)
        found[size - step], found[step] = right, left
        yield
    right, left = ring_send(right[:half], 1), ring_send(left[half:], -1)
    yield
    found[far] = jnp.concatenate(in_order(right, left))
    yield
    return found


def ring_scatter(term, in_order, last=None):
    size = lax.axis_size("ctx")
    far = size // 2
    first = term(far)
    half = first.shape[0] // 2
    right, left = ring_send(first[:half].astype(BF), 1), ring_send(first[half:].astype(BF), -1)
    for offset in range(far - 1, 0, -1):
        yield
        right, left = in_order(right, left)
        yield
        ahead, behind = term(offset), term(size - offset)
        if offset == far - 1:
            ahead = jnp.concatenate([ahead[:half].astype(F32) + right.astype(F32), ahead[half:].astype(F32)])
            behind = jnp.concatenate([behind[:half].astype(F32), behind[half:].astype(F32) + left.astype(F32)])
        else:
            ahead, behind = ahead.astype(F32) + right.astype(F32), behind.astype(F32) + left.astype(F32)
        right, left = ring_send(ahead.astype(BF), 1), ring_send(behind.astype(BF), -1)
    yield
    right, left = in_order(right, left)
    yield
    if last is not None:
        return last(term(0), right, left)
    return term(0).astype(F32) + right.astype(F32) + left.astype(F32)


def after(v, *others):
    return lax.optimization_barrier((v, *others))[0]


class Order:
    def __init__(self, first):
        self.last = first

    def __call__(self, *values):
        self.last, *values = lax.optimization_barrier((self.last, *values))
        return values[0] if len(values) == 1 else values


def sum_fsdp(v, in_order):
    size = lax.axis_size("fsdp")
    mask = 1
    while mask < size:
        other = swap(v, mask)
        yield
        v = v + in_order(other)
        yield
        mask *= 2
    return v


def body(
    tokens, attn_gain, w_query, w_key, w_value, query_gain, key_gain, w_out,
    ffn_gain, w_router, w_gate, w_up, w_down, routes, cotangent,
):
    ctx_size = lax.axis_size("ctx")
    parts = lax.axis_size("fsdp")
    rows = tokens.shape[1]
    width = tokens.shape[2]
    slab = w_query.shape[0]
    head_dim = query_gain.shape[0]
    own_heads = width // head_dim // parts
    own_width = own_heads * head_dim
    own_rows = slab // ctx_size
    own_experts = w_gate.shape[1]
    hidden_units = w_gate.shape[2]
    experts = own_experts * ctx_size
    seq_length = rows * ctx_size
    in_order = Order(jnp.zeros((), F32))

    order = ring_order(ctx_size)
    offsets = [0] + [o for step in range(1, ctx_size // 2) for o in (step, ctx_size - step)] + [ctx_size // 2]
    at_ring, at_place, at_slab = 0, 1, [2 + mask for mask in range(parts)]
    at_from = 2 + parts
    at_blocks = {offset: at_from + ctx_size + index for index, offset in enumerate(offsets)}
    at_turn = at_from + 2 * ctx_size
    at_back = at_from + 3 * ctx_size
    lines = []
    for place in range(ctx_size):
        ring_place = order.index(place)
        for mine in range(parts):
            line = [ring_place, place] + [mine ^ mask for mask in range(parts)]
            line += [order[(ring_place + offset) % ctx_size] for offset in offsets]
            line += [(ring_place + offset) % ctx_size for offset in offsets]
            line += [(ring_place + index) % ctx_size for index in range(ctx_size)]
            line += [offsets.index((order.index(other) - ring_place) % ctx_size) for other in range(ctx_size)]
            lines.append(line)
    device = lax.axis_index("ctx").astype(jnp.uint32) * parts + lax.axis_index("fsdp").astype(jnp.uint32)
    table = lax.dynamic_slice(jnp.asarray(np.array(lines, np.int32)), (device, jnp.uint32(0)), (1, len(lines[0])))
    table = table.reshape(-1)

    pairs = own_heads * parts
    per = max(1, pairs // ctx_size)
    repeats = max(1, ctx_size // pairs)

    def spread_pairs(v):
        if repeats > 1:
            v = jnp.repeat(v, repeats, axis=0)
        return lax.all_to_all(v, "ctx", split_axis=0, concat_axis=0, tiled=True)

    def collect_pairs(v):
        v = lax.all_to_all(v, "ctx", split_axis=0, concat_axis=0, tiled=True)
        return v[::repeats] if repeats > 1 else v

    projections = (w_query, w_key, w_value)
    ring_row = table[at_ring].astype(jnp.uint32) * own_rows

    def fetched_part(slot):
        column = table[slot].astype(jnp.uint32) * own_width
        parts_of = [lax.dynamic_slice(w, (ring_row, column), (own_rows, own_width)) for w in projections]
        return jnp.concatenate(parts_of, axis=1)

    fetched = in_order(fetched_part(at_slab[2]), fetched_part(at_slab[3]))
    fetched = swap(fetched[0], 2), swap(fetched[1], 3)
    source = tokens[0].astype(F32)
    factor_one = lax.rsqrt(jnp.mean(source * source, axis=-1, keepdims=True) + EPSILON)
    normed = (source * factor_one * attn_gain).astype(BF)
    projections = after(projections, in_order.last)
    near, own = in_order(
        *take_parts(table, projections, (slab, own_width), [(None, at_slab[1]), (None, at_slab[0])], MEDIUM)
    )
    fetched = in_order(*fetched)
    column_blocks = {}
    ring = Ring(ring_gather(stack_rows(table, *fetched), in_order, column_blocks))
    normed, near = after((normed, near), fetched)
    across, beside, near = swap(normed, 2), swap(normed, 1), swap(near, 1)
    w_router = after(w_router, in_order.last)
    router = [w_router, swap(w_router, 1), swap(w_router, 2), swap(w_router, 3)]
    routes = after(routes, in_order.last)
    routes_all = lax.all_to_all(
        jnp.broadcast_to(routes, (ctx_size, *routes.shape[1:])), "ctx", split_axis=0, concat_axis=0, tiled=True
    )
    w_down = in_order(merge_experts(after(w_down, in_order.last)))
    ring.step()
    down_w = lax.all_gather(w_down, "fsdp", axis=0, tiled=True)
    across = after(across, in_order.last)
    diagonal = swap(across, 1)
    w_gate = in_order(merge_experts(after(w_gate, in_order.last)))
    ring.step()
    gate_w = lax.all_gather(w_gate, "fsdp", axis=0, tiled=True)
    normed = in_order(normed, beside, across, diagonal)
    w_up = in_order(merge_experts(after(w_up, in_order.last)))
    ring.step()
    up_w = lax.all_gather(w_up, "fsdp", axis=0, tiled=True)

    half = head_dim // 2
    frequency = ROPE_BASE ** (-jnp.arange(half, dtype=F32) * 2.0 / head_dim)
    angles = jnp.arange(seq_length, dtype=jnp.int32).astype(F32)[:, None] * frequency[None, :]
    cosine, sine = jnp.cos(angles), jnp.sin(angles)
    cosine = jnp.concatenate([cosine, cosine], axis=1)
    sine = jnp.concatenate([-sine, sine], axis=1)
    q_gain, k_gain = query_gain[None, :], key_gain[None, :]

    ring.finish()
    routes_all = in_order(routes_all)
    qkv, own_columns = own_pairs(
        table,
        normed,
        [own, near] + [column_blocks[offset] for offset in offsets],
        [((at_slab[0],), None), ((at_slab[1],), None)]
        + [((at_slab[2], at_slab[3]), at_blocks[offset]) for offset in offsets],
        3,
        per,
        head_dim,
    )
    qkv = spread_pairs(in_order(qkv))
    router = after(router, in_order.last)
    router_w = in_order(place_rows(table, router, parts, [((slot,), None) for slot in at_slab]))
    qkv = in_order(qkv)
    down_w = in_order(down_w)
    cot_blocks = {}
    ring = Ring(ring_gather(after(cotangent[0], qkv), in_order, cot_blocks))
    mixed = in_order(attend(qkv, q_gain, k_gain, cosine, sine))
    ring.step()
    mixed = in_order(collect_pairs(mixed))
    ring.step()
    hidden, near, across, far = in_order(*mixed_out(table, mixed, w_out, parts))
    far, near = swap(far, 1), swap(near, 1)
    far = in_order((across + in_order(far).astype(F32)).astype(BF))
    far = swap(far, 2)
    hidden = in_order(source + hidden + in_order(near).astype(F32))
    ring.step()
    hidden = hidden + in_order(far).astype(F32)
    factor_two = lax.rsqrt(jnp.mean(hidden * hidden, axis=-1, keepdims=True) + EPSILON)
    ffn_in = in_order((hidden * factor_two * ffn_gain).astype(BF))

    ffn_blocks = {}
    ffn_ring = Ring(ring_gather(ffn_in, in_order, ffn_blocks))
    gate_w = in_order(gate_w)
    ring.finish()
    ffn_ring.step()
    grad_act, cots = in_order(
        *grouped(lambda _unused, blocks: stacked_matmul(blocks, down_w), [cot_blocks[o] for o in offsets])
    )
    ffn_ring.step()

    size = 4
    groups = [offsets[first : first + size] for first in range(0, ctx_size, size)]

    def group_units(group):
        if group > 0:
            ffn_ring.finish()
        return in_order(
            *expert_units(
                table, at_place, at_from + group * size, group, [ffn_blocks[o] for o in groups[group]], routes_all,
                router_w, gate_w, up_w, grad_act, own_experts,
            )
        )

    up_w = in_order(up_w)
    units = [group_units(0)]
    order_of_rows = [ctx_size // 2] + [o for step in range(ctx_size // 2 - 1, 0, -1) for o in (step, ctx_size - step)]
    order_of_rows += [0]
    ffn_ring.step()
    normed_t = in_order(turned_transpose(table, after(normed, in_order.last), at_turn, own_rows, order_of_rows))
    for group in range(1, len(groups)):
        units.append(group_units(group))
    acts, gate_grads, up_grads, d_gates, inputs = zip(*units)

    def term_of(terms):
        def term(offset):
            group, index = divmod(offsets.index(offset), size)
            return terms[group][index * rows : (index + 1) * rows]

        return term

    def weight_grad(lefts, rights):
        lefts, rights = after((lefts, rights), in_order.last)
        return in_order(sum_of_outer(lefts, rights))

    def share(grad):
        return lax.psum_scatter(after(grad, in_order.last), "fsdp", scatter_dimension=0, tiled=True)

    grad_rows, weighted = {}, {}

    def make_rows(group):
        some = after((gate_grads[group], up_grads[group]), in_order.last)
        grad_rows[group] = in_order(expert_rows(*some, gate_w, up_w))

    for group in range(len(groups) - 1, 0, -1):
        make_rows(group)
    row_ring = Ring(ring_scatter(term_of(grad_rows), in_order))
    make_rows(0)
    row_ring.step()
    for group in range(len(groups) - 1, -1, -1):
        weighted[group] = in_order(times_transpose(after(acts[group], in_order.last), down_w))
    row_ring.step()
    d_gates = jnp.concatenate(after(d_gates, in_order.last), axis=1).reshape(own_experts, ctx_size, rows)
    d_gates = d_gates.at[:, table[at_back : at_back + ctx_size], :].get(mode="promise_in_bounds").transpose(1, 0, 2)
    d_gates = lax.all_to_all(d_gates, "ctx", split_axis=0, concat_axis=0, tiled=True)
    row_ring.step()
    d_gates = in_order(d_gates).reshape(experts, rows).T
    gates = routed_gates(dot(ffn_in, router_w), routes[0])
    grad_logits = gates * (d_gates - jnp.sum(gates * d_gates, axis=-1, keepdims=True))
    routed = dot(grad_logits, router_w.astype(F32), ((1,), (1,)), precision=lax.Precision.HIGHEST)
    routed = in_order(routed)
    grad_ffn_in = row_ring.finish() + routed

    inner = grad_ffn_in * ffn_gain
    grad_hidden = (
        cotangent[0].astype(F32)
        + factor_two * inner
        - hidden * (factor_two * factor_two * factor_two) * jnp.mean(inner * hidden, axis=-1, keepdims=True)
    )
    grad_proj, grad_hidden, grad_ffn_in = in_order(grad_hidden.astype(BF), grad_hidden, grad_ffn_in)

    across, beside = swap(grad_proj, 2), swap(grad_proj, 1)
    ring = Ring(ring_scatter(term_of(weighted), in_order))
    d_gate = weight_grad(inputs, gate_grads)
    ring.land()
    across = in_order(across)
    d_gate = share(d_gate)
    grad_proj = in_order(grad_proj, beside, across, swap(across, 1))
    ring.step()
    grad_mixed = in_order(matmul_to_pairs(grad_proj, w_out, NT, 1, per, head_dim, LONG))
    grad_mixed = spread_pairs(grad_mixed)
    d_up = weight_grad(inputs, up_grads)
    mixed, grad_ffn_in, *grad_proj = after((mixed, grad_ffn_in, *grad_proj), in_order.last)
    d_out = in_order(out_grads(table, mixed, grad_proj, at_turn, own_rows))
    d_ffn_gain = jnp.sum(grad_ffn_in * hidden * factor_two, axis=0, keepdims=True)
    d_router = dot(grad_logits, ffn_in.astype(F32), ((0,), (0,)), precision=lax.Precision.HIGHEST)
    early = in_order(jnp.concatenate([d_router, d_ffn_gain]))
    ring.land()
    grad_mixed = in_order(grad_mixed)
    d_up = share(d_up)
    early = Ring(sum_fsdp(early, in_order))
    ring.step()
    grads, head_gains = in_order(*attend_back(qkv, grad_mixed, q_gain, k_gain, cosine, sine))
    if repeats > 1:
        head_gains = jnp.where(lax.axis_index("ctx") % repeats == 0, head_gains, 0.0)
    early.step()
    ring.step()
    grads = collect_pairs(grads)
    d_down = weight_grad([cots[i * size * rows : (i + 1) * size * rows] for i in range(len(groups))], acts)
    ring.land()
    early = early.finish()
    output = in_order((hidden + ring.finish()).astype(BF))
    ring = Ring(ring_scatter(lambda offset: d_out[offset * own_rows : (offset + 1) * own_rows], in_order))
    grads = in_order(grads)
    d_down = share(d_down)
    ring.step()

    chunk = parts * own_rows
    all_grads = {0: in_order(pair_weights(grads, normed_t, 3, parts, 0))}

    def total_term(offset):
        half, index = divmod(order_of_rows.index(offset), ctx_size // 2)
        return all_grads[half][index * chunk : (index + 1) * chunk]

    total_ring = Ring(
        ring_scatter(
            total_term, in_order, lambda term, right, left: total_parts(table, term, right, left, at_slab)
        )
    )
    grads = after(grads, in_order.last)
    all_grads[1] = in_order(pair_weights(grads, normed_t, 3, parts, 1))
    ring.step()
    total_ring.step()
    grads = after(grads, in_order.last)
    own, near, across, far = in_order(*pair_normed(grads, own_columns, 3, parts))
    far, near = swap(far, 1), swap(near, 1)
    far = swap(in_order((across + in_order(far).astype(F32)).astype(BF)), 2)
    d_out = ring.finish()
    total_ring.step()
    grad_normed = own + near.astype(F32) + in_order(far).astype(F32)
    d_attn_gain = jnp.sum(grad_normed * source * factor_one, axis=0)
    inner = grad_normed * attn_gain
    d_tokens = (
        grad_hidden
        + factor_one * inner
        - source * (factor_one * factor_one * factor_one) * jnp.mean(inner * source, axis=-1, keepdims=True)
    )
    d_tokens, d_attn_gain = in_order(d_tokens, d_attn_gain)
    late = jnp.concatenate([d_attn_gain, head_gains[0], head_gains[1], jnp.zeros((width - 2 * head_dim,), F32)])
    late = Ring(sum_fsdp(late.reshape(2, width), in_order))
    total_ring.step()
    late.step()
    total = in_order(*total_ring.finish())
    total = [total[0]] + [swap(total[mask], mask) for mask in range(1, parts)]
    packed = pack_gains(table, early, late.finish(), at_slab[0], experts)
    d_out, packed, *total = in_order(d_out, packed, *total)

    pieces, seen, whole = {}, set(), None
    ring = Ring(ring_gather(join_columns(table, total, d_out, packed, at_slab, 3), in_order, pieces))
    d_down, d_gate, d_up = after((d_down, d_gate, d_up), in_order.last)
    expert_grads = [d_down, d_gate, d_up]
    while True:
        new = [offset for offset in pieces if offset not in seen]
        seen.update(new)
        whole = in_order(
            *spread_rows(
                table, [pieces[offset] for offset in new], [at_blocks[offset] for offset in new], (slab, width),
                ctx_size, 4, whole,
            )
        )
        if len(seen) == ctx_size:
            break
        if len(seen) < 6:
            index = len(seen) // 2
            expert_grads[index] = in_order(split_experts(expert_grads[index], own_experts))
        ring.step()
    d_query, d_key, d_value, d_out = whole
    d_down, d_gate, d_up = expert_grads
    d_router, gains = unpack_gains(table, [pieces[o] for o in offsets], at_back, experts, packed.shape[0])
    d_ffn_gain, d_attn_gain, head_gains = gains + in_order.last
    return (
        output[None],
        d_tokens[None],
        d_attn_gain,
        d_query,
        d_key,
        d_value,
        head_gains[:head_dim],
        head_gains[head_dim : 2 * head_dim],
        d_out,
        d_ffn_gain,
        d_router,
        d_gate,
        d_up,
        d_down,
    )


def solution(mesh):
    token_split = P("fsdp", "ctx", None)
    row_split = P("fsdp", None)
    return jax.shard_map(
        body,
        mesh=mesh,
        in_specs=(
            token_split, P(), row_split, row_split, row_split, P(), P(), row_split,
            P(), row_split, token_split, token_split, token_split, token_split, token_split,
        ),
        out_specs=(
            token_split, token_split, P(), row_split, row_split, row_split, P(), P(),
            row_split, P(), row_split, token_split, token_split, token_split,
        ),
        check_vma=False,
    )
```

```python
import functools

import jax
import jax.numpy as jnp
import numpy as np
from jax import lax
from jax.experimental import pallas as pl
from jax.experimental.pallas import tpu as pltpu
from jax.sharding import PartitionSpec as P

EPSILON = 1e-06
ROPE_BASE = 10000.0
BF = jnp.bfloat16
F32 = jnp.float32
LONG = pl.CostEstimate(flops=10**12, bytes_accessed=10**9, transcendentals=0)
MEDIUM = pl.CostEstimate(flops=2 * 10**10, bytes_accessed=5 * 10**7, transcendentals=0)
SMALL = pl.CostEstimate(flops=1, bytes_accessed=1, transcendentals=0)


def dot(a, b, contract=((1,), (0,)), precision=None):
    return lax.dot_general(a, b, (contract, ((), ())), precision=precision, preferred_element_type=F32)


def dot_nt(a, b):
    return dot(a, b, ((1,), (1,)))


def dot_tn(a, b):
    return dot(a, b, ((0,), (0,)))


def head_norm(v, gain):
    factor = lax.rsqrt(jnp.mean(v * v, axis=-1, keepdims=True) + EPSILON)
    return v * factor * gain, factor


def turn(v, cosine, sine):
    return v * cosine + pltpu.roll(v, v.shape[-1] // 2, 1) * sine


def head_back(grad, v, gain, cosine, sine):
    grad = turn(grad, cosine, -sine)
    factor = lax.rsqrt(jnp.mean(v * v, axis=-1, keepdims=True) + EPSILON)
    gain_grad = jnp.sum(grad * v * factor, axis=0, keepdims=True)
    inner = grad * gain
    return factor * inner - v * (factor * factor * factor) * jnp.mean(inner * v, axis=-1, keepdims=True), gain_grad


def rows_of(ref):
    block = ref[...]
    return block.reshape(-1, block.shape[-1])


def attend_kernel(q_ref, k_ref, v_ref, qg_ref, kg_ref, cos_ref, sin_ref, o_ref, keys, values_t):
    step = pl.program_id(1)

    @pl.when(step == 0)
    def _():
        normed, _unused = head_norm(rows_of(k_ref).astype(F32), kg_ref[...])
        keys[...] = turn(normed, cos_ref[...], sin_ref[...]).astype(BF)
        values_t[...] = rows_of(v_ref).astype(F32).T.astype(BF)

    queries = rows_of(q_ref).astype(F32)
    number, head_dim = queries.shape
    here = pl.ds(pl.multiple_of(step * number, number), number)
    normed, _unused = head_norm(queries, qg_ref[...])
    queries = turn(normed, cos_ref[here, :], sin_ref[here, :]).astype(BF)
    weights = jnp.exp(dot_nt(keys[...], queries) * (head_dim**-0.5))
    total = jnp.sum(weights, axis=0, keepdims=True)
    mixed = dot(values_t[...], weights.astype(BF)) / total
    o_ref[...] = mixed.T.astype(BF).reshape(o_ref.shape)


def attend_back_kernel(
    q_ref, k_ref, v_ref, m_ref, qg_ref, kg_ref, cos_ref, sin_ref,
    g_ref, gain_ref, keys, keys_t, key_acc, value_acc,
):
    pair = pl.program_id(0)
    step = pl.program_id(1)
    last = pl.num_programs(1) - 1

    @pl.when((pair == 0) & (step == 0))
    def _():
        gain_ref[...] = jnp.zeros_like(gain_ref)

    @pl.when(step == 0)
    def _():
        normed, _unused = head_norm(rows_of(k_ref).astype(F32), kg_ref[...])
        turned = turn(normed, cos_ref[...], sin_ref[...])
        keys[...] = turned.astype(BF)
        keys_t[...] = turned.T.astype(BF)
        key_acc[...] = jnp.zeros_like(key_acc)
        value_acc[...] = jnp.zeros_like(value_acc)

    query_pre = rows_of(q_ref).astype(F32)
    grad_mixed = rows_of(m_ref)
    number, head_dim = query_pre.shape
    scale = head_dim**-0.5
    here = pl.ds(pl.multiple_of(step * number, number), number)
    cosine, sine = cos_ref[here, :], sin_ref[here, :]
    normed, _unused = head_norm(query_pre, qg_ref[...])
    queries = turn(normed, cosine, sine).astype(BF)
    weights = jnp.exp(dot_nt(keys[...], queries) * scale)
    probs = weights * (1.0 / jnp.sum(weights, axis=0, keepdims=True))
    value_acc[...] += dot(probs.astype(BF), grad_mixed)
    weighted = probs * dot_nt(rows_of(v_ref), grad_mixed)
    delta = jnp.sum(weighted, axis=0, keepdims=True)
    grad_scores = (weighted - probs * delta).astype(BF)
    key_acc[...] += dot(grad_scores, queries)
    grad_query = dot(keys_t[...], grad_scores).T * scale
    grad_query, gain_grad = head_back(grad_query, query_pre, qg_ref[...], cosine, sine)
    rows = g_ref.shape[2]
    blocks = number // rows
    g_ref[pl.ds(step * blocks, blocks), 0] = grad_query.astype(BF).reshape(blocks, rows, head_dim)
    gain_ref[0:1, :] += gain_grad

    @pl.when(step == last)
    def _():
        grad_key, gain_grad = head_back(
            key_acc[...] * scale, rows_of(k_ref).astype(F32), kg_ref[...], cos_ref[...], sin_ref[...]
        )
        g_ref[:, 1] = grad_key.astype(BF).reshape(-1, rows, head_dim)
        g_ref[:, 2] = value_acc[...].astype(BF).reshape(-1, rows, head_dim)
        gain_ref[1:2, :] += gain_grad


def attention_specs(shape):
    blocks, pairs, rows, head_dim = shape
    at_once = max(1, 256 // rows)
    while blocks % at_once:
        at_once -= 1
    pairs //= 3
    part = pl.BlockSpec((at_once, 1, rows, head_dim), lambda p, i: (i, p, 0, 0))
    three = [
        pl.BlockSpec((at_once, 1, rows, head_dim), lambda p, i: (i, 3 * p, 0, 0)),
        pl.BlockSpec((blocks, 1, rows, head_dim), lambda p, i: (0, 3 * p + 1, 0, 0)),
        pl.BlockSpec((blocks, 1, rows, head_dim), lambda p, i: (0, 3 * p + 2, 0, 0)),
    ]
    gain = pl.BlockSpec((1, head_dim), lambda p, i: (0, 0))
    table = pl.BlockSpec((blocks * rows, head_dim), lambda p, i: (0, 0))
    params = pltpu.CompilerParams(
        dimension_semantics=("arbitrary", "arbitrary"),
        vmem_limit_bytes=(24 if blocks * rows <= 1024 else 56) * 2**20,
    )
    return part, three, gain, table, (pairs, blocks // at_once), params


def attend(qkv, query_gain, key_gain, cosine, sine):
    part, three, gain, table, grid, params = attention_specs(qkv.shape)
    blocks, _unused, rows, head_dim = qkv.shape
    length = blocks * rows
    return pl.pallas_call(
        attend_kernel,
        grid=grid,
        in_specs=[*three, gain, gain, table, table],
        out_specs=part,
        out_shape=jax.ShapeDtypeStruct((blocks, grid[0], rows, head_dim), BF),
        scratch_shapes=[pltpu.VMEM((length, head_dim), BF), pltpu.VMEM((head_dim, length), BF)],
        compiler_params=params,
        cost_estimate=MEDIUM,
        name="attend",
    )(qkv, qkv, qkv, query_gain, key_gain, cosine, sine)


def attend_back(qkv, grad_mixed, query_gain, key_gain, cosine, sine):
    part, three, gain, table, grid, params = attention_specs(qkv.shape)
    blocks, _unused, rows, head_dim = qkv.shape
    length = blocks * rows
    return pl.pallas_call(
        attend_back_kernel,
        grid=grid,
        in_specs=[*three, part, gain, gain, table, table],
        out_specs=[
            pl.BlockSpec((blocks, 3, rows, head_dim), lambda p, i: (0, p, 0, 0)),
            pl.BlockSpec((8, head_dim), lambda p, i: (0, 0)),
        ],
        out_shape=[jax.ShapeDtypeStruct(qkv.shape, BF), jax.ShapeDtypeStruct((8, head_dim), F32)],
        scratch_shapes=[
            pltpu.VMEM((length, head_dim), BF),
            pltpu.VMEM((head_dim, length), BF),
            pltpu.VMEM((length, head_dim), F32),
            pltpu.VMEM((length, head_dim), F32),
        ],
        compiler_params=params,
        cost_estimate=LONG,
        name="attend_back",
    )(qkv, qkv, qkv, grad_mixed, query_gain, key_gain, cosine, sine)


def stack_blocks(block_refs, out_ref):
    rows = block_refs[0].shape[0]
    for index, block_ref in enumerate(block_refs):
        out_ref[index * rows : (index + 1) * rows, :] = block_ref[...]


def stacked_kernel(w_ref, *refs):
    *block_refs, o_ref, rows_ref = refs

    @pl.when(pl.program_id(0) == 0)
    def _():
        stack_blocks(block_refs, rows_ref)

    o_ref[...] = dot(rows_ref[...], w_ref[...])


def stacked_matmul(blocks, weight):
    rows, depth = len(blocks) * blocks[0].shape[0], weight.shape[0]
    wide = min(512, weight.shape[1])
    return pl.pallas_call(
        stacked_kernel,
        grid=(weight.shape[1] // wide,),
        in_specs=[pl.BlockSpec((depth, wide), lambda n: (0, n))]
        + [pl.BlockSpec(block.shape, lambda n: (0, 0)) for block in blocks],
        out_specs=[pl.BlockSpec((rows, wide), lambda n: (0, n)), pl.BlockSpec((rows, depth), lambda n: (0, 0))],
        out_shape=[jax.ShapeDtypeStruct((rows, weight.shape[1]), F32), jax.ShapeDtypeStruct((rows, depth), BF)],
        compiler_params=pltpu.CompilerParams(dimension_semantics=("arbitrary",), vmem_limit_bytes=56 * 2**20),
        cost_estimate=LONG,
        name="stacked_matmul",
    )(weight, *blocks)


def routed_gates(logits, routes):
    columns = lax.broadcasted_iota(jnp.int32, logits.shape, 1)
    chosen = columns == routes[:, 0:1]
    for index in range(1, routes.shape[1]):
        chosen = chosen | (columns == routes[:, index : index + 1])
    high = jnp.max(jnp.where(chosen, logits, -1e30), axis=-1, keepdims=True)
    weights = jnp.where(chosen, jnp.exp(jnp.where(chosen, logits - high, 0.0)), 0.0)
    return weights / jnp.sum(weights, axis=-1, keepdims=True)


def expert_kernel(table_ref, router_ref, routes_ref, gate_w_ref, up_w_ref, grad_ref, *refs, per, place, at):
    *block_refs, act_ref, gate_ref, up_ref, d_gates_ref, x_ref, gates_ref = refs
    step = pl.program_id(0)

    @pl.when(step == 0)
    def _():
        stack_blocks(block_refs, x_ref)
        routes = jnp.concatenate([routes_ref[table_ref[at + index]] for index in range(len(block_refs))], axis=0)
        gates = routed_gates(dot(x_ref[...], router_ref[...]), routes)
        columns = lax.broadcasted_iota(jnp.int32, gates.shape, 1)
        count = gates_ref.shape[0]
        for index in range(count):
            here = columns == table_ref[place] * count + index
            gates_ref[index] = jnp.sum(jnp.where(here, gates, 0.0), axis=1, keepdims=True)

    @pl.when(step % per == 0)
    def _():
        d_gates_ref[...] = jnp.zeros_like(d_gates_ref)

    gate_pre = dot(x_ref[...], gate_w_ref[...])
    up_pre = dot(x_ref[...], up_w_ref[...])
    grad_act = grad_ref[...]
    gates = gates_ref[step // per]
    sigmoid = 1.0 / (1.0 + jnp.exp(-gate_pre))
    silu = gate_pre * sigmoid
    act = (silu * up_pre).astype(BF).astype(F32)
    d_gates_ref[0] += jnp.sum(act * grad_act, axis=1, keepdims=True)
    grad_act = grad_act * gates
    act_ref[...] = (act * gates).astype(BF)
    up_ref[...] = (grad_act * silu).astype(BF)
    gate_ref[...] = (grad_act * up_pre * (sigmoid * (1.0 + gate_pre * (1.0 - sigmoid)))).astype(BF)


def expert_units(table, place, at, blocks, routes, router_w, gate_w, up_w, grad_act, count):
    rows, width = len(blocks) * blocks[0].shape[0], blocks[0].shape[1]
    units = gate_w.shape[1]
    wide = min(512, units // count)
    per = units // wide // count
    weight = pl.BlockSpec((width, wide), lambda n: (0, n))
    tile = pl.BlockSpec((rows, wide), lambda n: (0, n))
    out = jax.ShapeDtypeStruct((rows, units), BF)
    return pl.pallas_call(
        functools.partial(expert_kernel, per=per, place=place, at=at),
        grid=(units // wide,),
        in_specs=[
            pl.BlockSpec(memory_space=pltpu.SMEM),
            pl.BlockSpec(router_w.shape, lambda n: (0, 0)),
            pl.BlockSpec(routes.shape, lambda n: (0, 0, 0)),
            weight,
            weight,
            tile,
        ]
        + [pl.BlockSpec(block.shape, lambda n: (0, 0)) for block in blocks],
        out_specs=[
            tile,
            tile,
            tile,
            pl.BlockSpec((1, rows, 1), lambda n: (n // per, 0, 0)),
            pl.BlockSpec((rows, width), lambda n: (0, 0)),
        ],
        out_shape=[
            out, out, out, jax.ShapeDtypeStruct((count, rows, 1), F32), jax.ShapeDtypeStruct((rows, width), BF),
        ],
        scratch_shapes=[pltpu.VMEM((count, rows, 1), F32)],
        compiler_params=pltpu.CompilerParams(dimension_semantics=("arbitrary",), vmem_limit_bytes=58 * 2**20),
        cost_estimate=LONG,
        name="expert_units",
    )(table, router_w, routes, gate_w, up_w, grad_act, *blocks)


def expert_rows_kernel(gate_ref, up_ref, gate_w_ref, up_w_ref, o_ref):
    o_ref[...] = (dot_nt(gate_ref[...], gate_w_ref[...]) + dot_nt(up_ref[...], up_w_ref[...])).astype(BF)


def expert_rows(gate_grads, up_grads, gate_w, up_w):
    rows, units = gate_grads.shape
    width = gate_w.shape[0]
    wide = min(512, width)
    whole = pl.BlockSpec((rows, units), lambda n: (0, 0))
    weight = pl.BlockSpec((wide, units), lambda n: (n, 0))
    return pl.pallas_call(
        expert_rows_kernel,
        grid=(width // wide,),
        in_specs=[whole, whole, weight, weight],
        out_specs=pl.BlockSpec((rows, wide), lambda n: (0, n)),
        out_shape=jax.ShapeDtypeStruct((rows, width), BF),
        compiler_params=pltpu.CompilerParams(dimension_semantics=("arbitrary",), vmem_limit_bytes=56 * 2**20),
        cost_estimate=LONG,
        name="expert_rows",
    )(gate_grads, up_grads, gate_w, up_w)


def times_kernel(b_ref, *refs):
    count = len(refs) // 2
    for a_ref, o_ref in zip(refs[:count], refs[count:]):
        o_ref[...] = dot_nt(a_ref[...], b_ref[...]).astype(o_ref.dtype)


def times_transpose(lefts, b):
    columns, depth = b.shape
    wide = min(512, columns)
    return pl.pallas_call(
        times_kernel,
        grid=(columns // wide,),
        in_specs=[pl.BlockSpec((wide, depth), lambda n: (n, 0))]
        + [pl.BlockSpec(left.shape, lambda n: (0, 0)) for left in lefts],
        out_specs=[pl.BlockSpec((left.shape[0], wide), lambda n: (0, n)) for left in lefts],
        out_shape=[jax.ShapeDtypeStruct((left.shape[0], columns), BF) for left in lefts],
        compiler_params=pltpu.CompilerParams(dimension_semantics=("arbitrary",), vmem_limit_bytes=58 * 2**20),
        cost_estimate=LONG,
        name="times_transpose",
    )(b, *lefts)


def sum_kernel(*refs):
    *pair_refs, o_ref = refs
    count = len(pair_refs) // 2
    total = dot_tn(pair_refs[0][...], pair_refs[count][...])
    for index in range(1, count):
        total = total + dot_tn(pair_refs[index][...], pair_refs[count + index][...])
    o_ref[...] = total.astype(o_ref.dtype)


def sum_of_outer(lefts, rights):
    whole = not isinstance(lefts, (list, tuple))
    count, depth = len(rights), rights[0].shape[0]
    rows, columns = (lefts if whole else lefts[0]).shape[1], rights[0].shape[1]
    tall, wide = min(512, rows), columns if count <= 2 else min(1024, columns)

    def left_spec(index):
        at = index if whole else 0
        return pl.BlockSpec((depth, tall), lambda n, m: (at, m))

    return pl.pallas_call(
        sum_kernel,
        grid=(columns // wide, rows // tall),
        in_specs=[left_spec(index) for index in range(count)]
        + [pl.BlockSpec((depth, wide), lambda n, m: (0, n)) for _unused in rights],
        out_specs=pl.BlockSpec((tall, wide), lambda n, m: (m, n)),
        out_shape=jax.ShapeDtypeStruct((rows, columns), BF),
        compiler_params=pltpu.CompilerParams(
            dimension_semantics=("arbitrary", "arbitrary"), vmem_limit_bytes=56 * 2**20
        ),
        cost_estimate=LONG,
        name="sum_of_outer",
    )(*([lefts] * count if whole else lefts), *rights)


NN, NT = ((1,), (0,)), ((1,), (1,))


def small_call(kernel, name, out_shape, *operands, cost=SMALL, scratch=(), **kwargs):
    vmem = pl.BlockSpec(memory_space=pltpu.VMEM)
    return pl.pallas_call(
        functools.partial(kernel, **kwargs),
        in_specs=[pl.BlockSpec(memory_space=pltpu.SMEM)] + [vmem] * (len(operands) - 1),
        out_specs=jax.tree.map(lambda _unused: vmem, out_shape),
        out_shape=out_shape,
        scratch_shapes=list(scratch),
        compiler_params=pltpu.CompilerParams(vmem_limit_bytes=48 * 2**20),
        cost_estimate=cost,
        name=name,
    )(*operands)


def payload_kernel(_unused, a_ref, b_ref, o_ref):
    rows, width = b_ref.shape[0], o_ref.shape[1]
    columns = b_ref.shape[1]
    rest = columns - width
    o_ref[:rows, :] = a_ref[:, :width]
    o_ref[rows : 2 * rows, :] = b_ref[:, :width]
    o_ref[2 * rows : 3 * rows, :rest] = a_ref[:, width:columns]
    o_ref[2 * rows : 3 * rows, rest:] = b_ref[:, width:]
    o_ref[3 * rows :, :] = a_ref[:, columns:]


def fetched_payload(table, from_beyond, from_across, width):
    out = jax.ShapeDtypeStruct((4 * from_across.shape[0], width), BF)
    return small_call(payload_kernel, "fetched_payload", out, table, from_beyond, from_across)


def own_pairs_kernel(table_ref, *refs, blocks, kinds, slabs, ring_slots):
    block_refs, refs = refs[:blocks], refs[blocks:]
    own_ref, near_ref, *piece_refs = refs[:-5]
    o_ref, columns_out, columns_ref, rows_ref, sems = refs[-5:]
    head_step, kind = pl.program_id(0), pl.program_id(1)
    slab, columns = own_ref.shape
    width = piece_refs[0].shape[1]
    part = piece_refs[0].shape[0] // 4
    rest = columns - width
    back = pltpu.make_async_copy(columns_ref, columns_out, sems.at[2 + 4 * len(piece_refs)])

    @pl.when((head_step == 0) & (kind == 0))
    def _():
        def at(slot, ring_slot=None):
            start = table_ref[slot] * slab
            if ring_slot is None:
                return pl.ds(pl.multiple_of(start, slab), slab)
            return pl.ds(pl.multiple_of(start + table_ref[ring_slot] * part, part), part)

        pairs = [(own_ref, columns_ref.at[at(slabs[0]), :]), (near_ref, columns_ref.at[at(slabs[1]), :])]
        for ring_slot, piece in zip(ring_slots, piece_refs):
            for index in range(2):
                to = at(slabs[2 + index], ring_slot)
                pairs.append((piece.at[index * part : (index + 1) * part, :], columns_ref.at[to, :width]))
                some = piece.at[2 * part : 3 * part, index * rest : (index + 1) * rest]
                pairs.append((some, columns_ref.at[to, width:]))
        copies = [pltpu.make_async_copy(*pair, sems.at[index]) for index, pair in enumerate(pairs)]
        for copy in copies:
            copy.start()
        stack_blocks(block_refs, rows_ref)
        for copy in copies:
            copy.wait()
        back.start()

    rows, head_dim = o_ref.shape[2:]
    wide = o_ref.shape[0] * head_dim
    at_column = (kind * pl.num_programs(0) + head_step) * wide
    product = dot(rows_ref[...], columns_ref[:, pl.ds(pl.multiple_of(at_column, wide), wide)]).astype(BF)
    for head in range(o_ref.shape[0]):
        for block in range(blocks):
            piece = product[block * rows : (block + 1) * rows, head * head_dim : (head + 1) * head_dim]
            o_ref[head, block * kinds + kind] = piece

    @pl.when((head_step == pl.num_programs(0) - 1) & (kind == kinds - 1))
    def _():
        back.wait()


def own_pairs(table, blocks, own, near, pieces, kinds, head_dim, slabs, ring_slots):
    rows, depth = blocks[0].shape
    columns = own.shape[1]
    heads = columns // head_dim // kinds
    at_once = 2
    anywhere = pl.BlockSpec(memory_space=pl.ANY)
    return pl.pallas_call(
        functools.partial(
            own_pairs_kernel, blocks=len(blocks), kinds=kinds, slabs=slabs, ring_slots=ring_slots
        ),
        grid=(heads // at_once, kinds),
        in_specs=[pl.BlockSpec(memory_space=pltpu.SMEM)]
        + [pl.BlockSpec(block.shape, lambda h, k: (0, 0)) for block in blocks]
        + [anywhere] * (2 + len(pieces)),
        out_specs=[
            pl.BlockSpec((at_once, len(blocks) * kinds, rows, head_dim), lambda h, k: (h, 0, 0, 0)),
            anywhere,
        ],
        out_shape=[
            jax.ShapeDtypeStruct((heads, len(blocks) * kinds, rows, head_dim), BF),
            jax.ShapeDtypeStruct((depth, columns), BF),
        ],
        scratch_shapes=[
            pltpu.VMEM((depth, columns), BF),
            pltpu.VMEM((len(blocks) * rows, depth), BF),
            pltpu.SemaphoreType.DMA((3 + 4 * len(pieces),)),
        ],
        compiler_params=pltpu.CompilerParams(
            dimension_semantics=("arbitrary", "arbitrary"), vmem_limit_bytes=40 * 2**20
        ),
        cost_estimate=SMALL,
        name="own_pairs",
    )(table, *blocks, own, near, *pieces)


def far_rows_kernel(table_ref, *refs, ring_slots):
    *pieces, o_ref = refs
    part = pieces[0].shape[0] // 4
    for slot, piece in zip(ring_slots, pieces):
        o_ref[pl.ds(pl.multiple_of(table_ref[slot] * part, part), part), :] = piece[3 * part :, :]


def far_rows(table, pieces, ring_slots):
    rows, width = pieces[0].shape
    out = jax.ShapeDtypeStruct((rows // 4 * len(pieces), width), BF)
    return small_call(far_rows_kernel, "far_rows", out, table, *pieces, ring_slots=ring_slots)


def heads_of(ref, side, sequence, count):
    return [ref[side * count + head, sequence] for head in range(count)]


def mixed_out_kernel(table_ref, m_ref, w_ref, far_ref, *refs, side):
    count = m_ref.shape[0] // 2
    for sequence, ref in enumerate(refs):
        own = jnp.concatenate(heads_of(m_ref, table_ref[side], sequence, count), axis=1)
        far = jnp.concatenate(heads_of(m_ref, 1 - table_ref[side], sequence, count), axis=1)
        ref[...] = (dot(own, w_ref[...]) + dot(far, far_ref[...])).astype(ref.dtype)


def mixed_out(table, mixed, w_out, w_far, side):
    shape = (mixed.shape[2], w_out.shape[1])
    out = [jax.ShapeDtypeStruct(shape, kind) for kind in (F32, BF)]
    return small_call(mixed_out_kernel, "mixed_out", out, table, mixed, w_out, w_far, cost=MEDIUM, side=side)


def grad_pairs_kernel(table_ref, own_ref, beside_ref, w_ref, far_ref, o_ref, *, side):
    rows, head_dim = o_ref.shape[2:]
    count = o_ref.shape[0] // 2
    grads = jnp.concatenate([own_ref[...], beside_ref[...]], axis=0)
    for slab_ref, at in ((w_ref, table_ref[side]), (far_ref, 1 - table_ref[side])):
        product = dot_nt(grads, slab_ref[...]).astype(BF)
        for head in range(count):
            for sequence in range(2):
                piece = product[sequence * rows : (sequence + 1) * rows, head * head_dim : (head + 1) * head_dim]
                o_ref[at * count + head, sequence] = piece


def grad_pairs(table, own, beside, w_out, w_far, side, head_dim):
    out = jax.ShapeDtypeStruct((2 * w_out.shape[0] // head_dim, 2, own.shape[0], head_dim), BF)
    return small_call(
        grad_pairs_kernel, "grad_pairs", out, table, own, beside, w_out, w_far, cost=LONG, side=side
    )


def out_grads_kernel(table_ref, m_ref, other_ref, *refs, turn, own_rows, side):
    *block_refs, o_ref, mixed_ref, turned_ref, grads_ref = refs
    head_dim = m_ref.shape[3]
    count = m_ref.shape[0] // 2
    for head in range(count):
        rows = [m_ref[table_ref[side] * count + head, sequence] for sequence in range(2)]
        rows += [other_ref[head, sequence] for sequence in range(2)]
        rows = jnp.concatenate(rows, axis=0)
        mixed_ref[head * head_dim : (head + 1) * head_dim, :] = rows.astype(F32).T.astype(BF)
    for index in range(mixed_ref.shape[0] // own_rows):
        at = pl.multiple_of(table_ref[turn + index] * own_rows, own_rows)
        turned_ref[index * own_rows : (index + 1) * own_rows, :] = mixed_ref[pl.ds(at, own_rows), :]
    stack_blocks(block_refs, grads_ref)
    o_ref[...] = dot(turned_ref[...], grads_ref[...])


def out_grads(table, mixed, other, blocks, turn, own_rows, side):
    rows, width = blocks[0].shape
    features = mixed.shape[0] // 2 * mixed.shape[3]
    turned = pltpu.VMEM((features, len(blocks) * rows), BF)
    out = jax.ShapeDtypeStruct((features, width), F32)
    scratch = [turned, turned, pltpu.VMEM((len(blocks) * rows, width), BF)]
    return small_call(
        out_grads_kernel, "out_grads", out, table, mixed, other, *blocks, scratch=scratch, turn=turn,
        own_rows=own_rows, side=side,
    )


def transposed_kernel(table_ref, *refs, slots):
    *block_refs, o_ref = refs
    rows, width = block_refs[0].shape
    slab = width // len(slots)
    for index, block_ref in enumerate(block_refs):
        for number, slot in enumerate(slots):
            here = pl.ds(pl.multiple_of(table_ref[slot] * slab, slab), slab)
            some = block_ref[:, here].astype(F32).T.astype(BF)
            o_ref[number * slab : (number + 1) * slab, index * rows : (index + 1) * rows] = some


def transposed(table, blocks, slots):
    rows, width = blocks[0].shape
    out = jax.ShapeDtypeStruct((width, len(blocks) * rows), BF)
    return small_call(transposed_kernel, "transposed", out, table, *blocks, cost=LONG, slots=slots)


def head_weights_kernel(table_ref, g_ref, own_ref, beside_ref, o_ref, grads_ref, *, kinds, places):
    rows, head_dim = g_ref.shape[2:]

    @pl.when(pl.program_id(0) == 0)
    def _():
        for index in range(g_ref.shape[0]):
            for sequence in range(2):
                for kind in range(kinds):
                    piece = g_ref[table_ref[places + index], sequence * kinds + kind]
                    here = slice(kind * head_dim, (kind + 1) * head_dim)
                    grads_ref[sequence, index * rows : (index + 1) * rows, here] = piece

    o_ref[...] = (dot(own_ref[...], grads_ref[0]) + dot(beside_ref[...], grads_ref[1])).astype(BF)


def head_weights(table, grads, own, beside, kinds, places):
    blocks, _unused, rows, head_dim = grads.shape
    width, total = own.shape
    tall = width // 4
    row = pl.BlockSpec((tall, total), lambda m: (m, 0))
    return pl.pallas_call(
        functools.partial(head_weights_kernel, kinds=kinds, places=places),
        grid=(4,),
        in_specs=[pl.BlockSpec(memory_space=pltpu.SMEM), pl.BlockSpec(grads.shape, lambda m: (0, 0, 0, 0)), row, row],
        out_specs=pl.BlockSpec((tall, kinds * head_dim), lambda m: (m, 0)),
        out_shape=jax.ShapeDtypeStruct((width, kinds * head_dim), BF),
        scratch_shapes=[pltpu.VMEM((2, total, kinds * head_dim), BF)],
        compiler_params=pltpu.CompilerParams(dimension_semantics=("arbitrary",), vmem_limit_bytes=48 * 2**20),
        cost_estimate=LONG,
        name="head_weights",
    )(table, grads, own, beside)


def chip_total_kernel(table_ref, own_ref, other_ref, keep_ref, send_ref, *, core):
    slab = keep_ref.shape[0]
    for ref, at in ((keep_ref, table_ref[core]), (send_ref, 1 - table_ref[core])):
        here = pl.ds(pl.multiple_of(at * slab, slab), slab)
        ref[...] = (own_ref[here, :].astype(F32) + other_ref[here, :].astype(F32)).astype(BF)


def chip_total(table, own, other, core):
    out = [jax.ShapeDtypeStruct((other.shape[0] // 2, own.shape[1]), BF)] * 2
    return small_call(chip_total_kernel, "chip_total", out, table, own, other, core=core)


def beside_kernel(_unused, left_ref, right_ref, o_ref):
    columns = left_ref.shape[1]
    o_ref[:, :columns] = left_ref[...].astype(BF)
    o_ref[:, columns:] = right_ref[...].astype(BF)


def side_by_side(table, left, right):
    out = jax.ShapeDtypeStruct((left.shape[0], left.shape[1] + right.shape[1]), BF)
    return small_call(beside_kernel, "side_by_side", out, table, left, right)


def pair_rows_kernel(g_ref, w_ref, own_ref, beside_ref, dn_ref, *, kinds):
    kind = pl.program_id(1)

    @pl.when((pl.program_id(0) == 0) & (kind == 0))
    def _():
        dn_ref[...] = jnp.zeros_like(dn_ref)

    heads = []
    for head in range(g_ref.shape[0]):
        heads.append(jnp.concatenate([g_ref[head, sequence * kinds + kind] for sequence in range(2)], axis=0))
    dn_ref[...] += dot_nt(jnp.concatenate(heads, axis=1), w_ref[...])

    @pl.when((pl.program_id(0) == pl.num_programs(0) - 1) & (kind == kinds - 1))
    def _():
        rows = own_ref.shape[0]
        own_ref[...] = dn_ref[:rows, :]
        beside_ref[...] = dn_ref[rows:, :].astype(BF)


def pair_normed(grads, columns, kinds):
    heads, _unused, rows, head_dim = grads.shape
    width, at_once = columns.shape[0], 2
    whole = pl.BlockSpec((rows, width), lambda h, k: (0, 0))
    return pl.pallas_call(
        functools.partial(pair_rows_kernel, kinds=kinds),
        grid=(heads // at_once, kinds),
        in_specs=[
            pl.BlockSpec((at_once, 2 * kinds, rows, head_dim), lambda h, k: (h, 0, 0, 0)),
            pl.BlockSpec((width, at_once * head_dim), lambda h, k: (0, k * (heads // at_once) + h)),
        ],
        out_specs=[whole, whole],
        out_shape=[jax.ShapeDtypeStruct((rows, width), kind) for kind in (F32, BF)],
        scratch_shapes=[pltpu.VMEM((2 * rows, width), F32)],
        compiler_params=pltpu.CompilerParams(
            dimension_semantics=("arbitrary", "arbitrary"), vmem_limit_bytes=40 * 2**20
        ),
        cost_estimate=LONG,
        name="pair_normed",
    )(grads, columns)


def take_kernel(table_ref, *refs, count, sides):
    weights, outs, sems = refs[:count], refs[count : count + len(sides)], refs[-1]
    copies = []
    for out, (row, rows, pieces) in zip(outs, sides):
        at = 0
        if row is None:
            here = slice(None)
        else:
            here = pl.ds(pl.multiple_of(table_ref[row] * rows, rows), rows)
        for number, slot, wide in pieces:
            there = slice(None)
            if slot is not None:
                there = pl.ds(pl.multiple_of(table_ref[slot] * wide, wide), wide)
            copies.append(
                pltpu.make_async_copy(
                    weights[number].at[here, there], out.at[:, at : at + wide], sems.at[len(copies)]
                )
            )
            at += wide
    for copy in copies:
        copy.start()
    for copy in copies:
        copy.wait()


def take_parts(table, weights, sides, cost):
    outs = []
    for row, rows, pieces in sides:
        outs.append(jax.ShapeDtypeStruct((rows, sum(wide for _unused, _unused2, wide in pieces)), BF))
    number = sum(len(pieces) for _unused, _unused2, pieces in sides)
    return pl.pallas_call(
        functools.partial(take_kernel, count=len(weights), sides=sides),
        in_specs=[pl.BlockSpec(memory_space=pltpu.SMEM)] + [pl.BlockSpec(memory_space=pl.ANY)] * len(weights),
        out_specs=[pl.BlockSpec(memory_space=pltpu.VMEM)] * len(sides),
        out_shape=outs,
        scratch_shapes=[pltpu.SemaphoreType.DMA((number,))],
        compiler_params=pltpu.CompilerParams(vmem_limit_bytes=40 * 2**20),
        cost_estimate=cost,
        name="take_parts",
    )(table, *weights)


def place_kernel(table_ref, *refs, slots):
    *pieces, out = refs
    for piece, slot in zip(pieces, slots):
        rows = piece.shape[0]
        out[pl.ds(pl.multiple_of(table_ref[slot] * rows, rows), rows), :] = piece[...]


def place_rows(table, pieces, slots):
    rows = sum(piece.shape[0] for piece in pieces)
    out = jax.ShapeDtypeStruct((rows, pieces[0].shape[1]), pieces[0].dtype)
    return small_call(place_kernel, "place_rows", out, table, *pieces, slots=slots)


def pack_kernel(table_ref, below_ref, early_ref, late_ref, o_ref, *, slot, experts):
    slab = o_ref.shape[1] // 4
    first = below_ref.shape[0]
    here = pl.ds(pl.multiple_of(table_ref[slot] * slab, slab), slab)
    o_ref[...] = jnp.zeros_like(o_ref)
    o_ref[:first, :] = below_ref[...].astype(BF)
    for index in range(experts):
        at = first + index // 4
        o_ref[at : at + 1, index % 4 * slab : (index % 4 + 1) * slab] = early_ref[index : index + 1, here].astype(BF)
    at = first + experts // 4
    o_ref[at : at + 1, :] = early_ref[experts : experts + 1, :].astype(BF)
    o_ref[at + 1 : at + 3, :] = late_ref[...].astype(BF)


def pack_gains(table, below, early, late, slot, experts):
    height = below.shape[0] + -(-(experts // 4 + 3) // 16) * 16
    out = jax.ShapeDtypeStruct((height, early.shape[1]), BF)
    return small_call(pack_kernel, "pack_gains", out, table, below, early, late, slot=slot, experts=experts)


def unpack_kernel(table_ref, *refs, back, experts):
    *pieces, router_ref, gains_ref, all_ref = refs
    height = all_ref.shape[1]
    for index, piece in enumerate(pieces):
        all_ref[index] = piece[piece.shape[0] - height :, :].astype(F32)
    total = all_ref[table_ref[back]]
    for place in range(1, len(pieces)):
        total = total + all_ref[table_ref[back + place]]
    slab = total.shape[1] // 4
    rows = [total[i // 4 : i // 4 + 1, i % 4 * slab : (i % 4 + 1) * slab] for i in range(experts)]
    router_ref[...] = jnp.concatenate(rows, axis=0).T
    gains_ref[...] = total[experts // 4 : experts // 4 + 3, :]


def unpack_gains(table, pieces, back, experts, height):
    width = pieces[0].shape[1]
    out = [jax.ShapeDtypeStruct((width // 4, experts), F32), jax.ShapeDtypeStruct((3, width), F32)]
    scratch = [pltpu.VMEM((len(pieces), height, width), F32)]
    return small_call(
        unpack_kernel, "unpack_gains", out, table, *pieces, scratch=scratch, back=back, experts=experts
    )


def spread_kernel(table_ref, *refs, count, outs, cuts):
    pieces = refs[:count]
    out_refs = refs[-2 - outs : -2]
    wide_ref, sems = refs[-2:]
    copies = []
    for index, (number, rows, columns, out, slot, by_rows) in enumerate(cuts):
        wide_ref[index] = pieces[number][rows[0] : rows[1], columns[0] : columns[1]].astype(F32)
        size = rows[1] - rows[0] if by_rows else columns[1] - columns[0]
        here = pl.ds(pl.multiple_of(table_ref[slot] * size, size), size)
        to = out_refs[out].at[here, :] if by_rows else out_refs[out].at[:, here]
        copies.append(pltpu.make_async_copy(wide_ref.at[index], to, sems.at[index]))
        copies[-1].start()
    for copy in copies:
        copy.wait()


def spread(table, pieces, cuts, shape, outs, before):
    vmem, anywhere = pl.BlockSpec(memory_space=pltpu.VMEM), pl.BlockSpec(memory_space=pl.ANY)
    old = [] if before is None else list(before)
    _unused, rows, columns, *_rest = cuts[0]
    return pl.pallas_call(
        functools.partial(spread_kernel, count=len(pieces), outs=outs, cuts=cuts),
        in_specs=[pl.BlockSpec(memory_space=pltpu.SMEM)] + [vmem] * len(pieces) + [anywhere] * len(old),
        out_specs=[anywhere] * outs,
        out_shape=[jax.ShapeDtypeStruct(shape, F32)] * outs,
        input_output_aliases={1 + len(pieces) + index: index for index in range(len(old))},
        scratch_shapes=[
            pltpu.VMEM((len(cuts), rows[1] - rows[0], columns[1] - columns[0]), F32),
            pltpu.SemaphoreType.DMA((len(cuts),)),
        ],
        compiler_params=pltpu.CompilerParams(vmem_limit_bytes=24 * 2**20),
        cost_estimate=SMALL,
        name="spread",
    )(table, *pieces, *old)


def merge_kernel(w_ref, o_ref):
    units = w_ref.shape[2]
    for index in range(w_ref.shape[1]):
        o_ref[:, index * units : (index + 1) * units] = w_ref[:, index, :]


def merge_experts(weight):
    rows, count, units = weight.shape
    at_once = 128
    return pl.pallas_call(
        merge_kernel,
        grid=(rows // at_once,),
        in_specs=[pl.BlockSpec((at_once, count, units), lambda m: (m, 0, 0))],
        out_specs=pl.BlockSpec((at_once, count * units), lambda m: (m, 0)),
        out_shape=jax.ShapeDtypeStruct((rows, count * units), weight.dtype),
        cost_estimate=MEDIUM,
        name="merge_experts",
    )(weight)


def split_kernel(w_ref, o_ref):
    units = o_ref.shape[2]
    for index in range(o_ref.shape[1]):
        o_ref[:, index, :] = w_ref[:, index * units : (index + 1) * units].astype(F32)


def split_experts(grad, count):
    rows, columns = grad.shape
    at_once = 128
    return pl.pallas_call(
        split_kernel,
        grid=(rows // at_once,),
        in_specs=[pl.BlockSpec((at_once, columns), lambda m: (m, 0))],
        out_specs=pl.BlockSpec((at_once, count, columns // count), lambda m: (m, 0, 0)),
        out_shape=jax.ShapeDtypeStruct((rows, count, columns // count), F32),
        cost_estimate=SMALL,
        name="split_experts",
    )(grad)


def swap(v, mask):
    size = lax.axis_size("fsdp")
    return lax.ppermute(v, "fsdp", [(i, i ^ mask) for i in range(size)])


def ring_order(size):
    if size == 8:
        return [0, 2, 4, 6, 7, 5, 3, 1]
    return list(range(size))


def ring_send(v, direction):
    order = ring_order(lax.axis_size("ctx"))
    size = len(order)
    return lax.ppermute(v, "ctx", [(order[i], order[(i + direction) % size]) for i in range(size)])


class Ring:
    def __init__(self, steps):
        self.steps = steps
        self.value = None
        self.flying = False
        self.advance()

    def advance(self):
        try:
            next(self.steps)
            self.flying = not self.flying
        except StopIteration as end:
            self.value = end.value

    def land(self):
        if self.value is None and self.flying:
            self.advance()

    def step(self):
        self.land()
        if self.value is None:
            self.advance()

    def finish(self):
        while self.value is None:
            self.step()
        return self.value


def ring_gather(v, in_order, found):
    size = lax.axis_size("ctx")
    far, half = size // 2, v.shape[0] // 2
    found[0] = v
    right, left = v, v
    for step in range(1, far):
        right, left = ring_send(right, 1), ring_send(left, -1)
        yield
        right, left = in_order(right, left)
        found[size - step], found[step] = right, left
        yield
    right, left = ring_send(right[:half], 1), ring_send(left[half:], -1)
    yield
    found[far] = jnp.concatenate(in_order(right, left))
    yield
    return found


def ring_scatter(term, in_order):
    size = lax.axis_size("ctx")
    far = size // 2
    first = term(far)
    half = first.shape[0] // 2
    right, left = ring_send(first[:half].astype(BF), 1), ring_send(first[half:].astype(BF), -1)
    for offset in range(far - 1, 0, -1):
        yield
        right, left = in_order(right, left)
        yield
        ahead, behind = term(offset), term(size - offset)
        if offset == far - 1:
            ahead = jnp.concatenate([ahead[:half].astype(F32) + right.astype(F32), ahead[half:].astype(F32)])
            behind = jnp.concatenate([behind[:half].astype(F32), behind[half:].astype(F32) + left.astype(F32)])
        else:
            ahead, behind = ahead.astype(F32) + right.astype(F32), behind.astype(F32) + left.astype(F32)
        right, left = ring_send(ahead.astype(BF), 1), ring_send(behind.astype(BF), -1)
    yield
    right, left = in_order(right, left)
    yield
    return term(0).astype(F32) + right.astype(F32) + left.astype(F32)


def after(v, *others):
    return lax.optimization_barrier((v, *others))[0]


class Order:
    def __init__(self, first):
        self.last = first

    def __call__(self, *values):
        self.last, *values = lax.optimization_barrier((self.last, *values))
        return values[0] if len(values) == 1 else values


def sum_fsdp(v, in_order):
    size = lax.axis_size("fsdp")
    mask = 1
    while mask < size:
        other = swap(v, mask)
        yield
        v = v + in_order(other)
        yield
        mask *= 2
    return v


def body(
    tokens, attn_gain, w_query, w_key, w_value, query_gain, key_gain, w_out,
    ffn_gain, w_router, w_gate, w_up, w_down, routes, cotangent,
):
    ctx_size = lax.axis_size("ctx")
    parts = lax.axis_size("fsdp")
    rows = tokens.shape[1]
    width = tokens.shape[2]
    slab = w_query.shape[0]
    head_dim = query_gain.shape[0]
    own_heads = width // head_dim // parts
    own_width = own_heads * head_dim
    own_rows = slab // ctx_size
    own_experts = w_gate.shape[1]
    hidden_units = w_gate.shape[2]
    experts = own_experts * ctx_size
    seq_length = rows * ctx_size
    in_order = Order(jnp.zeros((), F32))

    heads = 2 * own_heads
    repeats = ctx_size // heads
    order = ring_order(ctx_size)
    offsets = [0] + [o for step in range(1, ctx_size // 2) for o in (step, ctx_size - step)] + [ctx_size // 2]
    at_ring, at_place, at_core, at_side = 0, 1, 2, 3
    at_slab = [4 + mask for mask in range(parts)]
    at_groups, at_beside, at_chip = (8, 9), (10, 11), (12, 13, 14, 15)
    at_from = 16
    at_blocks = [at_from + ctx_size + index for index in range(ctx_size)]
    at_heads = [(at_from + 2 * ctx_size + index, at_from + 3 * ctx_size + index) for index in range(ctx_size)]
    at_turn = at_from + 4 * ctx_size
    at_back = at_from + 5 * ctx_size
    lines = []
    for place in range(ctx_size):
        ring_place = order.index(place)
        for mine in range(parts):
            side, core = divmod(mine, 2)
            line = [ring_place, place, core, side] + [mine ^ mask for mask in range(parts)]
            line += [core, core + 2, 1 - core, 3 - core, 2 * side, 2 * side + 1, 2 - 2 * side, 3 - 2 * side]
            places = [order[(ring_place + offset) % ctx_size] for offset in offsets]
            line += places
            line += [(ring_place + offset) % ctx_size for offset in offsets]
            for first in (core, 1 - core):
                line += [first * own_heads + other // repeats + other // repeats // own_heads * own_heads for other in places]
            line += [(ring_place + index) % ctx_size for index in range(ctx_size)]
            line += [offsets.index((order.index(other) - ring_place) % ctx_size) for other in range(ctx_size)]
            lines.append(line)
    device = lax.axis_index("ctx").astype(jnp.uint32) * parts + lax.axis_index("fsdp").astype(jnp.uint32)
    table = lax.dynamic_slice(jnp.asarray(np.array(lines, np.int32)), (device, jnp.uint32(0)), (1, len(lines[0])))
    table = table.reshape(-1)

    def spread_pairs(v):
        if repeats > 1:
            v = jnp.repeat(v, repeats, axis=0)
        return lax.all_to_all(v, "ctx", split_axis=0, concat_axis=0, tiled=True)

    def collect_pairs(v):
        v = lax.all_to_all(v, "ctx", split_axis=0, concat_axis=0, tiled=True)
        return v[::repeats] if repeats > 1 else v

    projections = (w_query, w_key, w_value)

    def side_of(row, rows, slots):
        return row, rows, [(number, slot, own_width) for number in range(3) for slot in slots]

    row, rows_of, some = side_of(at_ring, own_rows, at_groups)
    fetched = in_order(
        *take_parts(
            table, (*projections, w_out), [(row, rows_of, some + [(3, None, width)]), side_of(row, rows_of, at_beside)], SMALL
        )
    )
    fetched = swap(fetched[0], 2), swap(fetched[1], 3)
    cot_blocks = {}
    cot_ring = Ring(ring_gather(after(cotangent[0], in_order.last), in_order, cot_blocks))
    source = tokens[0].astype(F32)
    factor_one = lax.rsqrt(jnp.mean(source * source, axis=-1, keepdims=True) + EPSILON)
    normed = (source * factor_one * attn_gain).astype(BF)
    projections, w_down, w_gate, w_up = after((projections, w_down, w_gate, w_up), in_order.last)
    near, own = in_order(
        *take_parts(
            table, projections, [side_of(None, slab, at_beside), side_of(None, slab, at_groups)], MEDIUM
        )
    )
    cot_ring.step()
    beside, near = swap(normed, 1), swap(near, 1)
    w_down = in_order(merge_experts(after(w_down, in_order.last)))
    cot_ring.land()
    fetched = in_order(*fetched)
    column_blocks = {}
    ring = Ring(ring_gather(fetched_payload(table, *fetched, width), in_order, column_blocks))
    down_w = lax.all_gather(after(w_down, in_order.last), "fsdp", axis=0, tiled=True)
    w_gate = in_order(merge_experts(after(w_gate, in_order.last)))
    ring.step()
    gate_w = lax.all_gather(after(w_gate, in_order.last), "fsdp", axis=0, tiled=True)
    w_router, routes = after((w_router, routes), in_order.last)
    router = [w_router, swap(w_router, 1), swap(w_router, 2), swap(w_router, 3)]
    routes_all = lax.all_to_all(
        jnp.broadcast_to(routes, (ctx_size, *routes.shape[1:])), "ctx", split_axis=0, concat_axis=0, tiled=True
    )
    normed, near, beside = in_order(normed, near, beside)
    w_up = in_order(merge_experts(after(w_up, in_order.last)))
    ring.step()
    up_w = lax.all_gather(after(w_up, in_order.last), "fsdp", axis=0, tiled=True)
    routes_all, *router = in_order(routes_all, *router)
    ring.step()

    half = head_dim // 2
    frequency = ROPE_BASE ** (-jnp.arange(half, dtype=F32) * 2.0 / head_dim)
    angles = jnp.arange(seq_length, dtype=jnp.int32).astype(F32)[:, None] * frequency[None, :]
    cosine, sine = jnp.cos(angles), jnp.sin(angles)
    cosine = jnp.concatenate([cosine, cosine], axis=1)
    sine = jnp.concatenate([-sine, sine], axis=1)
    q_gain, k_gain = query_gain[None, :], key_gain[None, :]

    ring.finish()
    qkv, own_columns = own_pairs(
        table,
        (normed, beside),
        own,
        near,
        [column_blocks[offset] for offset in offsets],
        3,
        head_dim,
        at_slab,
        at_blocks,
    )
    qkv = spread_pairs(in_order(qkv))
    router_w = in_order(place_rows(table, after(router, in_order.last), at_slab))
    w_far = in_order(far_rows(table, [column_blocks[offset] for offset in offsets], at_blocks))
    qkv = in_order(qkv)
    down_w, gate_w = in_order(down_w, gate_w)
    mixed = in_order(attend(qkv, q_gain, k_gain, cosine, sine))
    mixed = in_order(collect_pairs(mixed))
    hidden, far = in_order(*mixed_out(table, mixed, w_out, w_far, at_side))
    far = swap(far, 1)
    hidden = in_order(source + hidden)
    hidden = hidden + in_order(far).astype(F32)
    up_w = in_order(up_w)
    factor_two = lax.rsqrt(jnp.mean(hidden * hidden, axis=-1, keepdims=True) + EPSILON)
    ffn_in = in_order((hidden * factor_two * ffn_gain).astype(BF))

    ffn_blocks = {}
    ffn_ring = Ring(ring_gather(ffn_in, in_order, ffn_blocks))
    ffn_ring.step()

    size = 4
    groups = [offsets[first : first + size] for first in range(0, ctx_size, size)]

    def group_cots(group):
        return in_order(*stacked_matmul([cot_blocks[o] for o in groups[group]], down_w))

    def group_units(group, grad_act):
        return in_order(
            *expert_units(
                table, at_place, at_from + group * size, [ffn_blocks[o] for o in groups[group]], routes_all, router_w,
                gate_w, up_w, grad_act, own_experts,
            )
        )

    cots = [group_cots(0)]
    ffn_ring.step()
    cot_ring.step()
    units = [group_units(0, cots[0][0])]
    ffn_ring.step()
    cot_ring.step()
    other_side = (1 - table[at_side]).astype(jnp.uint32) * own_heads
    zero = jnp.uint32(0)
    other_mixed = lax.dynamic_slice(
        after(mixed, in_order.last), (other_side, zero, zero, zero), (own_heads, *mixed.shape[1:])
    )
    other_mixed = swap(other_mixed, 2)
    cot_ring.finish()
    ffn_ring.finish()
    normed_blocks = {}
    normed_ring = Ring(ring_gather(after(normed, in_order.last), in_order, normed_blocks))
    for group in range(1, len(groups)):
        cots.append(group_cots(group))
        if group == 1:
            normed_ring.step()
        units.append(group_units(group, cots[group][0]))
    cots = [part for _unused, part in cots]
    acts, gate_grads, up_grads, d_gates, inputs = zip(*units)

    def term_of(terms):
        def term(offset):
            group, index = divmod(offsets.index(offset), size)
            return terms[group][index * rows : (index + 1) * rows]

        return term

    def weight_grad(lefts, rights):
        lefts, rights = after((lefts, rights), in_order.last)
        return in_order(sum_of_outer(lefts, rights))

    def share(grad):
        return lax.psum_scatter(after(grad, in_order.last), "fsdp", scatter_dimension=0, tiled=True)

    grad_rows = {}

    def make_rows(group):
        some = after((gate_grads[group], up_grads[group]), in_order.last)
        grad_rows[group] = in_order(expert_rows(*some, gate_w, up_w))

    other_mixed = in_order(other_mixed)
    normed_ring.step()
    for group in range(len(groups) - 1, 0, -1):
        make_rows(group)
    normed_ring.step()
    row_ring = Ring(ring_scatter(term_of(grad_rows), in_order))
    d_gate = weight_grad(inputs, gate_grads)
    row_ring.step()
    d_gate = share(d_gate)
    normed_ring.finish()
    make_rows(0)
    row_ring.step()
    weighted = in_order(*times_transpose(after(acts, in_order.last), down_w))
    row_ring.step()
    ring = Ring(ring_scatter(term_of(weighted), in_order))
    d_gates = jnp.concatenate(after(d_gates, in_order.last), axis=1).reshape(own_experts, ctx_size, rows)
    d_gates = d_gates.at[:, table[at_back : at_back + ctx_size], :].get(mode="promise_in_bounds").transpose(1, 0, 2)
    d_gates = lax.all_to_all(d_gates, "ctx", split_axis=0, concat_axis=0, tiled=True)
    normed_t = in_order(transposed(table, [normed_blocks[offset] for offset in offsets], at_chip))
    row_ring.land()
    d_gates = in_order(d_gates).reshape(experts, rows).T
    beside_t = swap(normed_t, 1)
    gates = routed_gates(dot(ffn_in, router_w), routes[0])
    grad_logits = gates * (d_gates - jnp.sum(gates * d_gates, axis=-1, keepdims=True))
    routed = dot(grad_logits, router_w.astype(F32), ((1,), (1,)), precision=lax.Precision.HIGHEST)
    routed = in_order(routed)
    grad_ffn_in = row_ring.finish() + routed

    inner = grad_ffn_in * ffn_gain
    grad_hidden = (
        cotangent[0].astype(F32)
        + factor_two * inner
        - hidden * (factor_two * factor_two * factor_two) * jnp.mean(inner * hidden, axis=-1, keepdims=True)
    )
    grad_proj, grad_hidden, grad_ffn_in = in_order(grad_hidden.astype(BF), grad_hidden, grad_ffn_in)

    beside = swap(grad_proj, 1)
    grad_proj, beside, beside_t = in_order(grad_proj, beside, beside_t)
    grad_mixed = in_order(grad_pairs(table, grad_proj, beside, w_out, w_far, at_side, head_dim))
    across = swap(after(grad_proj, in_order.last), 2)
    ring.step()
    grad_mixed = spread_pairs(grad_mixed)
    d_up = weight_grad(inputs, up_grads)
    grad_mixed = in_order(grad_mixed)
    d_up = share(d_up)
    across = in_order(across)
    diagonal = in_order(swap(across, 1))
    mixed = after(mixed, in_order.last)
    d_out = in_order(
        out_grads(table, mixed, other_mixed, [grad_proj, beside, across, diagonal], at_turn, own_rows, at_side)
    )
    ring.step()
    out_ring = Ring(ring_scatter(lambda offset: d_out[offset * own_rows : (offset + 1) * own_rows], in_order))
    grads, head_gains = in_order(*attend_back(qkv, grad_mixed, q_gain, k_gain, cosine, sine))
    if repeats > 1:
        head_gains = jnp.where(lax.axis_index("ctx") % repeats == 0, head_gains, 0.0)
    ring.step()
    out_ring.step()

    half_grads = in_order(head_weights(table, grads, normed_t, beside_t, 3, at_from))
    other_half = swap(half_grads[width // 2 :], 2)
    grads = collect_pairs(grads)
    d_down = weight_grad(cots, acts)
    other_half = in_order(other_half)
    d_down = share(d_down)
    keep, send = in_order(*chip_total(table, half_grads, other_half, at_core))
    send = in_order(swap(send, 1))
    pieces = {}
    total_ring = Ring(ring_gather(side_by_side(table, keep, send), in_order, pieces))
    output = in_order((hidden + ring.finish()).astype(BF))
    out_ring.step()
    d_ffn_gain = jnp.sum(grad_ffn_in * hidden * factor_two, axis=0, keepdims=True)
    d_router = dot(grad_logits, ffn_in.astype(F32), ((0,), (0,)), precision=lax.Precision.HIGHEST)
    early = in_order(jnp.concatenate([d_router, d_ffn_gain]))
    early = Ring(sum_fsdp(early, in_order))
    grads = in_order(grads)
    own, far = in_order(*pair_normed(grads, own_columns, 3))
    far = swap(far, 1)
    early.step()
    total_ring.step()
    out_ring.step()

    whole = None
    seen = set()

    def take_whole(arrays):
        new = [index for index, offset in enumerate(offsets) if offset in pieces and index not in seen]
        seen.update(new)
        high = pieces[offsets[0]].shape[0]
        for first in range(0, len(new), 4):
            some = new[first : first + 4]
            cuts = []
            for number, index in enumerate(some):
                for where in range(2):
                    for kind in range(3):
                        at = (where * 3 + kind) * head_dim
                        cuts.append((number, (0, high), (at, at + head_dim), kind, at_heads[index][where], False))
            found = [pieces[offsets[index]] for index in some]
            arrays = in_order(*spread(table, found, cuts, (slab, width), 3, arrays))
        return arrays

    whole = take_whole(whole)
    early.finish()
    grad_normed = own + in_order(far).astype(F32)
    d_attn_gain = jnp.sum(grad_normed * source * factor_one, axis=0)
    inner = grad_normed * attn_gain
    d_tokens = (
        grad_hidden
        + factor_one * inner
        - source * (factor_one * factor_one * factor_one) * jnp.mean(inner * source, axis=-1, keepdims=True)
    )
    d_tokens, d_attn_gain = in_order(d_tokens, d_attn_gain)
    late = jnp.concatenate([d_attn_gain, head_gains[0], head_gains[1], jnp.zeros((width - 2 * head_dim,), F32)])
    late = Ring(sum_fsdp(late.reshape(2, width), in_order))
    d_gate = in_order(split_experts(after(d_gate, in_order.last), own_experts))
    total_ring.step()
    d_out = out_ring.finish()
    late.step()
    whole = take_whole(whole)
    packed = in_order(pack_gains(table, d_out, early.value, late.finish(), at_slab[0], experts))
    packed_pieces = {}
    packed_ring = Ring(ring_gather(packed, in_order, packed_pieces))
    d_up = in_order(split_experts(after(d_up, in_order.last), own_experts))
    total_ring.step()
    whole = take_whole(whole)
    packed_ring.step()
    total_ring.finish()
    whole = take_whole(whole)
    d_query, d_key, d_value = whole
    packed_ring.step()
    d_down = in_order(split_experts(after(d_down, in_order.last), own_experts))
    packed_ring.finish()
    packed_blocks = [packed_pieces[offset] for offset in offsets]
    cuts = [(index, (0, own_rows), (0, width), 0, at_blocks[index], True) for index in range(ctx_size)]
    (d_out,) = spread(table, packed_blocks, cuts, (slab, width), 1, None)
    height = packed.shape[0] - own_rows
    d_router, gains = unpack_gains(table, packed_blocks, at_back, experts, height)
    d_ffn_gain, d_attn_gain, head_gains = gains + in_order.last
    return (
        output[None],
        d_tokens[None],
        d_attn_gain,
        d_query,
        d_key,
        d_value,
        head_gains[:head_dim],
        head_gains[head_dim : 2 * head_dim],
        d_out,
        d_ffn_gain,
        d_router,
        d_gate,
        d_up,
        d_down,
    )


def solution(mesh):
    token_split = P("fsdp", "ctx", None)
    row_split = P("fsdp", None)
    return jax.shard_map(
        body,
        mesh=mesh,
        in_specs=(
            token_split, P(), row_split, row_split, row_split, P(), P(), row_split,
            P(), row_split, token_split, token_split, token_split, token_split, token_split,
        ),
        out_specs=(
            token_split, token_split, P(), row_split, row_split, row_split, P(), P(),
            row_split, P(), row_split, token_split, token_split, token_split,
        ),
        check_vma=False,
    )
```

```python
import functools

import jax
import jax.numpy as jnp
import numpy as np
from jax import lax
from jax.experimental import pallas as pl
from jax.experimental.pallas import tpu as pltpu
from jax.sharding import PartitionSpec as P

EPSILON = 1e-06
ROPE_BASE = 10000.0
BF = jnp.bfloat16
F32 = jnp.float32
LONG = pl.CostEstimate(flops=10**12, bytes_accessed=10**9, transcendentals=0)
MEDIUM = pl.CostEstimate(flops=2 * 10**10, bytes_accessed=5 * 10**7, transcendentals=0)
SMALL = pl.CostEstimate(flops=1, bytes_accessed=1, transcendentals=0)


def dot(a, b, contract=((1,), (0,)), precision=None):
    return lax.dot_general(a, b, (contract, ((), ())), precision=precision, preferred_element_type=F32)


def dot_nt(a, b):
    return dot(a, b, ((1,), (1,)))


def dot_tn(a, b):
    return dot(a, b, ((0,), (0,)))


def head_norm(v, gain):
    factor = lax.rsqrt(jnp.mean(v * v, axis=-1, keepdims=True) + EPSILON)
    return v * factor * gain, factor


def turn(v, cosine, sine):
    return v * cosine + pltpu.roll(v, v.shape[-1] // 2, 1) * sine


def head_back(grad, v, gain, cosine, sine):
    grad = turn(grad, cosine, -sine)
    factor = lax.rsqrt(jnp.mean(v * v, axis=-1, keepdims=True) + EPSILON)
    gain_grad = jnp.sum(grad * v * factor, axis=0, keepdims=True)
    inner = grad * gain
    return factor * inner - v * (factor * factor * factor) * jnp.mean(inner * v, axis=-1, keepdims=True), gain_grad


def rows_of(ref):
    block = ref[...]
    return block.reshape(-1, block.shape[-1])


def attend_kernel(q_ref, k_ref, v_ref, qg_ref, kg_ref, cos_ref, sin_ref, o_ref, keys, values_t):
    step = pl.program_id(1)

    @pl.when(step == 0)
    def _():
        normed, _unused = head_norm(rows_of(k_ref).astype(F32), kg_ref[...])
        keys[...] = turn(normed, cos_ref[...], sin_ref[...]).astype(BF)
        values_t[...] = rows_of(v_ref).astype(F32).T.astype(BF)

    queries = rows_of(q_ref).astype(F32)
    number, head_dim = queries.shape
    here = pl.ds(pl.multiple_of(step * number, number), number)
    normed, _unused = head_norm(queries, qg_ref[...])
    queries = turn(normed, cos_ref[here, :], sin_ref[here, :]).astype(BF)
    weights = jnp.exp(dot_nt(keys[...], queries) * (head_dim**-0.5))
    total = jnp.sum(weights, axis=0, keepdims=True)
    mixed = dot(values_t[...], weights.astype(BF)) / total
    o_ref[...] = mixed.T.astype(BF).reshape(o_ref.shape)


def attend_back_kernel(
    q_ref, k_ref, v_ref, m_ref, qg_ref, kg_ref, cos_ref, sin_ref,
    g_ref, gain_ref, keys, keys_t, key_acc, value_acc,
):
    pair = pl.program_id(0)
    step = pl.program_id(1)
    last = pl.num_programs(1) - 1

    @pl.when((pair == 0) & (step == 0))
    def _():
        gain_ref[...] = jnp.zeros_like(gain_ref)

    @pl.when(step == 0)
    def _():
        normed, _unused = head_norm(rows_of(k_ref).astype(F32), kg_ref[...])
        turned = turn(normed, cos_ref[...], sin_ref[...])
        keys[...] = turned.astype(BF)
        keys_t[...] = turned.T.astype(BF)
        key_acc[...] = jnp.zeros_like(key_acc)
        value_acc[...] = jnp.zeros_like(value_acc)

    query_pre = rows_of(q_ref).astype(F32)
    grad_mixed = rows_of(m_ref)
    number, head_dim = query_pre.shape
    scale = head_dim**-0.5
    here = pl.ds(pl.multiple_of(step * number, number), number)
    cosine, sine = cos_ref[here, :], sin_ref[here, :]
    normed, _unused = head_norm(query_pre, qg_ref[...])
    queries = turn(normed, cosine, sine).astype(BF)
    weights = jnp.exp(dot_nt(keys[...], queries) * scale)
    probs = weights * (1.0 / jnp.sum(weights, axis=0, keepdims=True))
    value_acc[...] += dot(probs.astype(BF), grad_mixed)
    weighted = probs * dot_nt(rows_of(v_ref), grad_mixed)
    delta = jnp.sum(weighted, axis=0, keepdims=True)
    grad_scores = (weighted - probs * delta).astype(BF)
    key_acc[...] += dot(grad_scores, queries)
    grad_query = dot(keys_t[...], grad_scores).T * scale
    grad_query, gain_grad = head_back(grad_query, query_pre, qg_ref[...], cosine, sine)
    rows = g_ref.shape[2]
    blocks = number // rows
    g_ref[pl.ds(step * blocks, blocks), 0] = grad_query.astype(BF).reshape(blocks, rows, head_dim)
    gain_ref[0:1, :] += gain_grad

    @pl.when(step == last)
    def _():
        grad_key, gain_grad = head_back(
            key_acc[...] * scale, rows_of(k_ref).astype(F32), kg_ref[...], cos_ref[...], sin_ref[...]
        )
        g_ref[:, 1] = grad_key.astype(BF).reshape(-1, rows, head_dim)
        g_ref[:, 2] = value_acc[...].astype(BF).reshape(-1, rows, head_dim)
        gain_ref[1:2, :] += gain_grad


def attention_specs(shape):
    blocks, pairs, rows, head_dim = shape
    at_once = max(1, 256 // rows)
    while blocks % at_once:
        at_once -= 1
    pairs //= 3
    part = pl.BlockSpec((at_once, 1, rows, head_dim), lambda p, i: (i, p, 0, 0))
    three = [
        pl.BlockSpec((at_once, 1, rows, head_dim), lambda p, i: (i, 3 * p, 0, 0)),
        pl.BlockSpec((blocks, 1, rows, head_dim), lambda p, i: (0, 3 * p + 1, 0, 0)),
        pl.BlockSpec((blocks, 1, rows, head_dim), lambda p, i: (0, 3 * p + 2, 0, 0)),
    ]
    gain = pl.BlockSpec((1, head_dim), lambda p, i: (0, 0))
    table = pl.BlockSpec((blocks * rows, head_dim), lambda p, i: (0, 0))
    params = pltpu.CompilerParams(
        dimension_semantics=("arbitrary", "arbitrary"),
        vmem_limit_bytes=(24 if blocks * rows <= 1024 else 56) * 2**20,
    )
    return part, three, gain, table, (pairs, blocks // at_once), params


def attend(qkv, query_gain, key_gain, cosine, sine):
    part, three, gain, table, grid, params = attention_specs(qkv.shape)
    blocks, _unused, rows, head_dim = qkv.shape
    length = blocks * rows
    return pl.pallas_call(
        attend_kernel,
        grid=grid,
        in_specs=[*three, gain, gain, table, table],
        out_specs=part,
        out_shape=jax.ShapeDtypeStruct((blocks, grid[0], rows, head_dim), BF),
        scratch_shapes=[pltpu.VMEM((length, head_dim), BF), pltpu.VMEM((head_dim, length), BF)],
        compiler_params=params,
        cost_estimate=MEDIUM,
        name="attend",
    )(qkv, qkv, qkv, query_gain, key_gain, cosine, sine)


def attend_back(qkv, grad_mixed, query_gain, key_gain, cosine, sine):
    part, three, gain, table, grid, params = attention_specs(qkv.shape)
    blocks, _unused, rows, head_dim = qkv.shape
    length = blocks * rows
    return pl.pallas_call(
        attend_back_kernel,
        grid=grid,
        in_specs=[*three, part, gain, gain, table, table],
        out_specs=[
            pl.BlockSpec((blocks, 3, rows, head_dim), lambda p, i: (0, p, 0, 0)),
            pl.BlockSpec((8, head_dim), lambda p, i: (0, 0)),
        ],
        out_shape=[jax.ShapeDtypeStruct(qkv.shape, BF), jax.ShapeDtypeStruct((8, head_dim), F32)],
        scratch_shapes=[
            pltpu.VMEM((length, head_dim), BF),
            pltpu.VMEM((head_dim, length), BF),
            pltpu.VMEM((length, head_dim), F32),
            pltpu.VMEM((length, head_dim), F32),
        ],
        compiler_params=params,
        cost_estimate=LONG,
        name="attend_back",
    )(qkv, qkv, qkv, grad_mixed, query_gain, key_gain, cosine, sine)


def stack_blocks(block_refs, out_ref):
    rows = block_refs[0].shape[0]
    for index, block_ref in enumerate(block_refs):
        out_ref[index * rows : (index + 1) * rows, :] = block_ref[...]


def stacked_kernel(w_ref, *refs):
    *block_refs, o_ref, rows_ref = refs

    @pl.when(pl.program_id(0) == 0)
    def _():
        stack_blocks(block_refs, rows_ref)

    o_ref[...] = dot(rows_ref[...], w_ref[...])


def stacked_matmul(blocks, weight):
    rows, depth = len(blocks) * blocks[0].shape[0], weight.shape[0]
    wide = min(512, weight.shape[1])
    return pl.pallas_call(
        stacked_kernel,
        grid=(weight.shape[1] // wide,),
        in_specs=[pl.BlockSpec((depth, wide), lambda n: (0, n))]
        + [pl.BlockSpec(block.shape, lambda n: (0, 0)) for block in blocks],
        out_specs=[pl.BlockSpec((rows, wide), lambda n: (0, n)), pl.BlockSpec((rows, depth), lambda n: (0, 0))],
        out_shape=[jax.ShapeDtypeStruct((rows, weight.shape[1]), F32), jax.ShapeDtypeStruct((rows, depth), BF)],
        compiler_params=pltpu.CompilerParams(dimension_semantics=("arbitrary",), vmem_limit_bytes=56 * 2**20),
        cost_estimate=LONG,
        name="stacked_matmul",
    )(weight, *blocks)


def routed_gates(logits, routes):
    columns = lax.broadcasted_iota(jnp.int32, logits.shape, 1)
    chosen = columns == routes[:, 0:1]
    for index in range(1, routes.shape[1]):
        chosen = chosen | (columns == routes[:, index : index + 1])
    high = jnp.max(jnp.where(chosen, logits, -1e30), axis=-1, keepdims=True)
    weights = jnp.where(chosen, jnp.exp(jnp.where(chosen, logits - high, 0.0)), 0.0)
    return weights / jnp.sum(weights, axis=-1, keepdims=True)


def expert_kernel(table_ref, router_ref, routes_ref, gate_w_ref, up_w_ref, grad_ref, *refs, per, place, at):
    *block_refs, act_ref, gate_ref, up_ref, d_gates_ref, x_ref, gates_ref = refs
    step = pl.program_id(0)

    @pl.when(step == 0)
    def _():
        stack_blocks(block_refs, x_ref)
        routes = jnp.concatenate([routes_ref[table_ref[at + index]] for index in range(len(block_refs))], axis=0)
        gates = routed_gates(dot(x_ref[...], router_ref[...]), routes)
        columns = lax.broadcasted_iota(jnp.int32, gates.shape, 1)
        count = gates_ref.shape[0]
        for index in range(count):
            here = columns == table_ref[place] * count + index
            gates_ref[index] = jnp.sum(jnp.where(here, gates, 0.0), axis=1, keepdims=True)

    @pl.when(step % per == 0)
    def _():
        d_gates_ref[...] = jnp.zeros_like(d_gates_ref)

    gate_pre = dot(x_ref[...], gate_w_ref[...])
    up_pre = dot(x_ref[...], up_w_ref[...])
    grad_act = grad_ref[...]
    gates = gates_ref[step // per]
    sigmoid = 1.0 / (1.0 + jnp.exp(-gate_pre))
    silu = gate_pre * sigmoid
    act = (silu * up_pre).astype(BF).astype(F32)
    d_gates_ref[0] += jnp.sum(act * grad_act, axis=1, keepdims=True)
    grad_act = grad_act * gates
    act_ref[...] = (act * gates).astype(BF)
    up_ref[...] = (grad_act * silu).astype(BF)
    gate_ref[...] = (grad_act * up_pre * (sigmoid * (1.0 + gate_pre * (1.0 - sigmoid)))).astype(BF)


def expert_units(table, place, at, blocks, routes, router_w, gate_w, up_w, grad_act, count):
    rows, width = len(blocks) * blocks[0].shape[0], blocks[0].shape[1]
    units = gate_w.shape[1]
    wide = min(512, units // count)
    per = units // wide // count
    weight = pl.BlockSpec((width, wide), lambda n: (0, n))
    tile = pl.BlockSpec((rows, wide), lambda n: (0, n))
    out = jax.ShapeDtypeStruct((rows, units), BF)
    return pl.pallas_call(
        functools.partial(expert_kernel, per=per, place=place, at=at),
        grid=(units // wide,),
        in_specs=[
            pl.BlockSpec(memory_space=pltpu.SMEM),
            pl.BlockSpec(router_w.shape, lambda n: (0, 0)),
            pl.BlockSpec(routes.shape, lambda n: (0, 0, 0)),
            weight,
            weight,
            tile,
        ]
        + [pl.BlockSpec(block.shape, lambda n: (0, 0)) for block in blocks],
        out_specs=[
            tile,
            tile,
            tile,
            pl.BlockSpec((1, rows, 1), lambda n: (n // per, 0, 0)),
            pl.BlockSpec((rows, width), lambda n: (0, 0)),
        ],
        out_shape=[
            out, out, out, jax.ShapeDtypeStruct((count, rows, 1), F32), jax.ShapeDtypeStruct((rows, width), BF),
        ],
        scratch_shapes=[pltpu.VMEM((count, rows, 1), F32)],
        compiler_params=pltpu.CompilerParams(dimension_semantics=("arbitrary",), vmem_limit_bytes=58 * 2**20),
        cost_estimate=MEDIUM,
        name="expert_units",
    )(table, router_w, routes, gate_w, up_w, grad_act, *blocks)


def expert_rows_kernel(gate_ref, up_ref, gate_w_ref, up_w_ref, o_ref):
    o_ref[...] = (dot_nt(gate_ref[...], gate_w_ref[...]) + dot_nt(up_ref[...], up_w_ref[...])).astype(BF)


def expert_rows(gate_grads, up_grads, gate_w, up_w):
    rows, units = gate_grads.shape
    width = gate_w.shape[0]
    wide = min(512, width)
    whole = pl.BlockSpec((rows, units), lambda n: (0, 0))
    weight = pl.BlockSpec((wide, units), lambda n: (n, 0))
    return pl.pallas_call(
        expert_rows_kernel,
        grid=(width // wide,),
        in_specs=[whole, whole, weight, weight],
        out_specs=pl.BlockSpec((rows, wide), lambda n: (0, n)),
        out_shape=jax.ShapeDtypeStruct((rows, width), BF),
        compiler_params=pltpu.CompilerParams(dimension_semantics=("arbitrary",), vmem_limit_bytes=56 * 2**20),
        cost_estimate=MEDIUM,
        name="expert_rows",
    )(gate_grads, up_grads, gate_w, up_w)


def times_kernel(b_ref, *refs):
    count = len(refs) // 2
    for a_ref, o_ref in zip(refs[:count], refs[count:]):
        o_ref[...] = dot_nt(a_ref[...], b_ref[...]).astype(o_ref.dtype)


def times_transpose(lefts, b):
    columns, depth = b.shape
    wide = min(512, columns)
    return pl.pallas_call(
        times_kernel,
        grid=(columns // wide,),
        in_specs=[pl.BlockSpec((wide, depth), lambda n: (n, 0))]
        + [pl.BlockSpec(left.shape, lambda n: (0, 0)) for left in lefts],
        out_specs=[pl.BlockSpec((left.shape[0], wide), lambda n: (0, n)) for left in lefts],
        out_shape=[jax.ShapeDtypeStruct((left.shape[0], columns), BF) for left in lefts],
        compiler_params=pltpu.CompilerParams(dimension_semantics=("arbitrary",), vmem_limit_bytes=58 * 2**20),
        cost_estimate=MEDIUM,
        name="times_transpose",
    )(b, *lefts)


def sum_kernel(_unused, *refs):
    *pair_refs, o_ref = refs
    count = len(pair_refs) // 2
    total = dot_tn(pair_refs[0][...], pair_refs[count][...])
    for index in range(1, count):
        total = total + dot_tn(pair_refs[index][...], pair_refs[count + index][...])
    o_ref[...] = total.astype(o_ref.dtype)


def sum_of_outer(table, lefts, rights, slots=None):
    whole = not isinstance(lefts, (list, tuple))
    count, depth = len(rights), rights[0].shape[0]
    rows, columns = (lefts if whole else lefts[0]).shape[1], rights[0].shape[1]
    tall, wide = 512, columns if count <= 2 else min(1024, columns)

    def left_spec(index):
        at = index if whole else 0
        if slots is None:
            return pl.BlockSpec((depth, tall), lambda n, m, t: (at, m))
        return pl.BlockSpec((depth, tall), lambda n, m, t: (at, t[slots[0] + m]))

    return pl.pallas_call(
        sum_kernel,
        grid_spec=pltpu.PrefetchScalarGridSpec(
            num_scalar_prefetch=1,
            grid=(columns // wide, rows // tall),
            in_specs=[left_spec(index) for index in range(count)]
            + [pl.BlockSpec((depth, wide), lambda n, m, t: (0, n)) for _unused in rights],
            out_specs=pl.BlockSpec((tall, wide), lambda n, m, t: (m, n)),
        ),
        out_shape=jax.ShapeDtypeStruct((rows, columns), BF),
        compiler_params=pltpu.CompilerParams(
            dimension_semantics=("arbitrary", "arbitrary"), vmem_limit_bytes=56 * 2**20
        ),
        cost_estimate=LONG,
        name="sum_of_outer",
    )(table, *([lefts] * count if whole else lefts), *rights)


def add_kernel(_unused, left_ref, right_ref, o_ref):
    o_ref[...] = (left_ref[...].astype(F32) + right_ref[...].astype(F32)).astype(BF)


def add_slabs(table, left, right, first, second):
    columns = left.shape[1]
    slab = left.shape[0] // 4
    tall = slab // 4

    def spec(at):
        return pl.BlockSpec((tall, columns), lambda m, t: (4 * at + m, 0))

    return pl.pallas_call(
        add_kernel,
        grid_spec=pltpu.PrefetchScalarGridSpec(
            num_scalar_prefetch=1, grid=(4,), in_specs=[spec(first), spec(second)], out_specs=spec(0)
        ),
        out_shape=jax.ShapeDtypeStruct((slab, columns), BF),
        cost_estimate=SMALL,
        name="add_slabs",
    )(table, left, right)


NN, NT = ((1,), (0,)), ((1,), (1,))


def small_call(kernel, name, out_shape, *operands, cost=SMALL, scratch=(), **kwargs):
    vmem = pl.BlockSpec(memory_space=pltpu.VMEM)
    return pl.pallas_call(
        functools.partial(kernel, **kwargs),
        in_specs=[pl.BlockSpec(memory_space=pltpu.SMEM)] + [vmem] * (len(operands) - 1),
        out_specs=jax.tree.map(lambda _unused: vmem, out_shape),
        out_shape=out_shape,
        scratch_shapes=list(scratch),
        compiler_params=pltpu.CompilerParams(vmem_limit_bytes=48 * 2**20),
        cost_estimate=cost,
        name=name,
    )(*operands)


def payload_kernel(_unused, a_ref, b_ref, o_ref):
    rows, width = b_ref.shape[0], o_ref.shape[1]
    columns = b_ref.shape[1]
    rest = columns - width
    o_ref[:rows, :] = a_ref[:, :width]
    o_ref[rows : 2 * rows, :] = b_ref[:, :width]
    o_ref[2 * rows : 3 * rows, :rest] = a_ref[:, width:columns]
    o_ref[2 * rows : 3 * rows, rest:] = b_ref[:, width:]
    o_ref[3 * rows :, :] = a_ref[:, columns:]


def fetched_payload(table, from_beyond, from_across, width):
    out = jax.ShapeDtypeStruct((4 * from_across.shape[0], width), BF)
    return small_call(payload_kernel, "fetched_payload", out, table, from_beyond, from_across)


def own_pairs_kernel(table_ref, *refs, blocks, kinds, slabs, ring_slots):
    block_refs, refs = refs[:blocks], refs[blocks:]
    own_ref, near_ref, *piece_refs = refs[:-5]
    o_ref, columns_out, columns_ref, rows_ref, sems = refs[-5:]
    head_step, kind = pl.program_id(0), pl.program_id(1)
    slab, columns = own_ref.shape
    width = piece_refs[0].shape[1]
    part = piece_refs[0].shape[0] // 4
    rest = columns - width
    back = pltpu.make_async_copy(columns_ref, columns_out, sems.at[2 + 4 * len(piece_refs)])

    @pl.when((head_step == 0) & (kind == 0))
    def _():
        def at(slot, ring_slot=None):
            start = table_ref[slot] * slab
            if ring_slot is None:
                return pl.ds(pl.multiple_of(start, slab), slab)
            return pl.ds(pl.multiple_of(start + table_ref[ring_slot] * part, part), part)

        pairs = [(own_ref, columns_ref.at[at(slabs[0]), :]), (near_ref, columns_ref.at[at(slabs[1]), :])]
        for ring_slot, piece in zip(ring_slots, piece_refs):
            for index in range(2):
                to = at(slabs[2 + index], ring_slot)
                pairs.append((piece.at[index * part : (index + 1) * part, :], columns_ref.at[to, :width]))
                some = piece.at[2 * part : 3 * part, index * rest : (index + 1) * rest]
                pairs.append((some, columns_ref.at[to, width:]))
        copies = [pltpu.make_async_copy(*pair, sems.at[index]) for index, pair in enumerate(pairs)]
        for copy in copies:
            copy.start()
        stack_blocks(block_refs, rows_ref)
        for copy in copies:
            copy.wait()
        back.start()

    rows, head_dim = o_ref.shape[2:]
    wide = o_ref.shape[0] * head_dim
    at_column = (kind * pl.num_programs(0) + head_step) * wide
    product = dot(rows_ref[...], columns_ref[:, pl.ds(pl.multiple_of(at_column, wide), wide)]).astype(BF)
    for head in range(o_ref.shape[0]):
        for block in range(blocks):
            piece = product[block * rows : (block + 1) * rows, head * head_dim : (head + 1) * head_dim]
            o_ref[head, block * kinds + kind] = piece

    @pl.when((head_step == pl.num_programs(0) - 1) & (kind == kinds - 1))
    def _():
        back.wait()


def own_pairs(table, blocks, own, near, pieces, kinds, head_dim, slabs, ring_slots):
    rows, depth = blocks[0].shape
    columns = own.shape[1]
    heads = columns // head_dim // kinds
    at_once = 2
    anywhere = pl.BlockSpec(memory_space=pl.ANY)
    return pl.pallas_call(
        functools.partial(
            own_pairs_kernel, blocks=len(blocks), kinds=kinds, slabs=slabs, ring_slots=ring_slots
        ),
        grid=(heads // at_once, kinds),
        in_specs=[pl.BlockSpec(memory_space=pltpu.SMEM)]
        + [pl.BlockSpec(block.shape, lambda h, k: (0, 0)) for block in blocks]
        + [anywhere] * (2 + len(pieces)),
        out_specs=[
            pl.BlockSpec((at_once, len(blocks) * kinds, rows, head_dim), lambda h, k: (h, 0, 0, 0)),
            anywhere,
        ],
        out_shape=[
            jax.ShapeDtypeStruct((heads, len(blocks) * kinds, rows, head_dim), BF),
            jax.ShapeDtypeStruct((depth, columns), BF),
        ],
        scratch_shapes=[
            pltpu.VMEM((depth, columns), BF),
            pltpu.VMEM((len(blocks) * rows, depth), BF),
            pltpu.SemaphoreType.DMA((3 + 4 * len(pieces),)),
        ],
        compiler_params=pltpu.CompilerParams(
            dimension_semantics=("arbitrary", "arbitrary"), vmem_limit_bytes=40 * 2**20
        ),
        cost_estimate=SMALL,
        name="own_pairs",
    )(table, *blocks, own, near, *pieces)


def far_rows_kernel(table_ref, *refs, ring_slots):
    *pieces, o_ref = refs
    part = pieces[0].shape[0] // 4
    for slot, piece in zip(ring_slots, pieces):
        o_ref[pl.ds(pl.multiple_of(table_ref[slot] * part, part), part), :] = piece[3 * part :, :]


def far_rows(table, pieces, ring_slots):
    rows, width = pieces[0].shape
    out = jax.ShapeDtypeStruct((rows // 4 * len(pieces), width), BF)
    return small_call(far_rows_kernel, "far_rows", out, table, *pieces, ring_slots=ring_slots)


def heads_of(ref, side, sequence, count):
    return [ref[side * count + head, sequence] for head in range(count)]


def mixed_out_kernel(table_ref, m_ref, w_ref, far_ref, *refs, side):
    count = m_ref.shape[0] // 2
    for sequence, ref in enumerate(refs):
        own = jnp.concatenate(heads_of(m_ref, table_ref[side], sequence, count), axis=1)
        far = jnp.concatenate(heads_of(m_ref, 1 - table_ref[side], sequence, count), axis=1)
        ref[...] = (dot(own, w_ref[...]) + dot(far, far_ref[...])).astype(ref.dtype)


def mixed_out(table, mixed, w_out, w_far, side):
    shape = (mixed.shape[2], w_out.shape[1])
    out = [jax.ShapeDtypeStruct(shape, kind) for kind in (F32, BF)]
    return small_call(mixed_out_kernel, "mixed_out", out, table, mixed, w_out, w_far, cost=MEDIUM, side=side)


def grad_pairs_kernel(table_ref, own_ref, beside_ref, w_ref, far_ref, o_ref, *, side):
    rows, head_dim = o_ref.shape[2:]
    count = o_ref.shape[0] // 2
    grads = jnp.concatenate([own_ref[...], beside_ref[...]], axis=0)
    for slab_ref, at in ((w_ref, table_ref[side]), (far_ref, 1 - table_ref[side])):
        product = dot_nt(grads, slab_ref[...]).astype(BF)
        for head in range(count):
            for sequence in range(2):
                piece = product[sequence * rows : (sequence + 1) * rows, head * head_dim : (head + 1) * head_dim]
                o_ref[at * count + head, sequence] = piece


def grad_pairs(table, own, beside, w_out, w_far, side, head_dim):
    out = jax.ShapeDtypeStruct((2 * w_out.shape[0] // head_dim, 2, own.shape[0], head_dim), BF)
    return small_call(
        grad_pairs_kernel, "grad_pairs", out, table, own, beside, w_out, w_far, cost=LONG, side=side
    )


def out_grads_kernel(table_ref, m_ref, other_ref, *refs, turn, own_rows, side):
    *block_refs, o_ref, mixed_ref, turned_ref, grads_ref = refs
    head_dim = m_ref.shape[3]
    count = m_ref.shape[0] // 2
    for head in range(count):
        rows = [m_ref[table_ref[side] * count + head, sequence] for sequence in range(2)]
        rows += [other_ref[head, sequence] for sequence in range(2)]
        rows = jnp.concatenate(rows, axis=0)
        mixed_ref[head * head_dim : (head + 1) * head_dim, :] = rows.astype(F32).T.astype(BF)
    for index in range(mixed_ref.shape[0] // own_rows):
        at = pl.multiple_of(table_ref[turn + index] * own_rows, own_rows)
        turned_ref[index * own_rows : (index + 1) * own_rows, :] = mixed_ref[pl.ds(at, own_rows), :]
    stack_blocks(block_refs, grads_ref)
    o_ref[...] = dot(turned_ref[...], grads_ref[...])


def out_grads(table, mixed, other, blocks, turn, own_rows, side):
    rows, width = blocks[0].shape
    features = mixed.shape[0] // 2 * mixed.shape[3]
    turned = pltpu.VMEM((features, len(blocks) * rows), BF)
    out = jax.ShapeDtypeStruct((features, width), F32)
    scratch = [turned, turned, pltpu.VMEM((len(blocks) * rows, width), BF)]
    return small_call(
        out_grads_kernel, "out_grads", out, table, mixed, other, *blocks, cost=LONG, scratch=scratch, turn=turn,
        own_rows=own_rows, side=side,
    )


def transposed_kernel(table_ref, *refs, slots):
    *block_refs, o_ref = refs
    rows, width = block_refs[0].shape
    slab = width // len(slots)
    for index, block_ref in enumerate(block_refs):
        for number, slot in enumerate(slots):
            here = pl.ds(pl.multiple_of(table_ref[slot] * slab, slab), slab)
            some = block_ref[:, here].astype(F32).T.astype(BF)
            o_ref[number * slab : (number + 1) * slab, index * rows : (index + 1) * rows] = some


def transposed(table, blocks, slots):
    rows, width = blocks[0].shape
    out = jax.ShapeDtypeStruct((width, len(blocks) * rows), BF)
    return small_call(transposed_kernel, "transposed", out, table, *blocks, cost=LONG, slots=slots)


def head_weights_kernel(table_ref, g_ref, own_ref, beside_ref, o_ref, grads_ref, *, kinds, places):
    rows, head_dim = g_ref.shape[2:]

    @pl.when(pl.program_id(0) == 0)
    def _():
        for index in range(g_ref.shape[0]):
            for sequence in range(2):
                for kind in range(kinds):
                    piece = g_ref[table_ref[places + index], sequence * kinds + kind]
                    here = slice(kind * head_dim, (kind + 1) * head_dim)
                    grads_ref[sequence, index * rows : (index + 1) * rows, here] = piece

    o_ref[...] = (dot(own_ref[...], grads_ref[0]) + dot(beside_ref[...], grads_ref[1])).astype(BF)


def head_weights(table, grads, own, beside, kinds, places):
    blocks, _unused, rows, head_dim = grads.shape
    width, total = own.shape
    tall = width // 4
    row = pl.BlockSpec((tall, total), lambda m: (m, 0))
    return pl.pallas_call(
        functools.partial(head_weights_kernel, kinds=kinds, places=places),
        grid=(4,),
        in_specs=[pl.BlockSpec(memory_space=pltpu.SMEM), pl.BlockSpec(grads.shape, lambda m: (0, 0, 0, 0)), row, row],
        out_specs=pl.BlockSpec((tall, kinds * head_dim), lambda m: (m, 0)),
        out_shape=jax.ShapeDtypeStruct((width, kinds * head_dim), BF),
        scratch_shapes=[pltpu.VMEM((2, total, kinds * head_dim), BF)],
        compiler_params=pltpu.CompilerParams(dimension_semantics=("arbitrary",), vmem_limit_bytes=48 * 2**20),
        cost_estimate=LONG,
        name="head_weights",
    )(table, grads, own, beside)


def chip_total_kernel(table_ref, own_ref, other_ref, keep_ref, send_ref, *, core):
    slab = keep_ref.shape[0]
    for ref, at in ((keep_ref, table_ref[core]), (send_ref, 1 - table_ref[core])):
        here = pl.ds(pl.multiple_of(at * slab, slab), slab)
        ref[...] = (own_ref[here, :].astype(F32) + other_ref[here, :].astype(F32)).astype(BF)


def chip_total(table, own, other, core):
    out = [jax.ShapeDtypeStruct((other.shape[0] // 2, own.shape[1]), BF)] * 2
    return small_call(chip_total_kernel, "chip_total", out, table, own, other, core=core)


def beside_kernel(_unused, left_ref, right_ref, o_ref):
    columns = left_ref.shape[1]
    o_ref[:, :columns] = left_ref[...].astype(BF)
    o_ref[:, columns:] = right_ref[...].astype(BF)


def side_by_side(table, left, right):
    out = jax.ShapeDtypeStruct((left.shape[0], left.shape[1] + right.shape[1]), BF)
    return small_call(beside_kernel, "side_by_side", out, table, left, right)


def pair_rows_kernel(g_ref, w_ref, own_ref, beside_ref, dn_ref, *, kinds):
    kind = pl.program_id(1)

    @pl.when((pl.program_id(0) == 0) & (kind == 0))
    def _():
        dn_ref[...] = jnp.zeros_like(dn_ref)

    heads = []
    for head in range(g_ref.shape[0]):
        heads.append(jnp.concatenate([g_ref[head, sequence * kinds + kind] for sequence in range(2)], axis=0))
    dn_ref[...] += dot_nt(jnp.concatenate(heads, axis=1), w_ref[...])

    @pl.when((pl.program_id(0) == pl.num_programs(0) - 1) & (kind == kinds - 1))
    def _():
        rows = own_ref.shape[0]
        own_ref[...] = dn_ref[:rows, :]
        beside_ref[...] = dn_ref[rows:, :].astype(BF)


def pair_normed(grads, columns, kinds):
    heads, _unused, rows, head_dim = grads.shape
    width, at_once = columns.shape[0], 2
    whole = pl.BlockSpec((rows, width), lambda h, k: (0, 0))
    return pl.pallas_call(
        functools.partial(pair_rows_kernel, kinds=kinds),
        grid=(heads // at_once, kinds),
        in_specs=[
            pl.BlockSpec((at_once, 2 * kinds, rows, head_dim), lambda h, k: (h, 0, 0, 0)),
            pl.BlockSpec((width, at_once * head_dim), lambda h, k: (0, k * (heads // at_once) + h)),
        ],
        out_specs=[whole, whole],
        out_shape=[jax.ShapeDtypeStruct((rows, width), kind) for kind in (F32, BF)],
        scratch_shapes=[pltpu.VMEM((2 * rows, width), F32)],
        compiler_params=pltpu.CompilerParams(
            dimension_semantics=("arbitrary", "arbitrary"), vmem_limit_bytes=40 * 2**20
        ),
        cost_estimate=LONG,
        name="pair_normed",
    )(grads, columns)


def take_kernel(table_ref, *refs, count, sides):
    weights, outs, sems = refs[:count], refs[count : count + len(sides)], refs[-1]
    copies = []
    for out, (row, rows, pieces) in zip(outs, sides):
        at = 0
        if row is None:
            here = slice(None)
        else:
            here = pl.ds(pl.multiple_of(table_ref[row] * rows, rows), rows)
        for number, slot, wide in pieces:
            there = slice(None)
            if slot is not None:
                there = pl.ds(pl.multiple_of(table_ref[slot] * wide, wide), wide)
            copies.append(
                pltpu.make_async_copy(
                    weights[number].at[here, there], out.at[:, at : at + wide], sems.at[len(copies)]
                )
            )
            at += wide
    for copy in copies:
        copy.start()
    for copy in copies:
        copy.wait()


def take_parts(table, weights, sides, cost):
    outs = []
    for row, rows, pieces in sides:
        outs.append(jax.ShapeDtypeStruct((rows, sum(wide for _unused, _unused2, wide in pieces)), BF))
    number = sum(len(pieces) for _unused, _unused2, pieces in sides)
    return pl.pallas_call(
        functools.partial(take_kernel, count=len(weights), sides=sides),
        in_specs=[pl.BlockSpec(memory_space=pltpu.SMEM)] + [pl.BlockSpec(memory_space=pl.ANY)] * len(weights),
        out_specs=[pl.BlockSpec(memory_space=pltpu.VMEM)] * len(sides),
        out_shape=outs,
        scratch_shapes=[pltpu.SemaphoreType.DMA((number,))],
        compiler_params=pltpu.CompilerParams(vmem_limit_bytes=60 * 2**20),
        cost_estimate=cost,
        name="take_parts",
    )(table, *weights)


def place_kernel(table_ref, *refs, slots):
    *pieces, out = refs
    for piece, slot in zip(pieces, slots):
        rows = piece.shape[0]
        out[pl.ds(pl.multiple_of(table_ref[slot] * rows, rows), rows), :] = piece[...]


def place_rows(table, pieces, slots):
    rows = sum(piece.shape[0] for piece in pieces)
    out = jax.ShapeDtypeStruct((rows, pieces[0].shape[1]), pieces[0].dtype)
    return small_call(place_kernel, "place_rows", out, table, *pieces, slots=slots)


def pack_kernel(table_ref, below_ref, early_ref, late_ref, o_ref, *, slot, experts):
    slab = o_ref.shape[1] // 4
    first = below_ref.shape[0]
    here = pl.ds(pl.multiple_of(table_ref[slot] * slab, slab), slab)
    o_ref[...] = jnp.zeros_like(o_ref)
    o_ref[:first, :] = below_ref[...].astype(BF)
    for index in range(experts):
        at = first + index // 4
        o_ref[at : at + 1, index % 4 * slab : (index % 4 + 1) * slab] = early_ref[index : index + 1, here].astype(BF)
    at = first + experts // 4
    o_ref[at : at + 1, :] = early_ref[experts : experts + 1, :].astype(BF)
    o_ref[at + 1 : at + 3, :] = late_ref[...].astype(BF)


def pack_gains(table, below, early, late, slot, experts):
    height = below.shape[0] + -(-(experts // 4 + 3) // 16) * 16
    out = jax.ShapeDtypeStruct((height, early.shape[1]), BF)
    return small_call(pack_kernel, "pack_gains", out, table, below, early, late, slot=slot, experts=experts)


def unpack_kernel(table_ref, *refs, back, experts):
    *pieces, router_ref, gains_ref, all_ref = refs
    height = all_ref.shape[1]
    for index, piece in enumerate(pieces):
        all_ref[index] = piece[piece.shape[0] - height :, :].astype(F32)
    total = all_ref[table_ref[back]]
    for place in range(1, len(pieces)):
        total = total + all_ref[table_ref[back + place]]
    slab = total.shape[1] // 4
    rows = [total[i // 4 : i // 4 + 1, i % 4 * slab : (i % 4 + 1) * slab] for i in range(experts)]
    router_ref[...] = jnp.concatenate(rows, axis=0).T
    gains_ref[...] = total[experts // 4 : experts // 4 + 3, :]


def unpack_gains(table, pieces, back, experts, height):
    width = pieces[0].shape[1]
    out = [jax.ShapeDtypeStruct((width // 4, experts), F32), jax.ShapeDtypeStruct((3, width), F32)]
    scratch = [pltpu.VMEM((len(pieces), height, width), F32)]
    return small_call(
        unpack_kernel, "unpack_gains", out, table, *pieces, scratch=scratch, back=back, experts=experts
    )


def spread_kernel(table_ref, *refs, count, outs, cuts):
    pieces = refs[:count]
    out_refs = refs[-2 - outs : -2]
    wide_ref, sems = refs[-2:]
    copies = []
    for index, (number, rows, columns, out, slot, by_rows) in enumerate(cuts):
        wide_ref[index] = pieces[number][rows[0] : rows[1], columns[0] : columns[1]].astype(F32)
        size = rows[1] - rows[0] if by_rows else columns[1] - columns[0]
        here = pl.ds(pl.multiple_of(table_ref[slot] * size, size), size)
        to = out_refs[out].at[here, :] if by_rows else out_refs[out].at[:, here]
        copies.append(pltpu.make_async_copy(wide_ref.at[index], to, sems.at[index]))
        copies[-1].start()
    for copy in copies:
        copy.wait()


def spread(table, pieces, cuts, shape, outs, before):
    vmem, anywhere = pl.BlockSpec(memory_space=pltpu.VMEM), pl.BlockSpec(memory_space=pl.ANY)
    old = [] if before is None else list(before)
    _unused, rows, columns, *_rest = cuts[0]
    return pl.pallas_call(
        functools.partial(spread_kernel, count=len(pieces), outs=outs, cuts=cuts),
        in_specs=[pl.BlockSpec(memory_space=pltpu.SMEM)] + [vmem] * len(pieces) + [anywhere] * len(old),
        out_specs=[anywhere] * outs,
        out_shape=[jax.ShapeDtypeStruct(shape, F32)] * outs,
        input_output_aliases={1 + len(pieces) + index: index for index in range(len(old))},
        scratch_shapes=[
            pltpu.VMEM((len(cuts), rows[1] - rows[0], columns[1] - columns[0]), F32),
            pltpu.SemaphoreType.DMA((len(cuts),)),
        ],
        compiler_params=pltpu.CompilerParams(vmem_limit_bytes=24 * 2**20),
        cost_estimate=SMALL,
        name="spread",
    )(table, *pieces, *old)


def merge_kernel(w_ref, o_ref):
    units = w_ref.shape[2]
    for index in range(w_ref.shape[1]):
        o_ref[:, index * units : (index + 1) * units] = w_ref[:, index, :]


def merge_experts(weight):
    rows, count, units = weight.shape
    at_once = 128
    return pl.pallas_call(
        merge_kernel,
        grid=(rows // at_once,),
        in_specs=[pl.BlockSpec((at_once, count, units), lambda m: (m, 0, 0))],
        out_specs=pl.BlockSpec((at_once, count * units), lambda m: (m, 0)),
        out_shape=jax.ShapeDtypeStruct((rows, count * units), weight.dtype),
        cost_estimate=MEDIUM,
        name="merge_experts",
    )(weight)


def split_kernel(*refs):
    *term_refs, o_ref = refs
    units = o_ref.shape[2]
    for index in range(o_ref.shape[1]):
        here = slice(index * units, (index + 1) * units)
        total = term_refs[0][:, here].astype(F32)
        for term_ref in term_refs[1:]:
            total = total + term_ref[:, here].astype(F32)
        o_ref[:, index, :] = total


def split_experts(count, rows, *terms):
    columns = terms[0][0].shape[1]
    at_once = 128
    steps = rows // at_once

    def spec(at):
        return pl.BlockSpec((at_once, columns), lambda m: (at * steps + m, 0))

    return pl.pallas_call(
        split_kernel,
        grid=(steps,),
        in_specs=[spec(at) for _unused, at in terms],
        out_specs=pl.BlockSpec((at_once, count, columns // count), lambda m: (m, 0, 0)),
        out_shape=jax.ShapeDtypeStruct((rows, count, columns // count), F32),
        cost_estimate=SMALL,
        name="split_experts",
    )(*[array for array, _unused in terms])


def swap(v, mask):
    size = lax.axis_size("fsdp")
    return lax.ppermute(v, "fsdp", [(i, i ^ mask) for i in range(size)])


def ring_order(size):
    if size == 8:
        return [0, 2, 4, 6, 7, 5, 3, 1]
    return list(range(size))


def ring_send(v, direction):
    order = ring_order(lax.axis_size("ctx"))
    size = len(order)
    return lax.ppermute(v, "ctx", [(order[i], order[(i + direction) % size]) for i in range(size)])


class Flight(tuple):
    def noted(self, note):
        self.note = note
        return self


class Ring:
    def __init__(self, in_order, steps):
        self.in_order, self.steps, self.value, self.landed = in_order, steps, None, None
        self.flying = next(steps)

    def land(self):
        land(self.in_order, (self,))

    def step(self):
        if self.flying is None:
            return
        self.land()
        try:
            self.flying = self.steps.send(self.landed)
        except StopIteration as end:
            self.flying, self.value = None, end.value
        self.landed = None

    def finish(self):
        while self.flying is not None:
            self.step()
        return self.value


def land(in_order, rings, *more):
    rings = [ring for ring in rings if ring.flying is not None and ring.landed is None]
    found = [v for ring in rings for v in ring.flying] + list(more)
    if not found:
        return more
    found = in_order(*found) if len(found) > 1 else [in_order(*found)]
    for ring in rings:
        ring.landed, found = found[: len(ring.flying)], found[len(ring.flying) :]
        if isinstance(ring.flying, Flight):
            ring.flying.note(*ring.landed)
    return found


def ring_gather(v, in_order, found):
    size = lax.axis_size("ctx")
    far, half = size // 2, v.shape[0] // 2
    found[0] = v
    right, left = v, v
    for step in range(1, far):
        right, left = after((right, left), in_order.last)

        def note(right, left, step=step):
            found[size - step], found[step] = right, left

        right, left = yield Flight((ring_send(right, 1), ring_send(left, -1))).noted(note)

    def note_far(right, left):
        found[far] = jnp.concatenate([right, left])

    yield Flight((ring_send(right[:half], 1), ring_send(left[half:], -1))).noted(note_far)
    return found


def ring_scatter(term):
    size = lax.axis_size("ctx")
    far = size // 2
    first = term(far)
    half = first.shape[0] // 2
    right, left = yield (ring_send(first[:half].astype(BF), 1), ring_send(first[half:].astype(BF), -1))
    for offset in range(far - 1, 0, -1):
        ahead, behind = term(offset), term(size - offset)
        if offset == far - 1:
            ahead = jnp.concatenate([ahead[:half].astype(F32) + right.astype(F32), ahead[half:].astype(F32)])
            behind = jnp.concatenate([behind[:half].astype(F32), behind[half:].astype(F32) + left.astype(F32)])
        else:
            ahead, behind = ahead.astype(F32) + right.astype(F32), behind.astype(F32) + left.astype(F32)
        right, left = yield (ring_send(ahead.astype(BF), 1), ring_send(behind.astype(BF), -1))
    return term(0).astype(F32) + right.astype(F32) + left.astype(F32)


def after(v, *others):
    return lax.optimization_barrier((v, *others))[0]


class Order:
    def __init__(self, first):
        self.last = first

    def __call__(self, *values):
        self.last, *values = lax.optimization_barrier((self.last, *values))
        return values[0] if len(values) == 1 else values


def sum_fsdp(v):
    size = lax.axis_size("fsdp")
    mask = 1
    while mask < size:
        (other,) = yield (swap(v, mask),)
        v = v + other
        mask *= 2
    return v


def body(
    tokens, attn_gain, w_query, w_key, w_value, query_gain, key_gain, w_out,
    ffn_gain, w_router, w_gate, w_up, w_down, routes, cotangent,
):
    ctx_size = lax.axis_size("ctx")
    parts = lax.axis_size("fsdp")
    rows = tokens.shape[1]
    width = tokens.shape[2]
    slab = w_query.shape[0]
    head_dim = query_gain.shape[0]
    own_heads = width // head_dim // parts
    own_width = own_heads * head_dim
    own_rows = slab // ctx_size
    own_experts = w_gate.shape[1]
    hidden_units = w_gate.shape[2]
    experts = own_experts * ctx_size
    seq_length = rows * ctx_size
    in_order = Order(jnp.zeros((), F32))

    heads = 2 * own_heads
    repeats = ctx_size // heads
    order = ring_order(ctx_size)
    offsets = [0] + [o for step in range(1, ctx_size // 2) for o in (step, ctx_size - step)] + [ctx_size // 2]
    at_ring, at_place, at_core, at_side = 0, 1, 2, 3
    at_slab = [4 + mask for mask in range(parts)]
    at_groups, at_beside, at_chip = (8, 9), (10, 11), (12, 13, 14, 15)
    at_order = (16, 17, 18, 19)
    at_from = 20
    at_blocks = [at_from + ctx_size + index for index in range(ctx_size)]
    at_heads = [(at_from + 2 * ctx_size + index, at_from + 3 * ctx_size + index) for index in range(ctx_size)]
    at_turn = at_from + 4 * ctx_size
    at_back = at_from + 5 * ctx_size
    lines = []
    for place in range(ctx_size):
        ring_place = order.index(place)
        for mine in range(parts):
            side, core = divmod(mine, 2)
            line = [ring_place, place, core, side] + [mine ^ mask for mask in range(parts)]
            line += [core, core + 2, 1 - core, 3 - core, 2 * side, 2 * side + 1, 2 - 2 * side, 3 - 2 * side]
            line += [mine ^ 1, mine ^ 3, mine ^ 2, mine]
            places = [order[(ring_place + offset) % ctx_size] for offset in offsets]
            line += places
            line += [(ring_place + offset) % ctx_size for offset in offsets]
            for first in (core, 1 - core):
                line += [first * own_heads + other // repeats + other // repeats // own_heads * own_heads for other in places]
            line += [(ring_place + index) % ctx_size for index in range(ctx_size)]
            line += [offsets.index((order.index(other) - ring_place) % ctx_size) for other in range(ctx_size)]
            lines.append(line)
    device = lax.axis_index("ctx").astype(jnp.uint32) * parts + lax.axis_index("fsdp").astype(jnp.uint32)
    table = lax.dynamic_slice(jnp.asarray(np.array(lines, np.int32)), (device, jnp.uint32(0)), (1, len(lines[0])))
    table = table.reshape(-1)

    def spread_pairs(v):
        if repeats > 1:
            v = jnp.repeat(v, repeats, axis=0)
        return lax.all_to_all(v, "ctx", split_axis=0, concat_axis=0, tiled=True)

    def collect_pairs(v):
        v = lax.all_to_all(v, "ctx", split_axis=0, concat_axis=0, tiled=True)
        return v[::repeats] if repeats > 1 else v

    projections = (w_query, w_key, w_value)

    def side_of(row, rows, slots):
        return row, rows, [(number, slot, own_width) for number in range(3) for slot in slots]

    row, rows_of, some = side_of(at_ring, own_rows, at_groups)
    fetched = in_order(
        *take_parts(
            table, (*projections, w_out), [(row, rows_of, some + [(3, None, width)]), side_of(row, rows_of, at_beside)], SMALL
        )
    )
    fetched = swap(fetched[0], 2), swap(fetched[1], 3)
    cot_blocks = {}
    cot_ring = Ring(in_order, ring_gather(after(cotangent[0], in_order.last), in_order, cot_blocks))
    source = tokens[0].astype(F32)
    factor_one = lax.rsqrt(jnp.mean(source * source, axis=-1, keepdims=True) + EPSILON)
    normed = (source * factor_one * attn_gain).astype(BF)
    projections, w_down, w_gate, w_up = after((projections, w_down, w_gate, w_up), in_order.last)
    near, own, normed = in_order(
        *take_parts(
            table, projections, [side_of(None, slab, at_beside), side_of(None, slab, at_groups)], MEDIUM
        ),
        normed,
    )
    cot_ring.step()
    beside, near = swap(normed, 1), swap(near, 1)
    w_down = in_order(merge_experts(after(w_down, in_order.last)))
    cot_ring.land()
    fetched = in_order(*fetched)
    column_blocks = {}
    ring = Ring(in_order, ring_gather(fetched_payload(table, *fetched, width), in_order, column_blocks))
    down_w = lax.all_gather(after(w_down, in_order.last), "fsdp", axis=0, tiled=True)
    w_gate = in_order(merge_experts(after(w_gate, in_order.last)))
    ring.step()
    gate_w = lax.all_gather(after(w_gate, in_order.last), "fsdp", axis=0, tiled=True)
    w_router, routes = after((w_router, routes), in_order.last)
    router = [w_router, swap(w_router, 1), swap(w_router, 2), swap(w_router, 3)]
    routes_all = lax.all_to_all(
        jnp.broadcast_to(routes, (ctx_size, *routes.shape[1:])), "ctx", split_axis=0, concat_axis=0, tiled=True
    )
    normed, near, beside = in_order(normed, near, beside)
    w_up = in_order(merge_experts(after(w_up, in_order.last)))
    ring.step()
    up_w = lax.all_gather(after(w_up, in_order.last), "fsdp", axis=0, tiled=True)
    routes_all, *router = in_order(routes_all, *router)
    ring.step()

    half = head_dim // 2
    frequency = ROPE_BASE ** (-jnp.arange(half, dtype=F32) * 2.0 / head_dim)
    angles = jnp.arange(seq_length, dtype=jnp.int32).astype(F32)[:, None] * frequency[None, :]
    cosine, sine = jnp.cos(angles), jnp.sin(angles)
    cosine = jnp.concatenate([cosine, cosine], axis=1)
    sine = jnp.concatenate([-sine, sine], axis=1)
    q_gain, k_gain = query_gain[None, :], key_gain[None, :]

    ring.finish()
    qkv, own_columns = own_pairs(
        table,
        (normed, beside),
        own,
        near,
        [column_blocks[offset] for offset in offsets],
        3,
        head_dim,
        at_slab,
        at_blocks,
    )
    qkv = spread_pairs(in_order(qkv))
    router_w = in_order(place_rows(table, after(router, in_order.last), at_slab))
    w_far = in_order(far_rows(table, [column_blocks[offset] for offset in offsets], at_blocks))
    qkv = in_order(qkv)
    down_w, gate_w = in_order(down_w, gate_w)
    mixed = in_order(attend(qkv, q_gain, k_gain, cosine, sine))
    mixed = in_order(collect_pairs(mixed))
    hidden, far = in_order(*mixed_out(table, mixed, w_out, w_far, at_side))
    far = swap(far, 1)
    hidden = in_order(source + hidden)
    hidden = hidden + in_order(far).astype(F32)
    up_w = in_order(up_w)
    factor_two = lax.rsqrt(jnp.mean(hidden * hidden, axis=-1, keepdims=True) + EPSILON)
    ffn_in = in_order((hidden * factor_two * ffn_gain).astype(BF))

    ffn_blocks = {}
    ffn_ring = Ring(in_order, ring_gather(ffn_in, in_order, ffn_blocks))
    ffn_ring.step()

    size = 4
    groups = [offsets[first : first + size] for first in range(0, ctx_size, size)]

    def group_cots(group):
        return in_order(*stacked_matmul([cot_blocks[o] for o in groups[group]], down_w))

    def group_units(group, grad_act):
        return in_order(
            *expert_units(
                table, at_place, at_from + group * size, [ffn_blocks[o] for o in groups[group]], routes_all, router_w,
                gate_w, up_w, grad_act, own_experts,
            )
        )

    cots = [group_cots(0)]
    ffn_ring.step()
    cot_ring.step()
    units = [group_units(0, cots[0][0])]
    ffn_ring.step()
    cot_ring.step()
    other_side = (1 - table[at_side]).astype(jnp.uint32) * own_heads
    zero = jnp.uint32(0)
    other_mixed = lax.dynamic_slice(
        after(mixed, in_order.last), (other_side, zero, zero, zero), (own_heads, *mixed.shape[1:])
    )
    other_mixed = swap(other_mixed, 2)
    cot_ring.finish()
    ffn_ring.finish()
    normed_blocks = {}
    normed_ring = Ring(in_order, ring_gather(after(normed, in_order.last), in_order, normed_blocks))
    for group in range(1, len(groups)):
        cots.append(group_cots(group))
        if group == 1:
            normed_ring.step()
        units.append(group_units(group, cots[group][0]))
    cots = [part for _unused, part in cots]
    acts, gate_grads, up_grads, d_gates, inputs = zip(*units)

    def term_of(terms):
        def term(offset):
            group, index = divmod(offsets.index(offset), size)
            return terms[group][index * rows : (index + 1) * rows]

        return term

    def weight_grad(lefts, rights):
        lefts, rights = after((lefts, rights), in_order.last)
        return in_order(sum_of_outer(table, lefts, rights))

    def share(grad):
        return lax.psum_scatter(after(grad, in_order.last), "fsdp", scatter_dimension=0, tiled=True)

    grad_rows = {}

    def make_rows(group):
        some = after((gate_grads[group], up_grads[group]), in_order.last)
        grad_rows[group] = in_order(expert_rows(*some, gate_w, up_w))

    other_mixed = in_order(other_mixed)
    normed_ring.step()
    for group in range(len(groups) - 1, 0, -1):
        make_rows(group)
    normed_ring.step()
    row_ring = Ring(in_order, ring_scatter(term_of(grad_rows)))
    d_gate = weight_grad(inputs, gate_grads)
    row_ring.step()
    d_gate = share(d_gate)
    normed_ring.finish()
    make_rows(0)
    row_ring.step()
    weighted = in_order(*times_transpose(after(acts, in_order.last), down_w))
    row_ring.step()
    ring = Ring(in_order, ring_scatter(term_of(weighted)))
    d_gates = jnp.concatenate(after(d_gates, in_order.last), axis=1).reshape(own_experts, ctx_size, rows)
    d_gates = d_gates.at[:, table[at_back : at_back + ctx_size], :].get(mode="promise_in_bounds").transpose(1, 0, 2)
    d_gates = lax.all_to_all(d_gates, "ctx", split_axis=0, concat_axis=0, tiled=True)
    some = after(tuple(normed_blocks[offset] for offset in offsets), in_order.last)
    normed_t = in_order(transposed(table, some, at_chip))
    land(in_order, (row_ring, ring))
    d_gates = in_order(d_gates).reshape(experts, rows).T
    beside_t = swap(normed_t, 1)
    gates = routed_gates(dot(ffn_in, router_w), routes[0])
    grad_logits = gates * (d_gates - jnp.sum(gates * d_gates, axis=-1, keepdims=True))
    routed = dot(grad_logits, router_w.astype(F32), ((1,), (1,)), precision=lax.Precision.HIGHEST)
    routed = in_order(routed)
    grad_ffn_in = row_ring.finish() + routed

    inner = grad_ffn_in * ffn_gain
    grad_hidden = (
        cotangent[0].astype(F32)
        + factor_two * inner
        - hidden * (factor_two * factor_two * factor_two) * jnp.mean(inner * hidden, axis=-1, keepdims=True)
    )
    grad_proj, grad_hidden, grad_ffn_in = in_order(grad_hidden.astype(BF), grad_hidden, grad_ffn_in)

    beside = swap(grad_proj, 1)
    grad_proj, beside, beside_t = in_order(grad_proj, beside, beside_t)
    grad_mixed = in_order(grad_pairs(table, grad_proj, beside, w_out, w_far, at_side, head_dim))
    across = swap(after(grad_proj, in_order.last), 2)
    ring.step()
    grad_mixed = spread_pairs(grad_mixed)
    d_up = weight_grad(inputs, up_grads)
    (grad_mixed,) = land(in_order, (ring,), grad_mixed)
    d_up = share(d_up)
    ring.step()
    grads, head_gains = in_order(
        *attend_back(qkv, after(grad_mixed, in_order.last), q_gain, k_gain, cosine, sine)
    )
    if repeats > 1:
        head_gains = jnp.where(lax.axis_index("ctx") % repeats == 0, head_gains, 0.0)
    across = in_order(across)
    diagonal = swap(across, 1)
    ring.land()

    grads = after(grads, in_order.last)
    ring.step()
    half_grads = in_order(head_weights(table, grads, normed_t, beside_t, 3, at_from))
    other_half = swap(half_grads[width // 2 :], 2)
    grads = collect_pairs(after(grads, in_order.last))
    mixed, diagonal = after((mixed, diagonal), in_order.last)
    d_out = in_order(
        out_grads(table, mixed, other_mixed, [grad_proj, beside, across, diagonal], at_turn, own_rows, at_side)
    )
    other_half = in_order(other_half)
    keep, send = in_order(*chip_total(table, half_grads, other_half, at_core))
    send = in_order(swap(send, 1))
    pieces = {}
    total_ring = Ring(in_order, ring_gather(side_by_side(table, keep, send), in_order, pieces))
    out_ring = Ring(in_order, ring_scatter(lambda offset: d_out[offset * own_rows : (offset + 1) * own_rows]))
    d_down = weight_grad(cots, acts)
    output = in_order((hidden + ring.finish()).astype(BF))
    grads = in_order(grads)
    total_ring.step()
    d_down = share(d_down)
    out_ring.step()
    grads, grad_ffn_in, grad_logits = after((grads, grad_ffn_in, grad_logits), in_order.last)
    own, far = in_order(*pair_normed(grads, own_columns, 3))
    far = swap(far, 1)
    d_ffn_gain = jnp.sum(grad_ffn_in * hidden * factor_two, axis=0, keepdims=True)
    d_router = dot(grad_logits, ffn_in.astype(F32), ((0,), (0,)), precision=lax.Precision.HIGHEST)
    early = in_order(jnp.concatenate([d_router, d_ffn_gain]))
    early = Ring(in_order, sum_fsdp(early))
    out_ring.step()
    total_ring.step()

    whole = None
    seen = set()

    def take_whole(arrays):
        new = [index for index, offset in enumerate(offsets) if offset in pieces and index not in seen]
        seen.update(new)
        high = pieces[offsets[0]].shape[0]
        for first in range(0, len(new), 4):
            some = new[first : first + 4]
            cuts = []
            for number, index in enumerate(some):
                for where in range(2):
                    for kind in range(3):
                        at = (where * 3 + kind) * head_dim
                        cuts.append((number, (0, high), (at, at + head_dim), kind, at_heads[index][where], False))
            found = [pieces[offsets[index]] for index in some]
            arrays = in_order(*spread(table, found, cuts, (slab, width), 3, arrays))
        return arrays

    whole = take_whole(whole)
    early.step()
    grad_normed = own + in_order(far).astype(F32)
    d_attn_gain = jnp.sum(grad_normed * source * factor_one, axis=0)
    inner = grad_normed * attn_gain
    d_tokens = (
        grad_hidden
        + factor_one * inner
        - source * (factor_one * factor_one * factor_one) * jnp.mean(inner * source, axis=-1, keepdims=True)
    )
    d_tokens, d_attn_gain = in_order(d_tokens, d_attn_gain)
    late = jnp.concatenate([d_attn_gain, head_gains[0], head_gains[1], jnp.zeros((width - 2 * head_dim,), F32)])
    late = Ring(in_order, sum_fsdp(late.reshape(2, width)))
    out_ring.step()
    early.finish()
    d_gate = in_order(split_experts(own_experts, slab, (after(d_gate, in_order.last), 0)))
    late.step()
    total_ring.step()
    d_out = out_ring.finish()
    whole = take_whole(whole)
    packed = in_order(pack_gains(table, d_out, early.value, late.finish(), at_slab[0], experts))
    packed_pieces = {}
    packed_ring = Ring(in_order, ring_gather(packed, in_order, packed_pieces))
    d_up = in_order(split_experts(own_experts, slab, (after(d_up, in_order.last), 0)))
    total_ring.finish()
    whole = take_whole(whole)
    d_query, d_key, d_value = whole
    packed_ring.step()
    packed_ring.step()
    d_down = in_order(split_experts(own_experts, slab, (after(d_down, in_order.last), 0)))
    packed_ring.finish()
    packed_blocks = [packed_pieces[offset] for offset in offsets]
    cuts = [(index, (0, own_rows), (0, width), 0, at_blocks[index], True) for index in range(ctx_size)]
    (d_out,) = spread(table, packed_blocks, cuts, (slab, width), 1, None)
    height = packed.shape[0] - own_rows
    d_router, gains = unpack_gains(table, packed_blocks, at_back, experts, height)
    d_ffn_gain, d_attn_gain, head_gains = gains + in_order.last
    return (
        output[None],
        d_tokens[None],
        d_attn_gain,
        d_query,
        d_key,
        d_value,
        head_gains[:head_dim],
        head_gains[head_dim : 2 * head_dim],
        d_out,
        d_ffn_gain,
        d_router,
        d_gate,
        d_up,
        d_down,
    )


def solution(mesh):
    token_split = P("fsdp", "ctx", None)
    row_split = P("fsdp", None)
    return jax.shard_map(
        body,
        mesh=mesh,
        in_specs=(
            token_split, P(), row_split, row_split, row_split, P(), P(), row_split,
            P(), row_split, token_split, token_split, token_split, token_split, token_split,
        ),
        out_specs=(
            token_split, token_split, P(), row_split, row_split, row_split, P(), P(),
            row_split, P(), row_split, token_split, token_split, token_split,
        ),
        check_vma=False,
    )
```

```python
import functools

import jax
import jax.numpy as jnp
import numpy as np
from jax import lax
from jax.experimental import pallas as pl
from jax.experimental.pallas import tpu as pltpu
from jax.sharding import PartitionSpec as P

EPSILON = 1e-06
ROPE_BASE = 10000.0
BF = jnp.bfloat16
F32 = jnp.float32
LONG = pl.CostEstimate(flops=10**12, bytes_accessed=10**9, transcendentals=0)
MEDIUM = pl.CostEstimate(flops=2 * 10**10, bytes_accessed=5 * 10**7, transcendentals=0)
SMALL = pl.CostEstimate(flops=1, bytes_accessed=1, transcendentals=0)


def dot(a, b, contract=((1,), (0,)), precision=None):
    return lax.dot_general(a, b, (contract, ((), ())), precision=precision, preferred_element_type=F32)


def dot_nt(a, b):
    return dot(a, b, ((1,), (1,)))


def dot_tn(a, b):
    return dot(a, b, ((0,), (0,)))


def head_norm(v, gain):
    factor = lax.rsqrt(jnp.mean(v * v, axis=-1, keepdims=True) + EPSILON)
    return v * factor * gain, factor


def turn(v, cosine, sine):
    return v * cosine + pltpu.roll(v, v.shape[-1] // 2, 1) * sine


def head_back(grad, v, gain, cosine, sine):
    grad = turn(grad, cosine, -sine)
    factor = lax.rsqrt(jnp.mean(v * v, axis=-1, keepdims=True) + EPSILON)
    gain_grad = jnp.sum(grad * v * factor, axis=0, keepdims=True)
    inner = grad * gain
    return factor * inner - v * (factor * factor * factor) * jnp.mean(inner * v, axis=-1, keepdims=True), gain_grad


def rows_of(ref):
    block = ref[...]
    return block.reshape(-1, block.shape[-1])


def attend_kernel(q_ref, k_ref, v_ref, qg_ref, kg_ref, cos_ref, sin_ref, o_ref, keys, values_t):
    step = pl.program_id(1)

    @pl.when(step == 0)
    def _():
        normed, _unused = head_norm(rows_of(k_ref).astype(F32), kg_ref[...])
        keys[...] = turn(normed, cos_ref[...], sin_ref[...]).astype(BF)
        values_t[...] = rows_of(v_ref).astype(F32).T.astype(BF)

    queries = rows_of(q_ref).astype(F32)
    number, head_dim = queries.shape
    here = pl.ds(pl.multiple_of(step * number, number), number)
    normed, _unused = head_norm(queries, qg_ref[...])
    queries = turn(normed, cos_ref[here, :], sin_ref[here, :]).astype(BF)
    weights = jnp.exp(dot_nt(keys[...], queries) * (head_dim**-0.5))
    total = jnp.sum(weights, axis=0, keepdims=True)
    mixed = dot(values_t[...], weights.astype(BF)) / total
    o_ref[...] = mixed.T.astype(BF).reshape(o_ref.shape)


def attend_back_kernel(
    q_ref, k_ref, v_ref, m_ref, qg_ref, kg_ref, cos_ref, sin_ref,
    g_ref, gain_ref, keys, keys_t, key_acc, value_acc,
):
    pair = pl.program_id(0)
    step = pl.program_id(1)
    last = pl.num_programs(1) - 1

    @pl.when((pair == 0) & (step == 0))
    def _():
        gain_ref[...] = jnp.zeros_like(gain_ref)

    @pl.when(step == 0)
    def _():
        normed, _unused = head_norm(rows_of(k_ref).astype(F32), kg_ref[...])
        turned = turn(normed, cos_ref[...], sin_ref[...])
        keys[...] = turned.astype(BF)
        keys_t[...] = turned.T.astype(BF)
        key_acc[...] = jnp.zeros_like(key_acc)
        value_acc[...] = jnp.zeros_like(value_acc)

    query_pre = rows_of(q_ref).astype(F32)
    grad_mixed = rows_of(m_ref)
    number, head_dim = query_pre.shape
    scale = head_dim**-0.5
    here = pl.ds(pl.multiple_of(step * number, number), number)
    cosine, sine = cos_ref[here, :], sin_ref[here, :]
    normed, _unused = head_norm(query_pre, qg_ref[...])
    queries = turn(normed, cosine, sine).astype(BF)
    weights = jnp.exp(dot_nt(keys[...], queries) * scale)
    probs = weights * (1.0 / jnp.sum(weights, axis=0, keepdims=True))
    value_acc[...] += dot(probs.astype(BF), grad_mixed)
    weighted = probs * dot_nt(rows_of(v_ref), grad_mixed)
    delta = jnp.sum(weighted, axis=0, keepdims=True)
    grad_scores = (weighted - probs * delta).astype(BF)
    key_acc[...] += dot(grad_scores, queries)
    grad_query = dot(keys_t[...], grad_scores).T * scale
    grad_query, gain_grad = head_back(grad_query, query_pre, qg_ref[...], cosine, sine)
    rows = g_ref.shape[2]
    blocks = number // rows
    g_ref[pl.ds(step * blocks, blocks), 0] = grad_query.astype(BF).reshape(blocks, rows, head_dim)
    gain_ref[0:1, :] += gain_grad

    @pl.when(step == last)
    def _():
        grad_key, gain_grad = head_back(
            key_acc[...] * scale, rows_of(k_ref).astype(F32), kg_ref[...], cos_ref[...], sin_ref[...]
        )
        g_ref[:, 1] = grad_key.astype(BF).reshape(-1, rows, head_dim)
        g_ref[:, 2] = value_acc[...].astype(BF).reshape(-1, rows, head_dim)
        gain_ref[1:2, :] += gain_grad


def attention_specs(shape):
    blocks, pairs, rows, head_dim = shape
    at_once = max(1, 256 // rows)
    while blocks % at_once:
        at_once -= 1
    pairs //= 3
    part = pl.BlockSpec((at_once, 1, rows, head_dim), lambda p, i: (i, p, 0, 0))
    three = [
        pl.BlockSpec((at_once, 1, rows, head_dim), lambda p, i: (i, 3 * p, 0, 0)),
        pl.BlockSpec((blocks, 1, rows, head_dim), lambda p, i: (0, 3 * p + 1, 0, 0)),
        pl.BlockSpec((blocks, 1, rows, head_dim), lambda p, i: (0, 3 * p + 2, 0, 0)),
    ]
    gain = pl.BlockSpec((1, head_dim), lambda p, i: (0, 0))
    table = pl.BlockSpec((blocks * rows, head_dim), lambda p, i: (0, 0))
    params = pltpu.CompilerParams(
        dimension_semantics=("arbitrary", "arbitrary"),
        vmem_limit_bytes=(24 if blocks * rows <= 1024 else 56) * 2**20,
    )
    return part, three, gain, table, (pairs, blocks // at_once), params


def attend(qkv, query_gain, key_gain, cosine, sine):
    part, three, gain, table, grid, params = attention_specs(qkv.shape)
    blocks, _unused, rows, head_dim = qkv.shape
    length = blocks * rows
    return pl.pallas_call(
        attend_kernel,
        grid=grid,
        in_specs=[*three, gain, gain, table, table],
        out_specs=part,
        out_shape=jax.ShapeDtypeStruct((blocks, grid[0], rows, head_dim), BF),
        scratch_shapes=[pltpu.VMEM((length, head_dim), BF), pltpu.VMEM((head_dim, length), BF)],
        compiler_params=params,
        cost_estimate=MEDIUM,
        name="attend",
    )(qkv, qkv, qkv, query_gain, key_gain, cosine, sine)


def attend_back(qkv, grad_mixed, query_gain, key_gain, cosine, sine):
    part, three, gain, table, grid, params = attention_specs(qkv.shape)
    blocks, _unused, rows, head_dim = qkv.shape
    length = blocks * rows
    return pl.pallas_call(
        attend_back_kernel,
        grid=grid,
        in_specs=[*three, part, gain, gain, table, table],
        out_specs=[
            pl.BlockSpec((blocks, 3, rows, head_dim), lambda p, i: (0, p, 0, 0)),
            pl.BlockSpec((8, head_dim), lambda p, i: (0, 0)),
        ],
        out_shape=[jax.ShapeDtypeStruct(qkv.shape, BF), jax.ShapeDtypeStruct((8, head_dim), F32)],
        scratch_shapes=[
            pltpu.VMEM((length, head_dim), BF),
            pltpu.VMEM((head_dim, length), BF),
            pltpu.VMEM((length, head_dim), F32),
            pltpu.VMEM((length, head_dim), F32),
        ],
        compiler_params=params,
        cost_estimate=LONG,
        name="attend_back",
    )(qkv, qkv, qkv, grad_mixed, query_gain, key_gain, cosine, sine)


def stack_blocks(block_refs, out_ref):
    rows = block_refs[0].shape[0]
    for index, block_ref in enumerate(block_refs):
        out_ref[index * rows : (index + 1) * rows, :] = block_ref[...]


def stacked_kernel(w_ref, *refs):
    *block_refs, o_ref, rows_ref = refs

    @pl.when(pl.program_id(0) == 0)
    def _():
        stack_blocks(block_refs, rows_ref)

    o_ref[...] = dot(rows_ref[...], w_ref[...])


def stacked_matmul(blocks, weight):
    rows, depth = len(blocks) * blocks[0].shape[0], weight.shape[0]
    wide = min(512, weight.shape[1])
    return pl.pallas_call(
        stacked_kernel,
        grid=(weight.shape[1] // wide,),
        in_specs=[pl.BlockSpec((depth, wide), lambda n: (0, n))]
        + [pl.BlockSpec(block.shape, lambda n: (0, 0)) for block in blocks],
        out_specs=[pl.BlockSpec((rows, wide), lambda n: (0, n)), pl.BlockSpec((rows, depth), lambda n: (0, 0))],
        out_shape=[jax.ShapeDtypeStruct((rows, weight.shape[1]), F32), jax.ShapeDtypeStruct((rows, depth), BF)],
        compiler_params=pltpu.CompilerParams(dimension_semantics=("arbitrary",), vmem_limit_bytes=56 * 2**20),
        cost_estimate=LONG,
        name="stacked_matmul",
    )(weight, *blocks)


def routed_gates(logits, routes):
    columns = lax.broadcasted_iota(jnp.int32, logits.shape, 1)
    chosen = columns == routes[:, 0:1]
    for index in range(1, routes.shape[1]):
        chosen = chosen | (columns == routes[:, index : index + 1])
    high = jnp.max(jnp.where(chosen, logits, -1e30), axis=-1, keepdims=True)
    weights = jnp.where(chosen, jnp.exp(jnp.where(chosen, logits - high, 0.0)), 0.0)
    return weights / jnp.sum(weights, axis=-1, keepdims=True)


def expert_kernel(table_ref, router_ref, routes_ref, gate_w_ref, up_w_ref, grad_ref, *refs, per, place, at):
    *block_refs, act_ref, gate_ref, up_ref, d_gates_ref, x_ref, gates_ref = refs
    step = pl.program_id(0)

    @pl.when(step == 0)
    def _():
        stack_blocks(block_refs, x_ref)
        routes = jnp.concatenate([routes_ref[table_ref[at + index]] for index in range(len(block_refs))], axis=0)
        gates = routed_gates(dot(x_ref[...], router_ref[...]), routes)
        columns = lax.broadcasted_iota(jnp.int32, gates.shape, 1)
        count = gates_ref.shape[0]
        for index in range(count):
            here = columns == table_ref[place] * count + index
            gates_ref[index] = jnp.sum(jnp.where(here, gates, 0.0), axis=1, keepdims=True)

    @pl.when(step % per == 0)
    def _():
        d_gates_ref[...] = jnp.zeros_like(d_gates_ref)

    gate_pre = dot(x_ref[...], gate_w_ref[...])
    up_pre = dot(x_ref[...], up_w_ref[...])
    grad_act = grad_ref[...]
    gates = gates_ref[step // per]
    sigmoid = 1.0 / (1.0 + jnp.exp(-gate_pre))
    silu = gate_pre * sigmoid
    act = (silu * up_pre).astype(BF).astype(F32)
    d_gates_ref[0] += jnp.sum(act * grad_act, axis=1, keepdims=True)
    grad_act = grad_act * gates
    act_ref[...] = (act * gates).astype(BF)
    up_ref[...] = (grad_act * silu).astype(BF)
    gate_ref[...] = (grad_act * up_pre * (sigmoid * (1.0 + gate_pre * (1.0 - sigmoid)))).astype(BF)


def expert_units(table, place, at, blocks, routes, router_w, gate_w, up_w, grad_act, count):
    rows, width = len(blocks) * blocks[0].shape[0], blocks[0].shape[1]
    units = gate_w.shape[1]
    wide = min(512, units // count)
    per = units // wide // count
    weight = pl.BlockSpec((width, wide), lambda n: (0, n))
    tile = pl.BlockSpec((rows, wide), lambda n: (0, n))
    out = jax.ShapeDtypeStruct((rows, units), BF)
    return pl.pallas_call(
        functools.partial(expert_kernel, per=per, place=place, at=at),
        grid=(units // wide,),
        in_specs=[
            pl.BlockSpec(memory_space=pltpu.SMEM),
            pl.BlockSpec(router_w.shape, lambda n: (0, 0)),
            pl.BlockSpec(routes.shape, lambda n: (0, 0, 0)),
            weight,
            weight,
            tile,
        ]
        + [pl.BlockSpec(block.shape, lambda n: (0, 0)) for block in blocks],
        out_specs=[
            tile,
            tile,
            tile,
            pl.BlockSpec((1, rows, 1), lambda n: (n // per, 0, 0)),
            pl.BlockSpec((rows, width), lambda n: (0, 0)),
        ],
        out_shape=[
            out, out, out, jax.ShapeDtypeStruct((count, rows, 1), F32), jax.ShapeDtypeStruct((rows, width), BF),
        ],
        scratch_shapes=[pltpu.VMEM((count, rows, 1), F32)],
        compiler_params=pltpu.CompilerParams(dimension_semantics=("arbitrary",), vmem_limit_bytes=58 * 2**20),
        cost_estimate=MEDIUM,
        name="expert_units",
    )(table, router_w, routes, gate_w, up_w, grad_act, *blocks)


def expert_rows_kernel(gate_ref, up_ref, gate_w_ref, up_w_ref, o_ref):
    o_ref[...] = (dot_nt(gate_ref[...], gate_w_ref[...]) + dot_nt(up_ref[...], up_w_ref[...])).astype(BF)


def expert_rows(gate_grads, up_grads, gate_w, up_w):
    rows, units = gate_grads.shape
    width = gate_w.shape[0]
    wide = min(512, width)
    whole = pl.BlockSpec((rows, units), lambda n: (0, 0))
    weight = pl.BlockSpec((wide, units), lambda n: (n, 0))
    return pl.pallas_call(
        expert_rows_kernel,
        grid=(width // wide,),
        in_specs=[whole, whole, weight, weight],
        out_specs=pl.BlockSpec((rows, wide), lambda n: (0, n)),
        out_shape=jax.ShapeDtypeStruct((rows, width), BF),
        compiler_params=pltpu.CompilerParams(dimension_semantics=("arbitrary",), vmem_limit_bytes=56 * 2**20),
        cost_estimate=MEDIUM,
        name="expert_rows",
    )(gate_grads, up_grads, gate_w, up_w)


def times_kernel(b_ref, *refs):
    count = len(refs) // 2
    for a_ref, o_ref in zip(refs[:count], refs[count:]):
        o_ref[...] = dot_nt(a_ref[...], b_ref[...]).astype(o_ref.dtype)


def times_transpose(lefts, b):
    columns, depth = b.shape
    wide = min(512, columns)
    return pl.pallas_call(
        times_kernel,
        grid=(columns // wide,),
        in_specs=[pl.BlockSpec((wide, depth), lambda n: (n, 0))]
        + [pl.BlockSpec(left.shape, lambda n: (0, 0)) for left in lefts],
        out_specs=[pl.BlockSpec((left.shape[0], wide), lambda n: (0, n)) for left in lefts],
        out_shape=[jax.ShapeDtypeStruct((left.shape[0], columns), BF) for left in lefts],
        compiler_params=pltpu.CompilerParams(dimension_semantics=("arbitrary",), vmem_limit_bytes=58 * 2**20),
        cost_estimate=MEDIUM,
        name="times_transpose",
    )(b, *lefts)


def sum_kernel(_unused, *refs):
    *pair_refs, o_ref = refs
    count = len(pair_refs) // 2
    total = dot_tn(pair_refs[0][...], pair_refs[count][...])
    for index in range(1, count):
        total = total + dot_tn(pair_refs[index][...], pair_refs[count + index][...])
    o_ref[...] = total.astype(o_ref.dtype)


def sum_of_outer(table, lefts, rights, slots=None):
    whole = not isinstance(lefts, (list, tuple))
    count, depth = len(rights), rights[0].shape[0]
    rows, columns = (lefts if whole else lefts[0]).shape[1], rights[0].shape[1]
    tall, wide = 512, columns if count <= 2 else min(1024, columns)

    def left_spec(index):
        at = index if whole else 0
        if slots is None:
            return pl.BlockSpec((depth, tall), lambda n, m, t: (at, m))
        return pl.BlockSpec((depth, tall), lambda n, m, t: (at, t[slots[0] + m]))

    return pl.pallas_call(
        sum_kernel,
        grid_spec=pltpu.PrefetchScalarGridSpec(
            num_scalar_prefetch=1,
            grid=(columns // wide, rows // tall),
            in_specs=[left_spec(index) for index in range(count)]
            + [pl.BlockSpec((depth, wide), lambda n, m, t: (0, n)) for _unused in rights],
            out_specs=pl.BlockSpec((tall, wide), lambda n, m, t: (m, n)),
        ),
        out_shape=jax.ShapeDtypeStruct((rows, columns), BF),
        compiler_params=pltpu.CompilerParams(
            dimension_semantics=("arbitrary", "arbitrary"), vmem_limit_bytes=56 * 2**20
        ),
        cost_estimate=LONG,
        name="sum_of_outer",
    )(table, *([lefts] * count if whole else lefts), *rights)


def add_kernel(_unused, left_ref, right_ref, o_ref):
    o_ref[...] = (left_ref[...].astype(F32) + right_ref[...].astype(F32)).astype(BF)


def add_slabs(table, left, right, first, second):
    columns = left.shape[1]
    slab = left.shape[0] // 4
    tall = slab // 4

    def spec(at):
        return pl.BlockSpec((tall, columns), lambda m, t: (4 * at + m, 0))

    return pl.pallas_call(
        add_kernel,
        grid_spec=pltpu.PrefetchScalarGridSpec(
            num_scalar_prefetch=1, grid=(4,), in_specs=[spec(first), spec(second)], out_specs=spec(0)
        ),
        out_shape=jax.ShapeDtypeStruct((slab, columns), BF),
        cost_estimate=SMALL,
        name="add_slabs",
    )(table, left, right)


NN, NT = ((1,), (0,)), ((1,), (1,))


def small_call(kernel, name, out_shape, *operands, cost=SMALL, scratch=(), **kwargs):
    vmem = pl.BlockSpec(memory_space=pltpu.VMEM)
    return pl.pallas_call(
        functools.partial(kernel, **kwargs),
        in_specs=[pl.BlockSpec(memory_space=pltpu.SMEM)] + [vmem] * (len(operands) - 1),
        out_specs=jax.tree.map(lambda _unused: vmem, out_shape),
        out_shape=out_shape,
        scratch_shapes=list(scratch),
        compiler_params=pltpu.CompilerParams(vmem_limit_bytes=48 * 2**20),
        cost_estimate=cost,
        name=name,
    )(*operands)


def payload_kernel(_unused, a_ref, b_ref, o_ref):
    rows, width = b_ref.shape[0], o_ref.shape[1]
    columns = b_ref.shape[1]
    rest = columns - width
    o_ref[:rows, :] = a_ref[:, :width]
    o_ref[rows : 2 * rows, :] = b_ref[:, :width]
    o_ref[2 * rows : 3 * rows, :rest] = a_ref[:, width:columns]
    o_ref[2 * rows : 3 * rows, rest:] = b_ref[:, width:]
    o_ref[3 * rows :, :] = a_ref[:, columns:]


def fetched_payload(table, from_beyond, from_across, width):
    out = jax.ShapeDtypeStruct((4 * from_across.shape[0], width), BF)
    return small_call(payload_kernel, "fetched_payload", out, table, from_beyond, from_across)


def own_pairs_kernel(table_ref, *refs, blocks, kinds, slabs, ring_slots):
    block_refs, refs = refs[:blocks], refs[blocks:]
    own_ref, near_ref, *piece_refs = refs[:-5]
    o_ref, columns_out, columns_ref, rows_ref, sems = refs[-5:]
    head_step, kind = pl.program_id(0), pl.program_id(1)
    slab, columns = own_ref.shape
    width = piece_refs[0].shape[1]
    part = piece_refs[0].shape[0] // 4
    rest = columns - width
    back = pltpu.make_async_copy(columns_ref, columns_out, sems.at[2 + 4 * len(piece_refs)])

    @pl.when((head_step == 0) & (kind == 0))
    def _():
        def at(slot, ring_slot=None):
            start = table_ref[slot] * slab
            if ring_slot is None:
                return pl.ds(pl.multiple_of(start, slab), slab)
            return pl.ds(pl.multiple_of(start + table_ref[ring_slot] * part, part), part)

        pairs = [(own_ref, columns_ref.at[at(slabs[0]), :]), (near_ref, columns_ref.at[at(slabs[1]), :])]
        for ring_slot, piece in zip(ring_slots, piece_refs):
            for index in range(2):
                to = at(slabs[2 + index], ring_slot)
                pairs.append((piece.at[index * part : (index + 1) * part, :], columns_ref.at[to, :width]))
                some = piece.at[2 * part : 3 * part, index * rest : (index + 1) * rest]
                pairs.append((some, columns_ref.at[to, width:]))
        copies = [pltpu.make_async_copy(*pair, sems.at[index]) for index, pair in enumerate(pairs)]
        for copy in copies:
            copy.start()
        stack_blocks(block_refs, rows_ref)
        for copy in copies:
            copy.wait()
        back.start()

    rows, head_dim = o_ref.shape[2:]
    wide = o_ref.shape[0] * head_dim
    at_column = (kind * pl.num_programs(0) + head_step) * wide
    product = dot(rows_ref[...], columns_ref[:, pl.ds(pl.multiple_of(at_column, wide), wide)]).astype(BF)
    for head in range(o_ref.shape[0]):
        for block in range(blocks):
            piece = product[block * rows : (block + 1) * rows, head * head_dim : (head + 1) * head_dim]
            o_ref[head, block * kinds + kind] = piece

    @pl.when((head_step == pl.num_programs(0) - 1) & (kind == kinds - 1))
    def _():
        back.wait()


def own_pairs(table, blocks, own, near, pieces, kinds, head_dim, slabs, ring_slots):
    rows, depth = blocks[0].shape
    columns = own.shape[1]
    heads = columns // head_dim // kinds
    at_once = 2
    anywhere = pl.BlockSpec(memory_space=pl.ANY)
    return pl.pallas_call(
        functools.partial(
            own_pairs_kernel, blocks=len(blocks), kinds=kinds, slabs=slabs, ring_slots=ring_slots
        ),
        grid=(heads // at_once, kinds),
        in_specs=[pl.BlockSpec(memory_space=pltpu.SMEM)]
        + [pl.BlockSpec(block.shape, lambda h, k: (0, 0)) for block in blocks]
        + [anywhere] * (2 + len(pieces)),
        out_specs=[
            pl.BlockSpec((at_once, len(blocks) * kinds, rows, head_dim), lambda h, k: (h, 0, 0, 0)),
            anywhere,
        ],
        out_shape=[
            jax.ShapeDtypeStruct((heads, len(blocks) * kinds, rows, head_dim), BF),
            jax.ShapeDtypeStruct((depth, columns), BF),
        ],
        scratch_shapes=[
            pltpu.VMEM((depth, columns), BF),
            pltpu.VMEM((len(blocks) * rows, depth), BF),
            pltpu.SemaphoreType.DMA((3 + 4 * len(pieces),)),
        ],
        compiler_params=pltpu.CompilerParams(
            dimension_semantics=("arbitrary", "arbitrary"), vmem_limit_bytes=40 * 2**20
        ),
        cost_estimate=SMALL,
        name="own_pairs",
    )(table, *blocks, own, near, *pieces)


def far_rows_kernel(table_ref, *refs, ring_slots):
    *pieces, o_ref = refs
    part = pieces[0].shape[0] // 4
    for slot, piece in zip(ring_slots, pieces):
        o_ref[pl.ds(pl.multiple_of(table_ref[slot] * part, part), part), :] = piece[3 * part :, :]


def far_rows(table, pieces, ring_slots):
    rows, width = pieces[0].shape
    out = jax.ShapeDtypeStruct((rows // 4 * len(pieces), width), BF)
    return small_call(far_rows_kernel, "far_rows", out, table, *pieces, ring_slots=ring_slots)


def heads_of(ref, side, sequence, count):
    return [ref[side * count + head, sequence] for head in range(count)]


def mixed_out_kernel(table_ref, m_ref, w_ref, far_ref, *refs, side):
    count = m_ref.shape[0] // 2
    for sequence, ref in enumerate(refs):
        own = jnp.concatenate(heads_of(m_ref, table_ref[side], sequence, count), axis=1)
        far = jnp.concatenate(heads_of(m_ref, 1 - table_ref[side], sequence, count), axis=1)
        ref[...] = (dot(own, w_ref[...]) + dot(far, far_ref[...])).astype(ref.dtype)


def mixed_out(table, mixed, w_out, w_far, side):
    shape = (mixed.shape[2], w_out.shape[1])
    out = [jax.ShapeDtypeStruct(shape, kind) for kind in (F32, BF)]
    return small_call(mixed_out_kernel, "mixed_out", out, table, mixed, w_out, w_far, cost=MEDIUM, side=side)


def grad_pairs_kernel(table_ref, own_ref, beside_ref, w_ref, far_ref, o_ref, *, side):
    rows, head_dim = o_ref.shape[2:]
    count = o_ref.shape[0] // 2
    grads = jnp.concatenate([own_ref[...], beside_ref[...]], axis=0)
    for slab_ref, at in ((w_ref, table_ref[side]), (far_ref, 1 - table_ref[side])):
        product = dot_nt(grads, slab_ref[...]).astype(BF)
        for head in range(count):
            for sequence in range(2):
                piece = product[sequence * rows : (sequence + 1) * rows, head * head_dim : (head + 1) * head_dim]
                o_ref[at * count + head, sequence] = piece


def grad_pairs(table, own, beside, w_out, w_far, side, head_dim):
    out = jax.ShapeDtypeStruct((2 * w_out.shape[0] // head_dim, 2, own.shape[0], head_dim), BF)
    return small_call(
        grad_pairs_kernel, "grad_pairs", out, table, own, beside, w_out, w_far, cost=LONG, side=side
    )


def out_grads_kernel(table_ref, m_ref, other_ref, *refs, turn, own_rows, side):
    *block_refs, o_ref, mixed_ref, turned_ref, grads_ref = refs
    head_dim = m_ref.shape[3]
    count = m_ref.shape[0] // 2
    for head in range(count):
        rows = [m_ref[table_ref[side] * count + head, sequence] for sequence in range(2)]
        rows += [other_ref[head, sequence] for sequence in range(2)]
        rows = jnp.concatenate(rows, axis=0)
        mixed_ref[head * head_dim : (head + 1) * head_dim, :] = rows.astype(F32).T.astype(BF)
    for index in range(mixed_ref.shape[0] // own_rows):
        at = pl.multiple_of(table_ref[turn + index] * own_rows, own_rows)
        turned_ref[index * own_rows : (index + 1) * own_rows, :] = mixed_ref[pl.ds(at, own_rows), :]
    stack_blocks(block_refs, grads_ref)
    o_ref[...] = dot(turned_ref[...], grads_ref[...])


def out_grads(table, mixed, other, blocks, turn, own_rows, side):
    rows, width = blocks[0].shape
    features = mixed.shape[0] // 2 * mixed.shape[3]
    turned = pltpu.VMEM((features, len(blocks) * rows), BF)
    out = jax.ShapeDtypeStruct((features, width), F32)
    scratch = [turned, turned, pltpu.VMEM((len(blocks) * rows, width), BF)]
    return small_call(
        out_grads_kernel, "out_grads", out, table, mixed, other, *blocks, cost=LONG, scratch=scratch, turn=turn,
        own_rows=own_rows, side=side,
    )


def transposed_kernel(table_ref, *refs, slots):
    *block_refs, o_ref = refs
    rows, width = block_refs[0].shape
    slab = width // len(slots)
    for index, block_ref in enumerate(block_refs):
        for number, slot in enumerate(slots):
            here = pl.ds(pl.multiple_of(table_ref[slot] * slab, slab), slab)
            some = block_ref[:, here].astype(F32).T.astype(BF)
            o_ref[number * slab : (number + 1) * slab, index * rows : (index + 1) * rows] = some


def transposed(table, blocks, slots):
    rows, width = blocks[0].shape
    out = jax.ShapeDtypeStruct((width, len(blocks) * rows), BF)
    return small_call(transposed_kernel, "transposed", out, table, *blocks, cost=LONG, slots=slots)


def head_weights_kernel(table_ref, g_ref, own_ref, beside_ref, o_ref, grads_ref, *, kinds, places):
    rows, head_dim = g_ref.shape[2:]

    @pl.when(pl.program_id(0) == 0)
    def _():
        for index in range(g_ref.shape[0]):
            for sequence in range(2):
                for kind in range(kinds):
                    piece = g_ref[table_ref[places + index], sequence * kinds + kind]
                    here = slice(kind * head_dim, (kind + 1) * head_dim)
                    grads_ref[sequence, index * rows : (index + 1) * rows, here] = piece

    o_ref[...] = (dot(own_ref[...], grads_ref[0]) + dot(beside_ref[...], grads_ref[1])).astype(BF)


def head_weights(table, grads, own, beside, kinds, places):
    blocks, _unused, rows, head_dim = grads.shape
    width, total = own.shape
    tall = width // 4
    row = pl.BlockSpec((tall, total), lambda m: (m, 0))
    return pl.pallas_call(
        functools.partial(head_weights_kernel, kinds=kinds, places=places),
        grid=(4,),
        in_specs=[pl.BlockSpec(memory_space=pltpu.SMEM), pl.BlockSpec(grads.shape, lambda m: (0, 0, 0, 0)), row, row],
        out_specs=pl.BlockSpec((tall, kinds * head_dim), lambda m: (m, 0)),
        out_shape=jax.ShapeDtypeStruct((width, kinds * head_dim), BF),
        scratch_shapes=[pltpu.VMEM((2, total, kinds * head_dim), BF)],
        compiler_params=pltpu.CompilerParams(dimension_semantics=("arbitrary",), vmem_limit_bytes=48 * 2**20),
        cost_estimate=LONG,
        name="head_weights",
    )(table, grads, own, beside)


def chip_total_kernel(table_ref, own_ref, other_ref, keep_ref, send_ref, *, core):
    slab = keep_ref.shape[0]
    for ref, at in ((keep_ref, table_ref[core]), (send_ref, 1 - table_ref[core])):
        here = pl.ds(pl.multiple_of(at * slab, slab), slab)
        ref[...] = (own_ref[here, :].astype(F32) + other_ref[here, :].astype(F32)).astype(BF)


def chip_total(table, own, other, core):
    out = [jax.ShapeDtypeStruct((other.shape[0] // 2, own.shape[1]), BF)] * 2
    return small_call(chip_total_kernel, "chip_total", out, table, own, other, core=core)


def beside_kernel(_unused, left_ref, right_ref, o_ref):
    columns = left_ref.shape[1]
    o_ref[:, :columns] = left_ref[...].astype(BF)
    o_ref[:, columns:] = right_ref[...].astype(BF)


def side_by_side(table, left, right):
    out = jax.ShapeDtypeStruct((left.shape[0], left.shape[1] + right.shape[1]), BF)
    return small_call(beside_kernel, "side_by_side", out, table, left, right)


def pair_rows_kernel(g_ref, w_ref, own_ref, beside_ref, dn_ref, *, kinds):
    kind = pl.program_id(1)

    @pl.when((pl.program_id(0) == 0) & (kind == 0))
    def _():
        dn_ref[...] = jnp.zeros_like(dn_ref)

    heads = []
    for head in range(g_ref.shape[0]):
        heads.append(jnp.concatenate([g_ref[head, sequence * kinds + kind] for sequence in range(2)], axis=0))
    dn_ref[...] += dot_nt(jnp.concatenate(heads, axis=1), w_ref[...])

    @pl.when((pl.program_id(0) == pl.num_programs(0) - 1) & (kind == kinds - 1))
    def _():
        rows = own_ref.shape[0]
        own_ref[...] = dn_ref[:rows, :]
        beside_ref[...] = dn_ref[rows:, :].astype(BF)


def pair_normed(grads, columns, kinds):
    heads, _unused, rows, head_dim = grads.shape
    width, at_once = columns.shape[0], 2
    whole = pl.BlockSpec((rows, width), lambda h, k: (0, 0))
    return pl.pallas_call(
        functools.partial(pair_rows_kernel, kinds=kinds),
        grid=(heads // at_once, kinds),
        in_specs=[
            pl.BlockSpec((at_once, 2 * kinds, rows, head_dim), lambda h, k: (h, 0, 0, 0)),
            pl.BlockSpec((width, at_once * head_dim), lambda h, k: (0, k * (heads // at_once) + h)),
        ],
        out_specs=[whole, whole],
        out_shape=[jax.ShapeDtypeStruct((rows, width), kind) for kind in (F32, BF)],
        scratch_shapes=[pltpu.VMEM((2 * rows, width), F32)],
        compiler_params=pltpu.CompilerParams(
            dimension_semantics=("arbitrary", "arbitrary"), vmem_limit_bytes=40 * 2**20
        ),
        cost_estimate=LONG,
        name="pair_normed",
    )(grads, columns)


def take_kernel(table_ref, *refs, count, sides):
    weights, outs, sems = refs[:count], refs[count : count + len(sides)], refs[-1]
    copies = []
    for out, (row, rows, pieces) in zip(outs, sides):
        at = 0
        if row is None:
            here = slice(None)
        else:
            here = pl.ds(pl.multiple_of(table_ref[row] * rows, rows), rows)
        for number, slot, wide in pieces:
            there = slice(None)
            if slot is not None:
                there = pl.ds(pl.multiple_of(table_ref[slot] * wide, wide), wide)
            copies.append(
                pltpu.make_async_copy(
                    weights[number].at[here, there], out.at[:, at : at + wide], sems.at[len(copies)]
                )
            )
            at += wide
    for copy in copies:
        copy.start()
    for copy in copies:
        copy.wait()


def take_parts(table, weights, sides, cost):
    outs = []
    for row, rows, pieces in sides:
        outs.append(jax.ShapeDtypeStruct((rows, sum(wide for _unused, _unused2, wide in pieces)), BF))
    number = sum(len(pieces) for _unused, _unused2, pieces in sides)
    return pl.pallas_call(
        functools.partial(take_kernel, count=len(weights), sides=sides),
        in_specs=[pl.BlockSpec(memory_space=pltpu.SMEM)] + [pl.BlockSpec(memory_space=pl.ANY)] * len(weights),
        out_specs=[pl.BlockSpec(memory_space=pltpu.VMEM)] * len(sides),
        out_shape=outs,
        scratch_shapes=[pltpu.SemaphoreType.DMA((number,))],
        compiler_params=pltpu.CompilerParams(vmem_limit_bytes=60 * 2**20),
        cost_estimate=cost,
        name="take_parts",
    )(table, *weights)


def place_kernel(table_ref, *refs, slots):
    *pieces, out = refs
    for piece, slot in zip(pieces, slots):
        rows = piece.shape[0]
        out[pl.ds(pl.multiple_of(table_ref[slot] * rows, rows), rows), :] = piece[...]


def place_rows(table, pieces, slots):
    rows = sum(piece.shape[0] for piece in pieces)
    out = jax.ShapeDtypeStruct((rows, pieces[0].shape[1]), pieces[0].dtype)
    return small_call(place_kernel, "place_rows", out, table, *pieces, slots=slots)


def pack_kernel(table_ref, below_ref, early_ref, late_ref, o_ref, *, slot, experts):
    slab = o_ref.shape[1] // 4
    first = below_ref.shape[0]
    here = pl.ds(pl.multiple_of(table_ref[slot] * slab, slab), slab)
    o_ref[...] = jnp.zeros_like(o_ref)
    o_ref[:first, :] = below_ref[...].astype(BF)
    for index in range(experts):
        at = first + index // 4
        o_ref[at : at + 1, index % 4 * slab : (index % 4 + 1) * slab] = early_ref[index : index + 1, here].astype(BF)
    at = first + experts // 4
    o_ref[at : at + 1, :] = early_ref[experts : experts + 1, :].astype(BF)
    o_ref[at + 1 : at + 3, :] = late_ref[...].astype(BF)


def pack_gains(table, below, early, late, slot, experts):
    height = below.shape[0] + -(-(experts // 4 + 3) // 16) * 16
    out = jax.ShapeDtypeStruct((height, early.shape[1]), BF)
    return small_call(pack_kernel, "pack_gains", out, table, below, early, late, slot=slot, experts=experts)


def unpack_kernel(table_ref, *refs, back, experts):
    *pieces, router_ref, gains_ref, all_ref = refs
    height = all_ref.shape[1]
    for index, piece in enumerate(pieces):
        all_ref[index] = piece[piece.shape[0] - height :, :].astype(F32)
    total = all_ref[table_ref[back]]
    for place in range(1, len(pieces)):
        total = total + all_ref[table_ref[back + place]]
    slab = total.shape[1] // 4
    rows = [total[i // 4 : i // 4 + 1, i % 4 * slab : (i % 4 + 1) * slab] for i in range(experts)]
    router_ref[...] = jnp.concatenate(rows, axis=0).T
    gains_ref[...] = total[experts // 4 : experts // 4 + 3, :]


def unpack_gains(table, pieces, back, experts, height):
    width = pieces[0].shape[1]
    out = [jax.ShapeDtypeStruct((width // 4, experts), F32), jax.ShapeDtypeStruct((3, width), F32)]
    scratch = [pltpu.VMEM((len(pieces), height, width), F32)]
    return small_call(
        unpack_kernel, "unpack_gains", out, table, *pieces, scratch=scratch, back=back, experts=experts
    )


def spread_kernel(table_ref, *refs, count, outs, cuts):
    pieces = refs[:count]
    out_refs = refs[-2 - outs : -2]
    wide_ref, sems = refs[-2:]
    copies = []
    for index, (number, rows, columns, out, slot, by_rows) in enumerate(cuts):
        wide_ref[index] = pieces[number][rows[0] : rows[1], columns[0] : columns[1]].astype(F32)
        size = rows[1] - rows[0] if by_rows else columns[1] - columns[0]
        here = pl.ds(pl.multiple_of(table_ref[slot] * size, size), size)
        to = out_refs[out].at[here, :] if by_rows else out_refs[out].at[:, here]
        copies.append(pltpu.make_async_copy(wide_ref.at[index], to, sems.at[index]))
        copies[-1].start()
    for copy in copies:
        copy.wait()


def spread(table, pieces, cuts, shape, outs, before):
    vmem, anywhere = pl.BlockSpec(memory_space=pltpu.VMEM), pl.BlockSpec(memory_space=pl.ANY)
    old = [] if before is None else list(before)
    _unused, rows, columns, *_rest = cuts[0]
    return pl.pallas_call(
        functools.partial(spread_kernel, count=len(pieces), outs=outs, cuts=cuts),
        in_specs=[pl.BlockSpec(memory_space=pltpu.SMEM)] + [vmem] * len(pieces) + [anywhere] * len(old),
        out_specs=[anywhere] * outs,
        out_shape=[jax.ShapeDtypeStruct(shape, F32)] * outs,
        input_output_aliases={1 + len(pieces) + index: index for index in range(len(old))},
        scratch_shapes=[
            pltpu.VMEM((len(cuts), rows[1] - rows[0], columns[1] - columns[0]), F32),
            pltpu.SemaphoreType.DMA((len(cuts),)),
        ],
        compiler_params=pltpu.CompilerParams(vmem_limit_bytes=24 * 2**20),
        cost_estimate=SMALL,
        name="spread",
    )(table, *pieces, *old)


def merge_kernel(w_ref, o_ref):
    units = w_ref.shape[2]
    for index in range(w_ref.shape[1]):
        o_ref[:, index * units : (index + 1) * units] = w_ref[:, index, :]


def merge_experts(weight):
    rows, count, units = weight.shape
    at_once = 128
    return pl.pallas_call(
        merge_kernel,
        grid=(rows // at_once,),
        in_specs=[pl.BlockSpec((at_once, count, units), lambda m: (m, 0, 0))],
        out_specs=pl.BlockSpec((at_once, count * units), lambda m: (m, 0)),
        out_shape=jax.ShapeDtypeStruct((rows, count * units), weight.dtype),
        cost_estimate=MEDIUM,
        name="merge_experts",
    )(weight)


def split_kernel(*refs):
    *term_refs, o_ref = refs
    units = o_ref.shape[2]
    for index in range(o_ref.shape[1]):
        here = slice(index * units, (index + 1) * units)
        total = term_refs[0][:, here].astype(F32)
        for term_ref in term_refs[1:]:
            total = total + term_ref[:, here].astype(F32)
        o_ref[:, index, :] = total


def split_experts(count, rows, *terms):
    columns = terms[0][0].shape[1]
    at_once = 128
    steps = rows // at_once

    def spec(at):
        return pl.BlockSpec((at_once, columns), lambda m: (at * steps + m, 0))

    return pl.pallas_call(
        split_kernel,
        grid=(steps,),
        in_specs=[spec(at) for _unused, at in terms],
        out_specs=pl.BlockSpec((at_once, count, columns // count), lambda m: (m, 0, 0)),
        out_shape=jax.ShapeDtypeStruct((rows, count, columns // count), F32),
        cost_estimate=SMALL,
        name="split_experts",
    )(*[array for array, _unused in terms])


def swap(v, mask):
    size = lax.axis_size("fsdp")
    return lax.ppermute(v, "fsdp", [(i, i ^ mask) for i in range(size)])


def ring_order(size):
    if size == 8:
        return [0, 2, 4, 6, 7, 5, 3, 1]
    return list(range(size))


def ring_send(v, direction):
    order = ring_order(lax.axis_size("ctx"))
    size = len(order)
    return lax.ppermute(v, "ctx", [(order[i], order[(i + direction) % size]) for i in range(size)])


class Flight(tuple):
    def noted(self, note):
        self.note = note
        return self


class Ring:
    def __init__(self, in_order, steps):
        self.in_order, self.steps, self.value, self.landed = in_order, steps, None, None
        self.flying = next(steps)

    def land(self):
        land(self.in_order, (self,))

    def step(self):
        if self.flying is None:
            return
        self.land()
        try:
            self.flying = self.steps.send(self.landed)
        except StopIteration as end:
            self.flying, self.value = None, end.value
        self.landed = None

    def finish(self):
        while self.flying is not None:
            self.step()
        return self.value


def land(in_order, rings, *more):
    rings = [ring for ring in rings if ring.flying is not None and ring.landed is None]
    found = [v for ring in rings for v in ring.flying] + list(more)
    if not found:
        return more
    found = in_order(*found) if len(found) > 1 else [in_order(*found)]
    for ring in rings:
        ring.landed, found = found[: len(ring.flying)], found[len(ring.flying) :]
        if isinstance(ring.flying, Flight):
            ring.flying.note(*ring.landed)
    return found


def ring_gather(v, in_order, found):
    size = lax.axis_size("ctx")
    far, half = size // 2, v.shape[0] // 2
    found[0] = v
    right, left = v, v
    for step in range(1, far):
        right, left = after((right, left), in_order.last)

        def note(right, left, step=step):
            found[size - step], found[step] = right, left

        right, left = yield Flight((ring_send(right, 1), ring_send(left, -1))).noted(note)

    def note_far(right, left):
        found[far] = jnp.concatenate([right, left])

    yield Flight((ring_send(right[:half], 1), ring_send(left[half:], -1))).noted(note_far)
    return found


def ring_scatter(term):
    size = lax.axis_size("ctx")
    far = size // 2
    first = term(far)
    half = first.shape[0] // 2
    right, left = yield (ring_send(first[:half].astype(BF), 1), ring_send(first[half:].astype(BF), -1))
    for offset in range(far - 1, 0, -1):
        ahead, behind = term(offset), term(size - offset)
        if offset == far - 1:
            ahead = jnp.concatenate([ahead[:half].astype(F32) + right.astype(F32), ahead[half:].astype(F32)])
            behind = jnp.concatenate([behind[:half].astype(F32), behind[half:].astype(F32) + left.astype(F32)])
        else:
            ahead, behind = ahead.astype(F32) + right.astype(F32), behind.astype(F32) + left.astype(F32)
        right, left = yield (ring_send(ahead.astype(BF), 1), ring_send(behind.astype(BF), -1))
    return term(0).astype(F32) + right.astype(F32) + left.astype(F32)


def after(v, *others):
    return lax.optimization_barrier((v, *others))[0]


class Order:
    def __init__(self, first):
        self.last = first

    def __call__(self, *values):
        self.last, *values = lax.optimization_barrier((self.last, *values))
        return values[0] if len(values) == 1 else values


def sum_fsdp(v):
    size = lax.axis_size("fsdp")
    mask = 1
    while mask < size:
        (other,) = yield (swap(v, mask),)
        v = v + other
        mask *= 2
    return v


def body(
    tokens, attn_gain, w_query, w_key, w_value, query_gain, key_gain, w_out,
    ffn_gain, w_router, w_gate, w_up, w_down, routes, cotangent,
):
    ctx_size = lax.axis_size("ctx")
    parts = lax.axis_size("fsdp")
    rows = tokens.shape[1]
    width = tokens.shape[2]
    slab = w_query.shape[0]
    head_dim = query_gain.shape[0]
    own_heads = width // head_dim // parts
    own_width = own_heads * head_dim
    own_rows = slab // ctx_size
    own_experts = w_gate.shape[1]
    hidden_units = w_gate.shape[2]
    experts = own_experts * ctx_size
    seq_length = rows * ctx_size
    in_order = Order(jnp.zeros((), F32))

    heads = 2 * own_heads
    repeats = ctx_size // heads
    order = ring_order(ctx_size)
    offsets = [0] + [o for step in range(1, ctx_size // 2) for o in (step, ctx_size - step)] + [ctx_size // 2]
    at_ring, at_place, at_core, at_side = 0, 1, 2, 3
    at_slab = [4 + mask for mask in range(parts)]
    at_groups, at_beside, at_chip = (8, 9), (10, 11), (12, 13, 14, 15)
    at_order = (16, 17, 18, 19)
    at_from = 20
    at_blocks = [at_from + ctx_size + index for index in range(ctx_size)]
    at_heads = [(at_from + 2 * ctx_size + index, at_from + 3 * ctx_size + index) for index in range(ctx_size)]
    at_turn = at_from + 4 * ctx_size
    at_back = at_from + 5 * ctx_size
    lines = []
    for place in range(ctx_size):
        ring_place = order.index(place)
        for mine in range(parts):
            side, core = divmod(mine, 2)
            line = [ring_place, place, core, side] + [mine ^ mask for mask in range(parts)]
            line += [core, core + 2, 1 - core, 3 - core, 2 * side, 2 * side + 1, 2 - 2 * side, 3 - 2 * side]
            line += [mine ^ 1, mine ^ 3, mine ^ 2, mine]
            places = [order[(ring_place + offset) % ctx_size] for offset in offsets]
            line += places
            line += [(ring_place + offset) % ctx_size for offset in offsets]
            for first in (core, 1 - core):
                line += [first * own_heads + other // repeats + other // repeats // own_heads * own_heads for other in places]
            line += [(ring_place + index) % ctx_size for index in range(ctx_size)]
            line += [offsets.index((order.index(other) - ring_place) % ctx_size) for other in range(ctx_size)]
            lines.append(line)
    device = lax.axis_index("ctx").astype(jnp.uint32) * parts + lax.axis_index("fsdp").astype(jnp.uint32)
    table = lax.dynamic_slice(jnp.asarray(np.array(lines, np.int32)), (device, jnp.uint32(0)), (1, len(lines[0])))
    table = table.reshape(-1)

    def spread_pairs(v):
        if repeats > 1:
            v = jnp.repeat(v, repeats, axis=0)
        return lax.all_to_all(v, "ctx", split_axis=0, concat_axis=0, tiled=True)

    def collect_pairs(v):
        v = lax.all_to_all(v, "ctx", split_axis=0, concat_axis=0, tiled=True)
        return v[::repeats] if repeats > 1 else v

    projections = (w_query, w_key, w_value)

    def side_of(row, rows, slots):
        return row, rows, [(number, slot, own_width) for number in range(3) for slot in slots]

    row, rows_of, some = side_of(at_ring, own_rows, at_groups)
    fetched = in_order(
        *take_parts(
            table, (*projections, w_out), [(row, rows_of, some + [(3, None, width)]), side_of(row, rows_of, at_beside)], SMALL
        )
    )
    fetched = swap(fetched[0], 2), swap(fetched[1], 3)
    cot_blocks = {}
    cot_ring = Ring(in_order, ring_gather(after(cotangent[0], in_order.last), in_order, cot_blocks))
    source = tokens[0].astype(F32)
    factor_one = lax.rsqrt(jnp.mean(source * source, axis=-1, keepdims=True) + EPSILON)
    normed = (source * factor_one * attn_gain).astype(BF)
    projections, w_down, w_gate, w_up = after((projections, w_down, w_gate, w_up), in_order.last)
    near, own, normed = in_order(
        *take_parts(
            table, projections, [side_of(None, slab, at_beside), side_of(None, slab, at_groups)], MEDIUM
        ),
        normed,
    )
    cot_ring.step()
    beside, near = swap(normed, 1), swap(near, 1)
    w_down = in_order(merge_experts(after(w_down, in_order.last)))
    cot_ring.land()
    fetched = in_order(*fetched)
    column_blocks = {}
    ring = Ring(in_order, ring_gather(fetched_payload(table, *fetched, width), in_order, column_blocks))
    down_w = lax.all_gather(after(w_down, in_order.last), "fsdp", axis=0, tiled=True)
    w_gate = in_order(merge_experts(after(w_gate, in_order.last)))
    ring.step()
    gate_w = lax.all_gather(after(w_gate, in_order.last), "fsdp", axis=0, tiled=True)
    w_router, routes = after((w_router, routes), in_order.last)
    router = [w_router, swap(w_router, 1), swap(w_router, 2), swap(w_router, 3)]
    routes_all = lax.all_to_all(
        jnp.broadcast_to(routes, (ctx_size, *routes.shape[1:])), "ctx", split_axis=0, concat_axis=0, tiled=True
    )
    normed, near, beside = in_order(normed, near, beside)
    w_up = in_order(merge_experts(after(w_up, in_order.last)))
    ring.step()
    up_w = lax.all_gather(after(w_up, in_order.last), "fsdp", axis=0, tiled=True)
    routes_all, *router = in_order(routes_all, *router)
    ring.step()

    half = head_dim // 2
    frequency = ROPE_BASE ** (-jnp.arange(half, dtype=F32) * 2.0 / head_dim)
    angles = jnp.arange(seq_length, dtype=jnp.int32).astype(F32)[:, None] * frequency[None, :]
    cosine, sine = jnp.cos(angles), jnp.sin(angles)
    cosine = jnp.concatenate([cosine, cosine], axis=1)
    sine = jnp.concatenate([-sine, sine], axis=1)
    q_gain, k_gain = query_gain[None, :], key_gain[None, :]

    ring.finish()
    qkv, own_columns = own_pairs(
        table,
        (normed, beside),
        own,
        near,
        [column_blocks[offset] for offset in offsets],
        3,
        head_dim,
        at_slab,
        at_blocks,
    )
    qkv = spread_pairs(in_order(qkv))
    router_w = in_order(place_rows(table, after(router, in_order.last), at_slab))
    w_far = in_order(far_rows(table, [column_blocks[offset] for offset in offsets], at_blocks))
    qkv = in_order(qkv)
    down_w, gate_w = in_order(down_w, gate_w)
    mixed = in_order(attend(qkv, q_gain, k_gain, cosine, sine))
    mixed = in_order(collect_pairs(mixed))
    hidden, far = in_order(*mixed_out(table, mixed, w_out, w_far, at_side))
    far = swap(far, 1)
    hidden = in_order(source + hidden)
    hidden = hidden + in_order(far).astype(F32)
    up_w = in_order(up_w)
    factor_two = lax.rsqrt(jnp.mean(hidden * hidden, axis=-1, keepdims=True) + EPSILON)
    ffn_in = in_order((hidden * factor_two * ffn_gain).astype(BF))

    ffn_blocks = {}
    ffn_ring = Ring(in_order, ring_gather(ffn_in, in_order, ffn_blocks))
    ffn_ring.step()

    size = 4
    groups = [offsets[first : first + size] for first in range(0, ctx_size, size)]

    def group_cots(group):
        return in_order(*stacked_matmul([cot_blocks[o] for o in groups[group]], down_w))

    def group_units(group, grad_act):
        return in_order(
            *expert_units(
                table, at_place, at_from + group * size, [ffn_blocks[o] for o in groups[group]], routes_all, router_w,
                gate_w, up_w, grad_act, own_experts,
            )
        )

    cots = [group_cots(0)]
    ffn_ring.step()
    cot_ring.step()
    units = [group_units(0, cots[0][0])]
    ffn_ring.step()
    cot_ring.step()
    other_side = (1 - table[at_side]).astype(jnp.uint32) * own_heads
    zero = jnp.uint32(0)
    other_mixed = lax.dynamic_slice(
        after(mixed, in_order.last), (other_side, zero, zero, zero), (own_heads, *mixed.shape[1:])
    )
    other_mixed = swap(other_mixed, 2)
    cot_ring.finish()
    ffn_ring.finish()
    normed_blocks = {}
    normed_ring = Ring(in_order, ring_gather(after(normed, in_order.last), in_order, normed_blocks))
    for group in range(1, len(groups)):
        cots.append(group_cots(group))
        if group == 1:
            normed_ring.step()
        units.append(group_units(group, cots[group][0]))
    cots = [part for _unused, part in cots]
    acts, gate_grads, up_grads, d_gates, inputs = zip(*units)

    def term_of(terms):
        def term(offset):
            group, index = divmod(offsets.index(offset), size)
            return terms[group][index * rows : (index + 1) * rows]

        return term

    def weight_grad(lefts, rights):
        lefts, rights = after((lefts, rights), in_order.last)
        return in_order(sum_of_outer(table, lefts, rights))

    def share(grad):
        return lax.psum_scatter(after(grad, in_order.last), "fsdp", scatter_dimension=0, tiled=True)

    grad_rows = {}

    def make_rows(group):
        some = after((gate_grads[group], up_grads[group]), in_order.last)
        grad_rows[group] = in_order(expert_rows(*some, gate_w, up_w))

    other_mixed = in_order(other_mixed)
    normed_ring.step()
    for group in range(len(groups) - 1, 0, -1):
        make_rows(group)
    normed_ring.step()
    row_ring = Ring(in_order, ring_scatter(term_of(grad_rows)))
    d_gate = weight_grad(inputs, gate_grads)
    row_ring.step()
    d_gate = share(d_gate)
    normed_ring.finish()
    make_rows(0)
    row_ring.step()
    weighted = in_order(*times_transpose(after(acts, in_order.last), down_w))
    row_ring.step()
    ring = Ring(in_order, ring_scatter(term_of(weighted)))
    d_gates = jnp.concatenate(after(d_gates, in_order.last), axis=1).reshape(own_experts, ctx_size, rows)
    d_gates = d_gates.at[:, table[at_back : at_back + ctx_size], :].get(mode="promise_in_bounds").transpose(1, 0, 2)
    d_gates = lax.all_to_all(d_gates, "ctx", split_axis=0, concat_axis=0, tiled=True)
    some = after(tuple(normed_blocks[offset] for offset in offsets), in_order.last)
    normed_t = in_order(transposed(table, some, at_chip))
    land(in_order, (row_ring, ring))
    d_gates = in_order(d_gates).reshape(experts, rows).T
    beside_t = swap(normed_t, 1)
    gates = routed_gates(dot(ffn_in, router_w), routes[0])
    grad_logits = gates * (d_gates - jnp.sum(gates * d_gates, axis=-1, keepdims=True))
    routed = dot(grad_logits, router_w.astype(F32), ((1,), (1,)), precision=lax.Precision.HIGHEST)
    routed = in_order(routed)
    grad_ffn_in = row_ring.finish() + routed

    inner = grad_ffn_in * ffn_gain
    grad_hidden = (
        cotangent[0].astype(F32)
        + factor_two * inner
        - hidden * (factor_two * factor_two * factor_two) * jnp.mean(inner * hidden, axis=-1, keepdims=True)
    )
    grad_proj, grad_hidden, grad_ffn_in = in_order(grad_hidden.astype(BF), grad_hidden, grad_ffn_in)

    beside = swap(grad_proj, 1)
    grad_proj, beside, beside_t = in_order(grad_proj, beside, beside_t)
    grad_mixed = in_order(grad_pairs(table, grad_proj, beside, w_out, w_far, at_side, head_dim))
    across = swap(after(grad_proj, in_order.last), 2)
    ring.step()
    grad_mixed = spread_pairs(grad_mixed)
    d_up = weight_grad(inputs, up_grads)
    (grad_mixed,) = land(in_order, (ring,), grad_mixed)
    d_up = share(d_up)
    ring.step()
    grads, head_gains = in_order(
        *attend_back(qkv, after(grad_mixed, in_order.last), q_gain, k_gain, cosine, sine)
    )
    if repeats > 1:
        head_gains = jnp.where(lax.axis_index("ctx") % repeats == 0, head_gains, 0.0)
    ring.land()

    grads = after(grads, in_order.last)
    ring.step()
    half_grads = in_order(head_weights(table, grads, normed_t, beside_t, 3, at_from))
    other_half = swap(half_grads[width // 2 :], 2)
    across = in_order(across)
    diagonal = swap(across, 1)
    grads = collect_pairs(after(grads, in_order.last))
    mixed, diagonal = after((mixed, diagonal), in_order.last)
    d_out = in_order(
        out_grads(table, mixed, other_mixed, [grad_proj, beside, across, diagonal], at_turn, own_rows, at_side)
    )
    other_half = in_order(other_half)
    keep, send = in_order(*chip_total(table, half_grads, other_half, at_core))
    send = in_order(swap(send, 1))
    pieces = {}
    total_ring = Ring(in_order, ring_gather(side_by_side(table, keep, send), in_order, pieces))
    out_ring = Ring(in_order, ring_scatter(lambda offset: d_out[offset * own_rows : (offset + 1) * own_rows]))
    d_down = weight_grad(cots, acts)
    (grads,) = land(in_order, (total_ring, out_ring, ring), grads)
    total_ring.step()
    out_ring.step()
    d_down = share(d_down)
    own, far = in_order(*pair_normed(after(grads, in_order.last), own_columns, 3))
    land(in_order, (total_ring, out_ring))
    far = swap(far, 1)
    total_ring.step()
    grad_ffn_in, grad_logits = after((grad_ffn_in, grad_logits), in_order.last)
    d_ffn_gain = jnp.sum(grad_ffn_in * hidden * factor_two, axis=0, keepdims=True)
    d_router = dot(grad_logits, ffn_in.astype(F32), ((0,), (0,)), precision=lax.Precision.HIGHEST)
    early = Ring(in_order, sum_fsdp(in_order(jnp.concatenate([d_router, d_ffn_gain]))))
    out_ring.step()
    early.step()
    grad_normed = own + in_order(far).astype(F32)
    d_attn_gain = jnp.sum(grad_normed * source * factor_one, axis=0)
    inner = grad_normed * attn_gain
    d_tokens = (
        grad_hidden
        + factor_one * inner
        - source * (factor_one * factor_one * factor_one) * jnp.mean(inner * source, axis=-1, keepdims=True)
    )
    late = jnp.concatenate([d_attn_gain, head_gains[0], head_gains[1], jnp.zeros((width - 2 * head_dim,), F32)])
    d_tokens, late = in_order(d_tokens, late.reshape(2, width))
    late = Ring(in_order, sum_fsdp(late))
    late.step()
    early.finish()
    out_ring.step()

    whole = None
    seen = set()

    def take_whole(arrays):
        new = [index for index, offset in enumerate(offsets) if offset in pieces and index not in seen]
        seen.update(new)
        high = pieces[offsets[0]].shape[0]
        for first in range(0, len(new), 4):
            some = new[first : first + 4]
            cuts = []
            for number, index in enumerate(some):
                for where in range(2):
                    for kind in range(3):
                        at = (where * 3 + kind) * head_dim
                        cuts.append((number, (0, high), (at, at + head_dim), kind, at_heads[index][where], False))
            found = [pieces[offsets[index]] for index in some]
            arrays = in_order(*spread(table, found, cuts, (slab, width), 3, arrays))
        return arrays

    whole = take_whole(whole)
    late.finish()
    output = in_order((hidden + ring.finish()).astype(BF))
    d_out = out_ring.finish()
    packed = in_order(pack_gains(table, d_out, early.value, late.value, at_slab[0], experts))
    packed_pieces = {}
    packed_ring = Ring(in_order, ring_gather(packed, in_order, packed_pieces))
    total_ring.step()
    d_gate = in_order(split_experts(own_experts, slab, (after(d_gate, in_order.last), 0)))
    whole = take_whole(whole)
    packed_ring.step()
    total_ring.finish()
    whole = take_whole(whole)
    d_query, d_key, d_value = whole
    packed_ring.step()
    d_up = in_order(split_experts(own_experts, slab, (after(d_up, in_order.last), 0)))
    packed_ring.step()
    d_down = in_order(split_experts(own_experts, slab, (after(d_down, in_order.last), 0)))
    packed_ring.finish()
    packed_blocks = [packed_pieces[offset] for offset in offsets]
    cuts = [(index, (0, own_rows), (0, width), 0, at_blocks[index], True) for index in range(ctx_size)]
    (d_out,) = spread(table, packed_blocks, cuts, (slab, width), 1, None)
    height = packed.shape[0] - own_rows
    d_router, gains = unpack_gains(table, packed_blocks, at_back, experts, height)
    d_ffn_gain, d_attn_gain, head_gains = gains + in_order.last
    return (
        output[None],
        d_tokens[None],
        d_attn_gain,
        d_query,
        d_key,
        d_value,
        head_gains[:head_dim],
        head_gains[head_dim : 2 * head_dim],
        d_out,
        d_ffn_gain,
        d_router,
        d_gate,
        d_up,
        d_down,
    )


def solution(mesh):
    token_split = P("fsdp", "ctx", None)
    row_split = P("fsdp", None)
    return jax.shard_map(
        body,
        mesh=mesh,
        in_specs=(
            token_split, P(), row_split, row_split, row_split, P(), P(), row_split,
            P(), row_split, token_split, token_split, token_split, token_split, token_split,
        ),
        out_specs=(
            token_split, token_split, P(), row_split, row_split, row_split, P(), P(),
            row_split, P(), row_split, token_split, token_split, token_split,
        ),
        check_vma=False,
    )
```

```python
import functools

import jax
import jax.numpy as jnp
import numpy as np
from jax import lax
from jax.experimental import pallas as pl
from jax.experimental.pallas import tpu as pltpu
from jax.sharding import PartitionSpec as P

EPSILON = 1e-06
ROPE_BASE = 10000.0
BF = jnp.bfloat16
F32 = jnp.float32
LONG = pl.CostEstimate(flops=10**12, bytes_accessed=10**9, transcendentals=0)
MEDIUM = pl.CostEstimate(flops=2 * 10**10, bytes_accessed=5 * 10**7, transcendentals=0)
SMALL = pl.CostEstimate(flops=1, bytes_accessed=1, transcendentals=0)


def dot(a, b, contract=((1,), (0,)), precision=None):
    return lax.dot_general(a, b, (contract, ((), ())), precision=precision, preferred_element_type=F32)


def dot_nt(a, b):
    return dot(a, b, ((1,), (1,)))


def dot_tn(a, b):
    return dot(a, b, ((0,), (0,)))


def head_norm(v, gain):
    factor = lax.rsqrt(jnp.mean(v * v, axis=-1, keepdims=True) + EPSILON)
    return v * factor * gain, factor


def turn(v, cosine, sine):
    return v * cosine + pltpu.roll(v, v.shape[-1] // 2, 1) * sine


def head_back(grad, v, gain, cosine, sine):
    grad = turn(grad, cosine, -sine)
    factor = lax.rsqrt(jnp.mean(v * v, axis=-1, keepdims=True) + EPSILON)
    gain_grad = jnp.sum(grad * v * factor, axis=0, keepdims=True)
    inner = grad * gain
    return factor * inner - v * (factor * factor * factor) * jnp.mean(inner * v, axis=-1, keepdims=True), gain_grad


def rows_of(ref):
    block = ref[...]
    return block.reshape(-1, block.shape[-1])


def attend_kernel(q_ref, k_ref, v_ref, qg_ref, kg_ref, cos_ref, sin_ref, o_ref, keys, values_t):
    step = pl.program_id(1)

    @pl.when(step == 0)
    def _():
        normed, _unused = head_norm(rows_of(k_ref).astype(F32), kg_ref[...])
        keys[...] = turn(normed, cos_ref[...], sin_ref[...]).astype(BF)
        values_t[...] = rows_of(v_ref).astype(F32).T.astype(BF)

    queries = rows_of(q_ref).astype(F32)
    number, head_dim = queries.shape
    here = pl.ds(pl.multiple_of(step * number, number), number)
    normed, _unused = head_norm(queries, qg_ref[...])
    queries = turn(normed, cos_ref[here, :], sin_ref[here, :]).astype(BF)
    weights = jnp.exp(dot_nt(keys[...], queries) * (head_dim**-0.5))
    total = jnp.sum(weights, axis=0, keepdims=True)
    mixed = dot(values_t[...], weights.astype(BF)) / total
    o_ref[...] = mixed.T.astype(BF).reshape(o_ref.shape)


def attend_back_kernel(
    q_ref, k_ref, v_ref, m_ref, qg_ref, kg_ref, cos_ref, sin_ref,
    g_ref, gain_ref, keys, keys_t, key_acc, value_acc,
):
    pair = pl.program_id(0)
    step = pl.program_id(1)
    last = pl.num_programs(1) - 1

    @pl.when((pair == 0) & (step == 0))
    def _():
        gain_ref[...] = jnp.zeros_like(gain_ref)

    @pl.when(step == 0)
    def _():
        normed, _unused = head_norm(rows_of(k_ref).astype(F32), kg_ref[...])
        turned = turn(normed, cos_ref[...], sin_ref[...])
        keys[...] = turned.astype(BF)
        keys_t[...] = turned.T.astype(BF)
        key_acc[...] = jnp.zeros_like(key_acc)
        value_acc[...] = jnp.zeros_like(value_acc)

    query_pre = rows_of(q_ref).astype(F32)
    grad_mixed = rows_of(m_ref)
    number, head_dim = query_pre.shape
    scale = head_dim**-0.5
    here = pl.ds(pl.multiple_of(step * number, number), number)
    cosine, sine = cos_ref[here, :], sin_ref[here, :]
    normed, _unused = head_norm(query_pre, qg_ref[...])
    queries = turn(normed, cosine, sine).astype(BF)
    weights = jnp.exp(dot_nt(keys[...], queries) * scale)
    probs = weights * (1.0 / jnp.sum(weights, axis=0, keepdims=True))
    value_acc[...] += dot(probs.astype(BF), grad_mixed)
    weighted = probs * dot_nt(rows_of(v_ref), grad_mixed)
    delta = jnp.sum(weighted, axis=0, keepdims=True)
    grad_scores = (weighted - probs * delta).astype(BF)
    key_acc[...] += dot(grad_scores, queries)
    grad_query = dot(keys_t[...], grad_scores).T * scale
    grad_query, gain_grad = head_back(grad_query, query_pre, qg_ref[...], cosine, sine)
    rows = g_ref.shape[2]
    blocks = number // rows
    g_ref[pl.ds(step * blocks, blocks), 0] = grad_query.astype(BF).reshape(blocks, rows, head_dim)
    gain_ref[0:1, :] += gain_grad

    @pl.when(step == last)
    def _():
        grad_key, gain_grad = head_back(
            key_acc[...] * scale, rows_of(k_ref).astype(F32), kg_ref[...], cos_ref[...], sin_ref[...]
        )
        g_ref[:, 1] = grad_key.astype(BF).reshape(-1, rows, head_dim)
        g_ref[:, 2] = value_acc[...].astype(BF).reshape(-1, rows, head_dim)
        gain_ref[1:2, :] += gain_grad


def attention_specs(shape):
    blocks, pairs, rows, head_dim = shape
    at_once = max(1, 256 // rows)
    while blocks % at_once:
        at_once -= 1
    pairs //= 3
    part = pl.BlockSpec((at_once, 1, rows, head_dim), lambda p, i: (i, p, 0, 0))
    three = [
        pl.BlockSpec((at_once, 1, rows, head_dim), lambda p, i: (i, 3 * p, 0, 0)),
        pl.BlockSpec((blocks, 1, rows, head_dim), lambda p, i: (0, 3 * p + 1, 0, 0)),
        pl.BlockSpec((blocks, 1, rows, head_dim), lambda p, i: (0, 3 * p + 2, 0, 0)),
    ]
    gain = pl.BlockSpec((1, head_dim), lambda p, i: (0, 0))
    table = pl.BlockSpec((blocks * rows, head_dim), lambda p, i: (0, 0))
    params = pltpu.CompilerParams(
        dimension_semantics=("arbitrary", "arbitrary"),
        vmem_limit_bytes=(24 if blocks * rows <= 1024 else 56) * 2**20,
    )
    return part, three, gain, table, (pairs, blocks // at_once), params


def attend(qkv, query_gain, key_gain, cosine, sine):
    part, three, gain, table, grid, params = attention_specs(qkv.shape)
    blocks, _unused, rows, head_dim = qkv.shape
    length = blocks * rows
    return pl.pallas_call(
        attend_kernel,
        grid=grid,
        in_specs=[*three, gain, gain, table, table],
        out_specs=part,
        out_shape=jax.ShapeDtypeStruct((blocks, grid[0], rows, head_dim), BF),
        scratch_shapes=[pltpu.VMEM((length, head_dim), BF), pltpu.VMEM((head_dim, length), BF)],
        compiler_params=params,
        cost_estimate=MEDIUM,
        name="attend",
    )(qkv, qkv, qkv, query_gain, key_gain, cosine, sine)


def attend_back(qkv, grad_mixed, query_gain, key_gain, cosine, sine):
    part, three, gain, table, grid, params = attention_specs(qkv.shape)
    blocks, _unused, rows, head_dim = qkv.shape
    length = blocks * rows
    return pl.pallas_call(
        attend_back_kernel,
        grid=grid,
        in_specs=[*three, part, gain, gain, table, table],
        out_specs=[
            pl.BlockSpec((blocks, 3, rows, head_dim), lambda p, i: (0, p, 0, 0)),
            pl.BlockSpec((8, head_dim), lambda p, i: (0, 0)),
        ],
        out_shape=[jax.ShapeDtypeStruct(qkv.shape, BF), jax.ShapeDtypeStruct((8, head_dim), F32)],
        scratch_shapes=[
            pltpu.VMEM((length, head_dim), BF),
            pltpu.VMEM((head_dim, length), BF),
            pltpu.VMEM((length, head_dim), F32),
            pltpu.VMEM((length, head_dim), F32),
        ],
        compiler_params=params,
        cost_estimate=LONG,
        name="attend_back",
    )(qkv, qkv, qkv, grad_mixed, query_gain, key_gain, cosine, sine)


def stack_blocks(block_refs, out_ref):
    rows = block_refs[0].shape[0]
    for index, block_ref in enumerate(block_refs):
        out_ref[index * rows : (index + 1) * rows, :] = block_ref[...]


def stacked_kernel(w_ref, *refs):
    *block_refs, o_ref, rows_ref = refs

    @pl.when(pl.program_id(0) == 0)
    def _():
        stack_blocks(block_refs, rows_ref)

    o_ref[...] = dot(rows_ref[...], w_ref[...])


def stacked_matmul(blocks, weight):
    rows, depth = len(blocks) * blocks[0].shape[0], weight.shape[0]
    wide = min(512, weight.shape[1])
    return pl.pallas_call(
        stacked_kernel,
        grid=(weight.shape[1] // wide,),
        in_specs=[pl.BlockSpec((depth, wide), lambda n: (0, n))]
        + [pl.BlockSpec(block.shape, lambda n: (0, 0)) for block in blocks],
        out_specs=[pl.BlockSpec((rows, wide), lambda n: (0, n)), pl.BlockSpec((rows, depth), lambda n: (0, 0))],
        out_shape=[jax.ShapeDtypeStruct((rows, weight.shape[1]), F32), jax.ShapeDtypeStruct((rows, depth), BF)],
        compiler_params=pltpu.CompilerParams(dimension_semantics=("arbitrary",), vmem_limit_bytes=56 * 2**20),
        cost_estimate=LONG,
        name="stacked_matmul",
    )(weight, *blocks)


def routed_gates(logits, routes):
    columns = lax.broadcasted_iota(jnp.int32, logits.shape, 1)
    chosen = columns == routes[:, 0:1]
    for index in range(1, routes.shape[1]):
        chosen = chosen | (columns == routes[:, index : index + 1])
    high = jnp.max(jnp.where(chosen, logits, -1e30), axis=-1, keepdims=True)
    weights = jnp.where(chosen, jnp.exp(jnp.where(chosen, logits - high, 0.0)), 0.0)
    return weights / jnp.sum(weights, axis=-1, keepdims=True)


def expert_kernel(table_ref, router_ref, routes_ref, gate_w_ref, up_w_ref, grad_ref, *refs, per, place, at):
    *block_refs, act_ref, gate_ref, up_ref, d_gates_ref, x_ref, gates_ref = refs
    step = pl.program_id(0)

    @pl.when(step == 0)
    def _():
        stack_blocks(block_refs, x_ref)
        routes = jnp.concatenate([routes_ref[table_ref[at + index]] for index in range(len(block_refs))], axis=0)
        gates = routed_gates(dot(x_ref[...], router_ref[...]), routes)
        columns = lax.broadcasted_iota(jnp.int32, gates.shape, 1)
        count = gates_ref.shape[0]
        for index in range(count):
            here = columns == table_ref[place] * count + index
            gates_ref[index] = jnp.sum(jnp.where(here, gates, 0.0), axis=1, keepdims=True)

    @pl.when(step % per == 0)
    def _():
        d_gates_ref[...] = jnp.zeros_like(d_gates_ref)

    gate_pre = dot(x_ref[...], gate_w_ref[...])
    up_pre = dot(x_ref[...], up_w_ref[...])
    grad_act = grad_ref[...]
    gates = gates_ref[step // per]
    sigmoid = 1.0 / (1.0 + jnp.exp(-gate_pre))
    silu = gate_pre * sigmoid
    act = (silu * up_pre).astype(BF).astype(F32)
    d_gates_ref[0] += jnp.sum(act * grad_act, axis=1, keepdims=True)
    grad_act = grad_act * gates
    act_ref[...] = (act * gates).astype(BF)
    up_ref[...] = (grad_act * silu).astype(BF)
    gate_ref[...] = (grad_act * up_pre * (sigmoid * (1.0 + gate_pre * (1.0 - sigmoid)))).astype(BF)


def expert_units(table, place, at, blocks, routes, router_w, gate_w, up_w, grad_act, count):
    rows, width = len(blocks) * blocks[0].shape[0], blocks[0].shape[1]
    units = gate_w.shape[1]
    wide = min(512, units // count)
    per = units // wide // count
    weight = pl.BlockSpec((width, wide), lambda n: (0, n))
    tile = pl.BlockSpec((rows, wide), lambda n: (0, n))
    out = jax.ShapeDtypeStruct((rows, units), BF)
    return pl.pallas_call(
        functools.partial(expert_kernel, per=per, place=place, at=at),
        grid=(units // wide,),
        in_specs=[
            pl.BlockSpec(memory_space=pltpu.SMEM),
            pl.BlockSpec(router_w.shape, lambda n: (0, 0)),
            pl.BlockSpec(routes.shape, lambda n: (0, 0, 0)),
            weight,
            weight,
            tile,
        ]
        + [pl.BlockSpec(block.shape, lambda n: (0, 0)) for block in blocks],
        out_specs=[
            tile,
            tile,
            tile,
            pl.BlockSpec((1, rows, 1), lambda n: (n // per, 0, 0)),
            pl.BlockSpec((rows, width), lambda n: (0, 0)),
        ],
        out_shape=[
            out, out, out, jax.ShapeDtypeStruct((count, rows, 1), F32), jax.ShapeDtypeStruct((rows, width), BF),
        ],
        scratch_shapes=[pltpu.VMEM((count, rows, 1), F32)],
        compiler_params=pltpu.CompilerParams(dimension_semantics=("arbitrary",), vmem_limit_bytes=58 * 2**20),
        cost_estimate=MEDIUM,
        name="expert_units",
    )(table, router_w, routes, gate_w, up_w, grad_act, *blocks)


def expert_rows_kernel(gate_ref, up_ref, gate_w_ref, up_w_ref, o_ref):
    o_ref[...] = (dot_nt(gate_ref[...], gate_w_ref[...]) + dot_nt(up_ref[...], up_w_ref[...])).astype(BF)


def expert_rows(gate_grads, up_grads, gate_w, up_w):
    rows, units = gate_grads.shape
    width = gate_w.shape[0]
    wide = min(512, width)
    whole = pl.BlockSpec((rows, units), lambda n: (0, 0))
    weight = pl.BlockSpec((wide, units), lambda n: (n, 0))
    return pl.pallas_call(
        expert_rows_kernel,
        grid=(width // wide,),
        in_specs=[whole, whole, weight, weight],
        out_specs=pl.BlockSpec((rows, wide), lambda n: (0, n)),
        out_shape=jax.ShapeDtypeStruct((rows, width), BF),
        compiler_params=pltpu.CompilerParams(dimension_semantics=("arbitrary",), vmem_limit_bytes=56 * 2**20),
        cost_estimate=MEDIUM,
        name="expert_rows",
    )(gate_grads, up_grads, gate_w, up_w)


def times_kernel(b_ref, *refs):
    count = len(refs) // 2
    for a_ref, o_ref in zip(refs[:count], refs[count:]):
        o_ref[...] = dot_nt(a_ref[...], b_ref[...]).astype(o_ref.dtype)


def times_transpose(lefts, b):
    columns, depth = b.shape
    wide = min(512, columns)
    return pl.pallas_call(
        times_kernel,
        grid=(columns // wide,),
        in_specs=[pl.BlockSpec((wide, depth), lambda n: (n, 0))]
        + [pl.BlockSpec(left.shape, lambda n: (0, 0)) for left in lefts],
        out_specs=[pl.BlockSpec((left.shape[0], wide), lambda n: (0, n)) for left in lefts],
        out_shape=[jax.ShapeDtypeStruct((left.shape[0], columns), BF) for left in lefts],
        compiler_params=pltpu.CompilerParams(dimension_semantics=("arbitrary",), vmem_limit_bytes=58 * 2**20),
        cost_estimate=MEDIUM,
        name="times_transpose",
    )(b, *lefts)


def sum_kernel(_unused, *refs):
    *pair_refs, o_ref = refs
    count = len(pair_refs) // 2
    total = dot_tn(pair_refs[0][...], pair_refs[count][...])
    for index in range(1, count):
        total = total + dot_tn(pair_refs[index][...], pair_refs[count + index][...])
    o_ref[...] = total.astype(o_ref.dtype)


def sum_of_outer(table, lefts, rights, slots=None):
    whole = not isinstance(lefts, (list, tuple))
    count, depth = len(rights), rights[0].shape[0]
    rows, columns = (lefts if whole else lefts[0]).shape[1], rights[0].shape[1]
    tall, wide = 512, columns if count <= 2 else min(1024, columns)

    def left_spec(index):
        at = index if whole else 0
        if slots is None:
            return pl.BlockSpec((depth, tall), lambda n, m, t: (at, m))
        return pl.BlockSpec((depth, tall), lambda n, m, t: (at, t[slots[0] + m]))

    return pl.pallas_call(
        sum_kernel,
        grid_spec=pltpu.PrefetchScalarGridSpec(
            num_scalar_prefetch=1,
            grid=(columns // wide, rows // tall),
            in_specs=[left_spec(index) for index in range(count)]
            + [pl.BlockSpec((depth, wide), lambda n, m, t: (0, n)) for _unused in rights],
            out_specs=pl.BlockSpec((tall, wide), lambda n, m, t: (m, n)),
        ),
        out_shape=jax.ShapeDtypeStruct((rows, columns), BF),
        compiler_params=pltpu.CompilerParams(
            dimension_semantics=("arbitrary", "arbitrary"), vmem_limit_bytes=56 * 2**20
        ),
        cost_estimate=LONG,
        name="sum_of_outer",
    )(table, *([lefts] * count if whole else lefts), *rights)


def add_kernel(_unused, left_ref, right_ref, o_ref):
    o_ref[...] = (left_ref[...].astype(F32) + right_ref[...].astype(F32)).astype(BF)


def add_slabs(table, left, right, first, second):
    columns = left.shape[1]
    slab = left.shape[0] // 4
    tall = slab // 4

    def spec(at):
        return pl.BlockSpec((tall, columns), lambda m, t: (4 * at + m, 0))

    return pl.pallas_call(
        add_kernel,
        grid_spec=pltpu.PrefetchScalarGridSpec(
            num_scalar_prefetch=1, grid=(4,), in_specs=[spec(first), spec(second)], out_specs=spec(0)
        ),
        out_shape=jax.ShapeDtypeStruct((slab, columns), BF),
        cost_estimate=SMALL,
        name="add_slabs",
    )(table, left, right)


NN, NT = ((1,), (0,)), ((1,), (1,))


def small_call(kernel, name, out_shape, *operands, cost=SMALL, scratch=(), **kwargs):
    vmem = pl.BlockSpec(memory_space=pltpu.VMEM)
    return pl.pallas_call(
        functools.partial(kernel, **kwargs),
        in_specs=[pl.BlockSpec(memory_space=pltpu.SMEM)] + [vmem] * (len(operands) - 1),
        out_specs=jax.tree.map(lambda _unused: vmem, out_shape),
        out_shape=out_shape,
        scratch_shapes=list(scratch),
        compiler_params=pltpu.CompilerParams(vmem_limit_bytes=48 * 2**20),
        cost_estimate=cost,
        name=name,
    )(*operands)


def payload_kernel(_unused, a_ref, b_ref, o_ref):
    rows, width = b_ref.shape[0], o_ref.shape[1]
    columns = b_ref.shape[1]
    rest = columns - width
    o_ref[:rows, :] = a_ref[:, :width]
    o_ref[rows : 2 * rows, :] = b_ref[:, :width]
    o_ref[2 * rows : 3 * rows, :rest] = a_ref[:, width:columns]
    o_ref[2 * rows : 3 * rows, rest:] = b_ref[:, width:]
    o_ref[3 * rows :, :] = a_ref[:, columns:]


def fetched_payload(table, from_beyond, from_across, width):
    out = jax.ShapeDtypeStruct((4 * from_across.shape[0], width), BF)
    return small_call(payload_kernel, "fetched_payload", out, table, from_beyond, from_across)


def own_pairs_kernel(table_ref, *refs, blocks, kinds, slabs, ring_slots):
    block_refs, refs = refs[:blocks], refs[blocks:]
    own_ref, near_ref, *piece_refs = refs[:-5]
    o_ref, columns_out, columns_ref, rows_ref, sems = refs[-5:]
    head_step, kind = pl.program_id(0), pl.program_id(1)
    slab, columns = own_ref.shape
    width = piece_refs[0].shape[1]
    part = piece_refs[0].shape[0] // 4
    rest = columns - width
    back = pltpu.make_async_copy(columns_ref, columns_out, sems.at[2 + 4 * len(piece_refs)])

    @pl.when((head_step == 0) & (kind == 0))
    def _():
        def at(slot, ring_slot=None):
            start = table_ref[slot] * slab
            if ring_slot is None:
                return pl.ds(pl.multiple_of(start, slab), slab)
            return pl.ds(pl.multiple_of(start + table_ref[ring_slot] * part, part), part)

        pairs = [(own_ref, columns_ref.at[at(slabs[0]), :]), (near_ref, columns_ref.at[at(slabs[1]), :])]
        for ring_slot, piece in zip(ring_slots, piece_refs):
            for index in range(2):
                to = at(slabs[2 + index], ring_slot)
                pairs.append((piece.at[index * part : (index + 1) * part, :], columns_ref.at[to, :width]))
                some = piece.at[2 * part : 3 * part, index * rest : (index + 1) * rest]
                pairs.append((some, columns_ref.at[to, width:]))
        copies = [pltpu.make_async_copy(*pair, sems.at[index]) for index, pair in enumerate(pairs)]
        for copy in copies:
            copy.start()
        stack_blocks(block_refs, rows_ref)
        for copy in copies:
            copy.wait()
        back.start()

    rows, head_dim = o_ref.shape[2:]
    wide = o_ref.shape[0] * head_dim
    at_column = (kind * pl.num_programs(0) + head_step) * wide
    product = dot(rows_ref[...], columns_ref[:, pl.ds(pl.multiple_of(at_column, wide), wide)]).astype(BF)
    for head in range(o_ref.shape[0]):
        for block in range(blocks):
            piece = product[block * rows : (block + 1) * rows, head * head_dim : (head + 1) * head_dim]
            o_ref[head, block * kinds + kind] = piece

    @pl.when((head_step == pl.num_programs(0) - 1) & (kind == kinds - 1))
    def _():
        back.wait()


def own_pairs(table, blocks, own, near, pieces, kinds, head_dim, slabs, ring_slots):
    rows, depth = blocks[0].shape
    columns = own.shape[1]
    heads = columns // head_dim // kinds
    at_once = 2
    anywhere = pl.BlockSpec(memory_space=pl.ANY)
    return pl.pallas_call(
        functools.partial(
            own_pairs_kernel, blocks=len(blocks), kinds=kinds, slabs=slabs, ring_slots=ring_slots
        ),
        grid=(heads // at_once, kinds),
        in_specs=[pl.BlockSpec(memory_space=pltpu.SMEM)]
        + [pl.BlockSpec(block.shape, lambda h, k: (0, 0)) for block in blocks]
        + [anywhere] * (2 + len(pieces)),
        out_specs=[
            pl.BlockSpec((at_once, len(blocks) * kinds, rows, head_dim), lambda h, k: (h, 0, 0, 0)),
            anywhere,
        ],
        out_shape=[
            jax.ShapeDtypeStruct((heads, len(blocks) * kinds, rows, head_dim), BF),
            jax.ShapeDtypeStruct((depth, columns), BF),
        ],
        scratch_shapes=[
            pltpu.VMEM((depth, columns), BF),
            pltpu.VMEM((len(blocks) * rows, depth), BF),
            pltpu.SemaphoreType.DMA((3 + 4 * len(pieces),)),
        ],
        compiler_params=pltpu.CompilerParams(
            dimension_semantics=("arbitrary", "arbitrary"), vmem_limit_bytes=40 * 2**20
        ),
        cost_estimate=SMALL,
        name="own_pairs",
    )(table, *blocks, own, near, *pieces)


def far_rows_kernel(table_ref, *refs, ring_slots):
    *pieces, o_ref = refs
    part = pieces[0].shape[0] // 4
    for slot, piece in zip(ring_slots, pieces):
        o_ref[pl.ds(pl.multiple_of(table_ref[slot] * part, part), part), :] = piece[3 * part :, :]


def far_rows(table, pieces, ring_slots):
    rows, width = pieces[0].shape
    out = jax.ShapeDtypeStruct((rows // 4 * len(pieces), width), BF)
    return small_call(far_rows_kernel, "far_rows", out, table, *pieces, ring_slots=ring_slots)


def heads_of(ref, side, sequence, count):
    return [ref[side * count + head, sequence] for head in range(count)]


def mixed_out_kernel(table_ref, m_ref, w_ref, far_ref, *refs, side):
    count = m_ref.shape[0] // 2
    for sequence, ref in enumerate(refs):
        own = jnp.concatenate(heads_of(m_ref, table_ref[side], sequence, count), axis=1)
        far = jnp.concatenate(heads_of(m_ref, 1 - table_ref[side], sequence, count), axis=1)
        ref[...] = (dot(own, w_ref[...]) + dot(far, far_ref[...])).astype(ref.dtype)


def mixed_out(table, mixed, w_out, w_far, side):
    shape = (mixed.shape[2], w_out.shape[1])
    out = [jax.ShapeDtypeStruct(shape, kind) for kind in (F32, BF)]
    return small_call(mixed_out_kernel, "mixed_out", out, table, mixed, w_out, w_far, cost=MEDIUM, side=side)


def grad_pairs_kernel(table_ref, own_ref, beside_ref, w_ref, far_ref, o_ref, *, side):
    rows, head_dim = o_ref.shape[2:]
    count = o_ref.shape[0] // 2
    grads = jnp.concatenate([own_ref[...], beside_ref[...]], axis=0)
    for slab_ref, at in ((w_ref, table_ref[side]), (far_ref, 1 - table_ref[side])):
        product = dot_nt(grads, slab_ref[...]).astype(BF)
        for head in range(count):
            for sequence in range(2):
                piece = product[sequence * rows : (sequence + 1) * rows, head * head_dim : (head + 1) * head_dim]
                o_ref[at * count + head, sequence] = piece


def grad_pairs(table, own, beside, w_out, w_far, side, head_dim):
    out = jax.ShapeDtypeStruct((2 * w_out.shape[0] // head_dim, 2, own.shape[0], head_dim), BF)
    return small_call(
        grad_pairs_kernel, "grad_pairs", out, table, own, beside, w_out, w_far, cost=LONG, side=side
    )


def out_grads_kernel(table_ref, m_ref, other_ref, *refs, turn, own_rows, side):
    *block_refs, o_ref, mixed_ref, turned_ref, grads_ref = refs
    head_dim = m_ref.shape[3]
    count = m_ref.shape[0] // 2
    for head in range(count):
        rows = [m_ref[table_ref[side] * count + head, sequence] for sequence in range(2)]
        rows += [other_ref[head, sequence] for sequence in range(2)]
        rows = jnp.concatenate(rows, axis=0)
        mixed_ref[head * head_dim : (head + 1) * head_dim, :] = rows.astype(F32).T.astype(BF)
    for index in range(mixed_ref.shape[0] // own_rows):
        at = pl.multiple_of(table_ref[turn + index] * own_rows, own_rows)
        turned_ref[index * own_rows : (index + 1) * own_rows, :] = mixed_ref[pl.ds(at, own_rows), :]
    stack_blocks(block_refs, grads_ref)
    o_ref[...] = dot(turned_ref[...], grads_ref[...])


def out_grads(table, mixed, other, blocks, turn, own_rows, side):
    rows, width = blocks[0].shape
    features = mixed.shape[0] // 2 * mixed.shape[3]
    turned = pltpu.VMEM((features, len(blocks) * rows), BF)
    out = jax.ShapeDtypeStruct((features, width), F32)
    scratch = [turned, turned, pltpu.VMEM((len(blocks) * rows, width), BF)]
    return small_call(
        out_grads_kernel, "out_grads", out, table, mixed, other, *blocks, cost=LONG, scratch=scratch, turn=turn,
        own_rows=own_rows, side=side,
    )


def transposed_kernel(table_ref, *refs, slots):
    *block_refs, o_ref = refs
    rows, width = block_refs[0].shape
    slab = width // len(slots)
    for index, block_ref in enumerate(block_refs):
        for number, slot in enumerate(slots):
            here = pl.ds(pl.multiple_of(table_ref[slot] * slab, slab), slab)
            some = block_ref[:, here].astype(F32).T.astype(BF)
            o_ref[number * slab : (number + 1) * slab, index * rows : (index + 1) * rows] = some


def transposed(table, blocks, slots):
    rows, width = blocks[0].shape
    out = jax.ShapeDtypeStruct((width, len(blocks) * rows), BF)
    return small_call(transposed_kernel, "transposed", out, table, *blocks, cost=LONG, slots=slots)


def head_weights_kernel(table_ref, g_ref, own_ref, beside_ref, o_ref, grads_ref, *, kinds, places):
    rows, head_dim = g_ref.shape[2:]

    @pl.when(pl.program_id(0) == 0)
    def _():
        for index in range(g_ref.shape[0]):
            for sequence in range(2):
                for kind in range(kinds):
                    piece = g_ref[table_ref[places + index], sequence * kinds + kind]
                    here = slice(kind * head_dim, (kind + 1) * head_dim)
                    grads_ref[sequence, index * rows : (index + 1) * rows, here] = piece

    o_ref[...] = (dot(own_ref[...], grads_ref[0]) + dot(beside_ref[...], grads_ref[1])).astype(BF)


def head_weights(table, grads, own, beside, kinds, places):
    blocks, _unused, rows, head_dim = grads.shape
    width, total = own.shape
    tall = width // 4
    row = pl.BlockSpec((tall, total), lambda m: (m, 0))
    return pl.pallas_call(
        functools.partial(head_weights_kernel, kinds=kinds, places=places),
        grid=(4,),
        in_specs=[pl.BlockSpec(memory_space=pltpu.SMEM), pl.BlockSpec(grads.shape, lambda m: (0, 0, 0, 0)), row, row],
        out_specs=pl.BlockSpec((tall, kinds * head_dim), lambda m: (m, 0)),
        out_shape=jax.ShapeDtypeStruct((width, kinds * head_dim), BF),
        scratch_shapes=[pltpu.VMEM((2, total, kinds * head_dim), BF)],
        compiler_params=pltpu.CompilerParams(dimension_semantics=("arbitrary",), vmem_limit_bytes=48 * 2**20),
        cost_estimate=LONG,
        name="head_weights",
    )(table, grads, own, beside)


def chip_total_kernel(table_ref, own_ref, other_ref, keep_ref, send_ref, *, core):
    slab = keep_ref.shape[0]
    for ref, at in ((keep_ref, table_ref[core]), (send_ref, 1 - table_ref[core])):
        here = pl.ds(pl.multiple_of(at * slab, slab), slab)
        ref[...] = (own_ref[here, :].astype(F32) + other_ref[here, :].astype(F32)).astype(BF)


def chip_total(table, own, other, core):
    out = [jax.ShapeDtypeStruct((other.shape[0] // 2, own.shape[1]), BF)] * 2
    return small_call(chip_total_kernel, "chip_total", out, table, own, other, core=core)


def beside_kernel(_unused, left_ref, right_ref, o_ref):
    columns = left_ref.shape[1]
    o_ref[:, :columns] = left_ref[...].astype(BF)
    o_ref[:, columns:] = right_ref[...].astype(BF)


def side_by_side(table, left, right):
    out = jax.ShapeDtypeStruct((left.shape[0], left.shape[1] + right.shape[1]), BF)
    return small_call(beside_kernel, "side_by_side", out, table, left, right)


def pair_rows_kernel(g_ref, w_ref, own_ref, beside_ref, dn_ref, *, kinds):
    kind = pl.program_id(1)

    @pl.when((pl.program_id(0) == 0) & (kind == 0))
    def _():
        dn_ref[...] = jnp.zeros_like(dn_ref)

    heads = []
    for head in range(g_ref.shape[0]):
        heads.append(jnp.concatenate([g_ref[head, sequence * kinds + kind] for sequence in range(2)], axis=0))
    dn_ref[...] += dot_nt(jnp.concatenate(heads, axis=1), w_ref[...])

    @pl.when((pl.program_id(0) == pl.num_programs(0) - 1) & (kind == kinds - 1))
    def _():
        rows = own_ref.shape[0]
        own_ref[...] = dn_ref[:rows, :]
        beside_ref[...] = dn_ref[rows:, :].astype(BF)


def pair_normed(grads, columns, kinds):
    heads, _unused, rows, head_dim = grads.shape
    width, at_once = columns.shape[0], 2
    whole = pl.BlockSpec((rows, width), lambda h, k: (0, 0))
    return pl.pallas_call(
        functools.partial(pair_rows_kernel, kinds=kinds),
        grid=(heads // at_once, kinds),
        in_specs=[
            pl.BlockSpec((at_once, 2 * kinds, rows, head_dim), lambda h, k: (h, 0, 0, 0)),
            pl.BlockSpec((width, at_once * head_dim), lambda h, k: (0, k * (heads // at_once) + h)),
        ],
        out_specs=[whole, whole],
        out_shape=[jax.ShapeDtypeStruct((rows, width), kind) for kind in (F32, BF)],
        scratch_shapes=[pltpu.VMEM((2 * rows, width), F32)],
        compiler_params=pltpu.CompilerParams(
            dimension_semantics=("arbitrary", "arbitrary"), vmem_limit_bytes=40 * 2**20
        ),
        cost_estimate=LONG,
        name="pair_normed",
    )(grads, columns)


def take_kernel(table_ref, *refs, count, sides):
    weights, outs, sems = refs[:count], refs[count : count + len(sides)], refs[-1]
    copies = []
    for out, (row, rows, pieces) in zip(outs, sides):
        at = 0
        if row is None:
            here = slice(None)
        else:
            here = pl.ds(pl.multiple_of(table_ref[row] * rows, rows), rows)
        for number, slot, wide in pieces:
            there = slice(None)
            if slot is not None:
                there = pl.ds(pl.multiple_of(table_ref[slot] * wide, wide), wide)
            copies.append(
                pltpu.make_async_copy(
                    weights[number].at[here, there], out.at[:, at : at + wide], sems.at[len(copies)]
                )
            )
            at += wide
    for copy in copies:
        copy.start()
    for copy in copies:
        copy.wait()


def take_parts(table, weights, sides, cost):
    outs = []
    for row, rows, pieces in sides:
        outs.append(jax.ShapeDtypeStruct((rows, sum(wide for _unused, _unused2, wide in pieces)), BF))
    number = sum(len(pieces) for _unused, _unused2, pieces in sides)
    return pl.pallas_call(
        functools.partial(take_kernel, count=len(weights), sides=sides),
        in_specs=[pl.BlockSpec(memory_space=pltpu.SMEM)] + [pl.BlockSpec(memory_space=pl.ANY)] * len(weights),
        out_specs=[pl.BlockSpec(memory_space=pltpu.VMEM)] * len(sides),
        out_shape=outs,
        scratch_shapes=[pltpu.SemaphoreType.DMA((number,))],
        compiler_params=pltpu.CompilerParams(vmem_limit_bytes=60 * 2**20),
        cost_estimate=cost,
        name="take_parts",
    )(table, *weights)


def place_kernel(table_ref, *refs, slots):
    *pieces, out = refs
    for piece, slot in zip(pieces, slots):
        rows = piece.shape[0]
        out[pl.ds(pl.multiple_of(table_ref[slot] * rows, rows), rows), :] = piece[...]


def place_rows(table, pieces, slots):
    rows = sum(piece.shape[0] for piece in pieces)
    out = jax.ShapeDtypeStruct((rows, pieces[0].shape[1]), pieces[0].dtype)
    return small_call(place_kernel, "place_rows", out, table, *pieces, slots=slots)


def pack_kernel(table_ref, below_ref, early_ref, late_ref, o_ref, rows_ref, *, slot, experts):
    slab = o_ref.shape[1] // 4
    first = below_ref.shape[0]
    here = pl.ds(pl.multiple_of(table_ref[slot] * slab, slab), slab)
    rows_ref[...] = jnp.zeros_like(rows_ref)
    for index in range(experts):
        at = index // 4
        rows_ref[at : at + 1, index % 4 * slab : (index % 4 + 1) * slab] = early_ref[index : index + 1, here]
    at = experts // 4
    rows_ref[at : at + 1, :] = early_ref[experts : experts + 1, :]
    rows_ref[at + 1 : at + 3, :] = late_ref[...]
    o_ref[:first, :] = below_ref[...].astype(BF)
    o_ref[first:, :] = rows_ref[...].astype(BF)


def pack_gains(table, below, early, late, slot, experts):
    height = -(-(experts // 4 + 3) // 16) * 16
    out = jax.ShapeDtypeStruct((below.shape[0] + height, early.shape[1]), BF)
    scratch = [pltpu.VMEM((height, early.shape[1]), F32)]
    return small_call(
        pack_kernel, "pack_gains", out, table, below, early, late, scratch=scratch, slot=slot, experts=experts
    )


def unpack_kernel(table_ref, *refs, back, experts):
    *pieces, router_ref, gains_ref, all_ref = refs
    height = all_ref.shape[1]
    for index, piece in enumerate(pieces):
        all_ref[index] = piece[piece.shape[0] - height :, :].astype(F32)
    total = all_ref[table_ref[back]]
    for place in range(1, len(pieces)):
        total = total + all_ref[table_ref[back + place]]
    slab = total.shape[1] // 4
    rows = [total[i // 4 : i // 4 + 1, i % 4 * slab : (i % 4 + 1) * slab] for i in range(experts)]
    router_ref[...] = jnp.concatenate(rows, axis=0).T
    gains_ref[...] = total[experts // 4 : experts // 4 + 3, :]


def unpack_gains(table, pieces, back, experts, height):
    width = pieces[0].shape[1]
    out = [jax.ShapeDtypeStruct((width // 4, experts), F32), jax.ShapeDtypeStruct((3, width), F32)]
    scratch = [pltpu.VMEM((len(pieces), height, width), F32)]
    return small_call(
        unpack_kernel, "unpack_gains", out, table, *pieces, scratch=scratch, back=back, experts=experts
    )


def spread_kernel(table_ref, *refs, count, outs, cuts):
    pieces = refs[:count]
    out_refs = refs[-2 - outs : -2]
    wide_ref, sems = refs[-2:]
    copies = []
    for index, (number, rows, columns, out, slot, by_rows) in enumerate(cuts):
        wide_ref[index] = pieces[number][rows[0] : rows[1], columns[0] : columns[1]].astype(F32)
        size = rows[1] - rows[0] if by_rows else columns[1] - columns[0]
        here = pl.ds(pl.multiple_of(table_ref[slot] * size, size), size)
        to = out_refs[out].at[here, :] if by_rows else out_refs[out].at[:, here]
        copies.append(pltpu.make_async_copy(wide_ref.at[index], to, sems.at[index]))
        copies[-1].start()
    for copy in copies:
        copy.wait()


def spread(table, pieces, cuts, shape, outs, before):
    vmem, anywhere = pl.BlockSpec(memory_space=pltpu.VMEM), pl.BlockSpec(memory_space=pl.ANY)
    old = [] if before is None else list(before)
    _unused, rows, columns, *_rest = cuts[0]
    return pl.pallas_call(
        functools.partial(spread_kernel, count=len(pieces), outs=outs, cuts=cuts),
        in_specs=[pl.BlockSpec(memory_space=pltpu.SMEM)] + [vmem] * len(pieces) + [anywhere] * len(old),
        out_specs=[anywhere] * outs,
        out_shape=[jax.ShapeDtypeStruct(shape, F32)] * outs,
        input_output_aliases={1 + len(pieces) + index: index for index in range(len(old))},
        scratch_shapes=[
            pltpu.VMEM((len(cuts), rows[1] - rows[0], columns[1] - columns[0]), F32),
            pltpu.SemaphoreType.DMA((len(cuts),)),
        ],
        compiler_params=pltpu.CompilerParams(vmem_limit_bytes=24 * 2**20),
        cost_estimate=SMALL,
        name="spread",
    )(table, *pieces, *old)


def merge_kernel(w_ref, o_ref):
    units = w_ref.shape[2]
    for index in range(w_ref.shape[1]):
        o_ref[:, index * units : (index + 1) * units] = w_ref[:, index, :]


def merge_experts(weight):
    rows, count, units = weight.shape
    at_once = 128
    return pl.pallas_call(
        merge_kernel,
        grid=(rows // at_once,),
        in_specs=[pl.BlockSpec((at_once, count, units), lambda m: (m, 0, 0))],
        out_specs=pl.BlockSpec((at_once, count * units), lambda m: (m, 0)),
        out_shape=jax.ShapeDtypeStruct((rows, count * units), weight.dtype),
        cost_estimate=MEDIUM,
        name="merge_experts",
    )(weight)


def split_kernel(*refs):
    *term_refs, o_ref = refs
    units = o_ref.shape[2]
    for index in range(o_ref.shape[1]):
        here = slice(index * units, (index + 1) * units)
        total = term_refs[0][:, here].astype(F32)
        for term_ref in term_refs[1:]:
            total = total + term_ref[:, here].astype(F32)
        o_ref[:, index, :] = total


def split_experts(count, rows, *terms):
    columns = terms[0][0].shape[1]
    at_once = 128
    steps = rows // at_once

    def spec(at):
        return pl.BlockSpec((at_once, columns), lambda m: (at * steps + m, 0))

    return pl.pallas_call(
        split_kernel,
        grid=(steps,),
        in_specs=[spec(at) for _unused, at in terms],
        out_specs=pl.BlockSpec((at_once, count, columns // count), lambda m: (m, 0, 0)),
        out_shape=jax.ShapeDtypeStruct((rows, count, columns // count), F32),
        cost_estimate=SMALL,
        name="split_experts",
    )(*[array for array, _unused in terms])


def swap(v, mask):
    size = lax.axis_size("fsdp")
    return lax.ppermute(v, "fsdp", [(i, i ^ mask) for i in range(size)])


def ring_order(size):
    if size == 8:
        return [0, 2, 4, 6, 7, 5, 3, 1]
    return list(range(size))


def ring_send(v, direction):
    order = ring_order(lax.axis_size("ctx"))
    size = len(order)
    return lax.ppermute(v, "ctx", [(order[i], order[(i + direction) % size]) for i in range(size)])


class Flight(tuple):
    def noted(self, note):
        self.note = note
        return self


class Ring:
    def __init__(self, in_order, steps):
        self.in_order, self.steps, self.value, self.landed = in_order, steps, None, None
        self.flying = next(steps)

    def land(self):
        land(self.in_order, (self,))

    def step(self):
        if self.flying is None:
            return
        self.land()
        try:
            self.flying = self.steps.send(self.landed)
        except StopIteration as end:
            self.flying, self.value = None, end.value
        self.landed = None

    def finish(self):
        while self.flying is not None:
            self.step()
        return self.value


def land(in_order, rings, *more):
    rings = [ring for ring in rings if ring.flying is not None and ring.landed is None]
    found = [v for ring in rings for v in ring.flying] + list(more)
    if not found:
        return more
    found = in_order(*found) if len(found) > 1 else [in_order(*found)]
    for ring in rings:
        ring.landed, found = found[: len(ring.flying)], found[len(ring.flying) :]
        if isinstance(ring.flying, Flight):
            ring.flying.note(*ring.landed)
    return found


def ring_gather(v, in_order, found):
    size = lax.axis_size("ctx")
    far, half = size // 2, v.shape[0] // 2
    found[0] = v
    right, left = v, v
    for step in range(1, far):
        right, left = after((right, left), in_order.last)

        def note(right, left, step=step):
            found[size - step], found[step] = right, left

        right, left = yield Flight((ring_send(right, 1), ring_send(left, -1))).noted(note)

    def note_far(right, left):
        found[far] = jnp.concatenate([right, left])

    yield Flight((ring_send(right[:half], 1), ring_send(left[half:], -1))).noted(note_far)
    return found


def ring_scatter(term):
    size = lax.axis_size("ctx")
    far = size // 2
    first = term(far)
    half = first.shape[0] // 2
    right, left = yield (ring_send(first[:half].astype(BF), 1), ring_send(first[half:].astype(BF), -1))
    for offset in range(far - 1, 0, -1):
        ahead, behind = term(offset), term(size - offset)
        if offset == far - 1:
            ahead = jnp.concatenate([ahead[:half].astype(F32) + right.astype(F32), ahead[half:].astype(F32)])
            behind = jnp.concatenate([behind[:half].astype(F32), behind[half:].astype(F32) + left.astype(F32)])
        else:
            ahead, behind = ahead.astype(F32) + right.astype(F32), behind.astype(F32) + left.astype(F32)
        right, left = yield (ring_send(ahead.astype(BF), 1), ring_send(behind.astype(BF), -1))
    return term(0).astype(F32) + right.astype(F32) + left.astype(F32)


def after(v, *others):
    return lax.optimization_barrier((v, *others))[0]


class Order:
    def __init__(self, first):
        self.last = first

    def __call__(self, *values):
        self.last, *values = lax.optimization_barrier((self.last, *values))
        return values[0] if len(values) == 1 else values


def sum_fsdp(v):
    size = lax.axis_size("fsdp")
    mask = 1
    while mask < size:
        (other,) = yield (swap(v, mask),)
        v = v + other
        mask *= 2
    return v


def body(
    tokens, attn_gain, w_query, w_key, w_value, query_gain, key_gain, w_out,
    ffn_gain, w_router, w_gate, w_up, w_down, routes, cotangent,
):
    ctx_size = lax.axis_size("ctx")
    parts = lax.axis_size("fsdp")
    rows = tokens.shape[1]
    width = tokens.shape[2]
    slab = w_query.shape[0]
    head_dim = query_gain.shape[0]
    own_heads = width // head_dim // parts
    own_width = own_heads * head_dim
    own_rows = slab // ctx_size
    own_experts = w_gate.shape[1]
    hidden_units = w_gate.shape[2]
    experts = own_experts * ctx_size
    seq_length = rows * ctx_size
    in_order = Order(jnp.zeros((), F32))

    heads = 2 * own_heads
    repeats = ctx_size // heads
    order = ring_order(ctx_size)
    offsets = [0] + [o for step in range(1, ctx_size // 2) for o in (step, ctx_size - step)] + [ctx_size // 2]
    at_ring, at_place, at_core, at_side = 0, 1, 2, 3
    at_slab = [4 + mask for mask in range(parts)]
    at_groups, at_beside, at_chip = (8, 9), (10, 11), (12, 13, 14, 15)
    at_order = (16, 17, 18, 19)
    at_from = 20
    at_blocks = [at_from + ctx_size + index for index in range(ctx_size)]
    at_heads = [(at_from + 2 * ctx_size + index, at_from + 3 * ctx_size + index) for index in range(ctx_size)]
    at_turn = at_from + 4 * ctx_size
    at_back = at_from + 5 * ctx_size
    lines = []
    for place in range(ctx_size):
        ring_place = order.index(place)
        for mine in range(parts):
            side, core = divmod(mine, 2)
            line = [ring_place, place, core, side] + [mine ^ mask for mask in range(parts)]
            line += [core, core + 2, 1 - core, 3 - core, 2 * side, 2 * side + 1, 2 - 2 * side, 3 - 2 * side]
            line += [mine ^ 1, mine ^ 3, mine ^ 2, mine]
            places = [order[(ring_place + offset) % ctx_size] for offset in offsets]
            line += places
            line += [(ring_place + offset) % ctx_size for offset in offsets]
            for first in (core, 1 - core):
                line += [first * own_heads + other // repeats + other // repeats // own_heads * own_heads for other in places]
            line += [(ring_place + index) % ctx_size for index in range(ctx_size)]
            line += [offsets.index((order.index(other) - ring_place) % ctx_size) for other in range(ctx_size)]
            lines.append(line)
    device = lax.axis_index("ctx").astype(jnp.uint32) * parts + lax.axis_index("fsdp").astype(jnp.uint32)
    table = lax.dynamic_slice(jnp.asarray(np.array(lines, np.int32)), (device, jnp.uint32(0)), (1, len(lines[0])))
    table = table.reshape(-1)

    def spread_pairs(v):
        if repeats > 1:
            v = jnp.repeat(v, repeats, axis=0)
        return lax.all_to_all(v, "ctx", split_axis=0, concat_axis=0, tiled=True)

    def collect_pairs(v):
        v = lax.all_to_all(v, "ctx", split_axis=0, concat_axis=0, tiled=True)
        return v[::repeats] if repeats > 1 else v

    projections = (w_query, w_key, w_value)

    def side_of(row, rows, slots):
        return row, rows, [(number, slot, own_width) for number in range(3) for slot in slots]

    row, rows_of, some = side_of(at_ring, own_rows, at_groups)
    fetched = in_order(
        *take_parts(
            table, (*projections, w_out), [(row, rows_of, some + [(3, None, width)]), side_of(row, rows_of, at_beside)], SMALL
        )
    )
    fetched = swap(fetched[0], 2), swap(fetched[1], 3)
    cot_blocks = {}
    cot_ring = Ring(in_order, ring_gather(after(cotangent[0], in_order.last), in_order, cot_blocks))
    source = tokens[0].astype(F32)
    factor_one = lax.rsqrt(jnp.mean(source * source, axis=-1, keepdims=True) + EPSILON)
    normed = (source * factor_one * attn_gain).astype(BF)
    projections, w_down, w_gate, w_up = after((projections, w_down, w_gate, w_up), in_order.last)
    near, own, normed = in_order(
        *take_parts(
            table, projections, [side_of(None, slab, at_beside), side_of(None, slab, at_groups)], MEDIUM
        ),
        normed,
    )
    cot_ring.step()
    beside, near = swap(normed, 1), swap(near, 1)
    w_down = in_order(merge_experts(after(w_down, in_order.last)))
    cot_ring.land()
    fetched = in_order(*fetched)
    column_blocks = {}
    ring = Ring(in_order, ring_gather(fetched_payload(table, *fetched, width), in_order, column_blocks))
    down_w = lax.all_gather(after(w_down, in_order.last), "fsdp", axis=0, tiled=True)
    w_gate = in_order(merge_experts(after(w_gate, in_order.last)))
    ring.step()
    gate_w = lax.all_gather(after(w_gate, in_order.last), "fsdp", axis=0, tiled=True)
    w_router, routes = after((w_router, routes), in_order.last)
    router = [w_router, swap(w_router, 1), swap(w_router, 2), swap(w_router, 3)]
    routes_all = lax.all_to_all(
        jnp.broadcast_to(routes, (ctx_size, *routes.shape[1:])), "ctx", split_axis=0, concat_axis=0, tiled=True
    )
    normed, near, beside = in_order(normed, near, beside)
    w_up = in_order(merge_experts(after(w_up, in_order.last)))
    ring.step()
    up_w = lax.all_gather(after(w_up, in_order.last), "fsdp", axis=0, tiled=True)
    routes_all, *router = in_order(routes_all, *router)
    ring.step()

    half = head_dim // 2
    frequency = ROPE_BASE ** (-jnp.arange(half, dtype=F32) * 2.0 / head_dim)
    angles = jnp.arange(seq_length, dtype=jnp.int32).astype(F32)[:, None] * frequency[None, :]
    cosine, sine = jnp.cos(angles), jnp.sin(angles)
    cosine = jnp.concatenate([cosine, cosine], axis=1)
    sine = jnp.concatenate([-sine, sine], axis=1)
    q_gain, k_gain = query_gain[None, :], key_gain[None, :]

    ring.finish()
    qkv, own_columns = own_pairs(
        table,
        (normed, beside),
        own,
        near,
        [column_blocks[offset] for offset in offsets],
        3,
        head_dim,
        at_slab,
        at_blocks,
    )
    qkv = spread_pairs(in_order(qkv))
    router_w = in_order(place_rows(table, after(router, in_order.last), at_slab))
    w_far = in_order(far_rows(table, [column_blocks[offset] for offset in offsets], at_blocks))
    qkv = in_order(qkv)
    down_w, gate_w = in_order(down_w, gate_w)
    mixed = in_order(attend(qkv, q_gain, k_gain, cosine, sine))
    mixed = in_order(collect_pairs(mixed))
    hidden, far = in_order(*mixed_out(table, mixed, w_out, w_far, at_side))
    far = swap(far, 1)
    hidden = in_order(source + hidden)
    hidden = hidden + in_order(far).astype(F32)
    up_w = in_order(up_w)
    factor_two = lax.rsqrt(jnp.mean(hidden * hidden, axis=-1, keepdims=True) + EPSILON)
    ffn_in = in_order((hidden * factor_two * ffn_gain).astype(BF))

    ffn_blocks = {}
    ffn_ring = Ring(in_order, ring_gather(ffn_in, in_order, ffn_blocks))
    ffn_ring.step()

    size = 4
    groups = [offsets[first : first + size] for first in range(0, ctx_size, size)]

    def group_cots(group):
        return in_order(*stacked_matmul([cot_blocks[o] for o in groups[group]], down_w))

    def group_units(group, grad_act):
        return in_order(
            *expert_units(
                table, at_place, at_from + group * size, [ffn_blocks[o] for o in groups[group]], routes_all, router_w,
                gate_w, up_w, grad_act, own_experts,
            )
        )

    cots = [group_cots(0)]
    ffn_ring.step()
    cot_ring.step()
    units = [group_units(0, cots[0][0])]
    ffn_ring.step()
    cot_ring.step()
    other_side = (1 - table[at_side]).astype(jnp.uint32) * own_heads
    zero = jnp.uint32(0)
    other_mixed = lax.dynamic_slice(
        after(mixed, in_order.last), (other_side, zero, zero, zero), (own_heads, *mixed.shape[1:])
    )
    other_mixed = swap(other_mixed, 2)
    cot_ring.finish()
    ffn_ring.finish()
    normed_blocks = {}
    normed_ring = Ring(in_order, ring_gather(after(normed, in_order.last), in_order, normed_blocks))
    for group in range(1, len(groups)):
        cots.append(group_cots(group))
        if group == 1:
            normed_ring.step()
        units.append(group_units(group, cots[group][0]))
    cots = [part for _unused, part in cots]
    acts, gate_grads, up_grads, d_gates, inputs = zip(*units)

    def term_of(terms):
        def term(offset):
            group, index = divmod(offsets.index(offset), size)
            return terms[group][index * rows : (index + 1) * rows]

        return term

    def weight_grad(lefts, rights):
        lefts, rights = after((lefts, rights), in_order.last)
        return in_order(sum_of_outer(table, lefts, rights))

    def share(grad):
        return lax.psum_scatter(after(grad, in_order.last), "fsdp", scatter_dimension=0, tiled=True)

    grad_rows = {}

    def make_rows(group):
        some = after((gate_grads[group], up_grads[group]), in_order.last)
        grad_rows[group] = in_order(expert_rows(*some, gate_w, up_w))

    other_mixed = in_order(other_mixed)
    normed_ring.step()
    for group in range(len(groups) - 1, 0, -1):
        make_rows(group)
    normed_ring.step()
    row_ring = Ring(in_order, ring_scatter(term_of(grad_rows)))
    d_gate = weight_grad(inputs, gate_grads)
    row_ring.step()
    d_gate = share(d_gate)
    normed_ring.finish()
    make_rows(0)
    row_ring.step()
    weighted = in_order(*times_transpose(after(acts, in_order.last), down_w))
    row_ring.step()
    ring = Ring(in_order, ring_scatter(term_of(weighted)))
    d_gates = jnp.concatenate(after(d_gates, in_order.last), axis=1).reshape(own_experts, ctx_size, rows)
    d_gates = d_gates.at[:, table[at_back : at_back + ctx_size], :].get(mode="promise_in_bounds").transpose(1, 0, 2)
    d_gates = lax.all_to_all(d_gates, "ctx", split_axis=0, concat_axis=0, tiled=True)
    some = after(tuple(normed_blocks[offset] for offset in offsets), in_order.last)
    normed_t = in_order(transposed(table, some, at_chip))
    land(in_order, (row_ring, ring))
    d_gates = in_order(d_gates).reshape(experts, rows).T
    beside_t = swap(normed_t, 1)
    gates = routed_gates(dot(ffn_in, router_w), routes[0])
    grad_logits = gates * (d_gates - jnp.sum(gates * d_gates, axis=-1, keepdims=True))
    routed = dot(grad_logits, router_w.astype(F32), ((1,), (1,)), precision=lax.Precision.HIGHEST)
    routed = in_order(routed)
    grad_ffn_in = row_ring.finish() + routed

    inner = grad_ffn_in * ffn_gain
    grad_hidden = (
        cotangent[0].astype(F32)
        + factor_two * inner
        - hidden * (factor_two * factor_two * factor_two) * jnp.mean(inner * hidden, axis=-1, keepdims=True)
    )
    grad_proj, grad_hidden, grad_ffn_in = in_order(grad_hidden.astype(BF), grad_hidden, grad_ffn_in)

    beside = swap(grad_proj, 1)
    grad_proj, beside, beside_t = in_order(grad_proj, beside, beside_t)
    grad_mixed = in_order(grad_pairs(table, grad_proj, beside, w_out, w_far, at_side, head_dim))
    across = swap(after(grad_proj, in_order.last), 2)
    ring.step()
    grad_mixed = spread_pairs(grad_mixed)
    d_up = weight_grad(inputs, up_grads)
    (grad_mixed,) = land(in_order, (ring,), grad_mixed)
    d_up = share(d_up)
    ring.step()
    grads, head_gains = in_order(
        *attend_back(qkv, after(grad_mixed, in_order.last), q_gain, k_gain, cosine, sine)
    )
    if repeats > 1:
        head_gains = jnp.where(lax.axis_index("ctx") % repeats == 0, head_gains, 0.0)
    ring.land()

    grads = after(grads, in_order.last)
    ring.step()
    half_grads = in_order(head_weights(table, grads, normed_t, beside_t, 3, at_from))
    other_half = swap(half_grads[width // 2 :], 2)
    across = in_order(across)
    diagonal = swap(across, 1)
    grads = collect_pairs(after(grads, in_order.last))
    mixed, diagonal = after((mixed, diagonal), in_order.last)
    d_out = in_order(
        out_grads(table, mixed, other_mixed, [grad_proj, beside, across, diagonal], at_turn, own_rows, at_side)
    )
    other_half = in_order(other_half)
    keep, send = in_order(*chip_total(table, half_grads, other_half, at_core))
    send = in_order(swap(send, 1))
    pieces = {}
    total_ring = Ring(in_order, ring_gather(side_by_side(table, keep, send), in_order, pieces))
    out_ring = Ring(in_order, ring_scatter(lambda offset: d_out[offset * own_rows : (offset + 1) * own_rows]))
    d_down = weight_grad(cots, acts)
    (grads,) = land(in_order, (total_ring, out_ring, ring), grads)
    total_ring.step()
    out_ring.step()
    d_down = share(d_down)
    own, far = in_order(*pair_normed(after(grads, in_order.last), own_columns, 3))
    land(in_order, (total_ring, out_ring))
    far = swap(far, 1)
    total_ring.step()
    grad_ffn_in, grad_logits = after((grad_ffn_in, grad_logits), in_order.last)
    d_ffn_gain = jnp.sum(grad_ffn_in * hidden * factor_two, axis=0, keepdims=True)
    d_router = dot(grad_logits, ffn_in.astype(F32), ((0,), (0,)), precision=lax.Precision.HIGHEST)
    early = Ring(in_order, sum_fsdp(in_order(jnp.concatenate([d_router, d_ffn_gain]))))
    out_ring.step()
    early.step()
    grad_normed = own + in_order(far).astype(F32)
    d_attn_gain = jnp.sum(grad_normed * source * factor_one, axis=0)
    inner = grad_normed * attn_gain
    d_tokens = (
        grad_hidden
        + factor_one * inner
        - source * (factor_one * factor_one * factor_one) * jnp.mean(inner * source, axis=-1, keepdims=True)
    )
    late = jnp.concatenate([d_attn_gain, head_gains[0], head_gains[1], jnp.zeros((width - 2 * head_dim,), F32)])
    d_tokens, late = in_order(d_tokens, late.reshape(2, width))
    late = Ring(in_order, sum_fsdp(late))
    late.step()
    early.finish()
    out_ring.step()

    whole = None
    seen = set()

    def take_whole(arrays):
        new = [index for index, offset in enumerate(offsets) if offset in pieces and index not in seen]
        seen.update(new)
        high = pieces[offsets[0]].shape[0]
        for first in range(0, len(new), 4):
            some = new[first : first + 4]
            cuts = []
            for number, index in enumerate(some):
                for where in range(2):
                    for kind in range(3):
                        at = (where * 3 + kind) * head_dim
                        cuts.append((number, (0, high), (at, at + head_dim), kind, at_heads[index][where], False))
            found = [pieces[offsets[index]] for index in some]
            arrays = in_order(*spread(table, found, cuts, (slab, width), 3, arrays))
        return arrays

    whole = take_whole(whole)
    late.finish()
    output = in_order((hidden + ring.finish()).astype(BF))
    d_out = out_ring.finish()
    packed = in_order(pack_gains(table, d_out, early.value, late.value, at_slab[0], experts))
    packed_pieces = {}
    packed_ring = Ring(in_order, ring_gather(packed, in_order, packed_pieces))
    total_ring.step()
    d_gate = in_order(split_experts(own_experts, slab, (after(d_gate, in_order.last), 0)))
    whole = take_whole(whole)
    packed_ring.step()
    total_ring.finish()
    whole = take_whole(whole)
    d_query, d_key, d_value = whole
    packed_ring.step()
    d_up = in_order(split_experts(own_experts, slab, (after(d_up, in_order.last), 0)))
    packed_ring.step()
    d_down = in_order(split_experts(own_experts, slab, (after(d_down, in_order.last), 0)))
    packed_ring.finish()
    packed_blocks = [packed_pieces[offset] for offset in offsets]
    cuts = [(index, (0, own_rows), (0, width), 0, at_blocks[index], True) for index in range(ctx_size)]
    (d_out,) = spread(table, packed_blocks, cuts, (slab, width), 1, None)
    height = packed.shape[0] - own_rows
    d_router, gains = unpack_gains(table, packed_blocks, at_back, experts, height)
    d_ffn_gain, d_attn_gain, head_gains = gains + in_order.last
    return (
        output[None],
        d_tokens[None],
        d_attn_gain,
        d_query,
        d_key,
        d_value,
        head_gains[:head_dim],
        head_gains[head_dim : 2 * head_dim],
        d_out,
        d_ffn_gain,
        d_router,
        d_gate,
        d_up,
        d_down,
    )


def solution(mesh):
    token_split = P("fsdp", "ctx", None)
    row_split = P("fsdp", None)
    return jax.shard_map(
        body,
        mesh=mesh,
        in_specs=(
            token_split, P(), row_split, row_split, row_split, P(), P(), row_split,
            P(), row_split, token_split, token_split, token_split, token_split, token_split,
        ),
        out_specs=(
            token_split, token_split, P(), row_split, row_split, row_split, P(), P(),
            row_split, P(), row_split, token_split, token_split, token_split,
        ),
        check_vma=False,
    )
```
